32 devices in a mesh: pipe: 4 (over z), seq: 8 (over y, x, core).
Axes of the slice: x: 2, y: 2, z: 4, core: 2. Of those that a mesh axis runs over, the one named last changes fastest.
Arguments:
- section_input: bfloat16 [4, 2048, 1024], P('pipe', 'seq'), may hold values from -6 to 6
- saved_input: bfloat16 [4, 2048, 1024], P('pipe', 'seq'), may hold values from -6 to 6
- grad_output: bfloat16 [4, 2048, 1024], P('pipe', 'seq'), may hold values from -6 to 6
- w_qkv: bfloat16 [4, 3072, 1024], P('pipe'), may hold values from -0.1875 to 0.1875
- w_out: bfloat16 [4, 1024, 1024], P('pipe'), may hold values from -0.75 to 0.75
- tile_cluster: int32 [16], replicated, may hold values from 0 to 7, as said below
Outputs:
- next_input: bfloat16 [4, 2048, 1024], P('pipe', 'seq')
- grad_input: bfloat16 [4, 2048, 1024], P('pipe', 'seq')
The draws below stay inside these ranges and needn't reach their ends.
Inputs may be any that keep to these rules, and one draw needn't show every extreme that they name: `tile_cluster`: each of the 8 ids names between 1 and 3 tiles, and some id names exactly 3. The id of tile i leaves the remainder i % 1 when divided by 1.
All inputs are finite; a program needn't handle non-finite values.
Results may differ from the reference program's by a relative error of at most 0.007.
Values may be sent and summed in bfloat16 or wider, within the bound.
No kernel may reach another device: no remote copies, remote signals or barrier semaphores. Data moves between devices by JAX's collectives and lax.ppermute only.
A program may use at most 128 MiB of HBM per device.

```python
import jax
import jax.numpy as jnp
from jax import lax

D = 1024
HEADS = 8
HD = 128
TILE = 128
INNER = 1024
TPD = 2
CAP = 3
TOKENS = 2048
NT = 16
CLUSTERS = 8
SECTIONS = 4


def shuffled_rows(key, count, length):
    keys = jax.random.split(key, count)
    rows = [jax.random.permutation(keys[index], length) for index in range(count)]
    return jnp.stack(rows).astype(jnp.int32)


def draw_tile_cluster(key, part):
    key_pattern, key_turn, key_order, key_label = jax.random.split(key, 4)
    spacing = CLUSTERS // HEADS
    members = TPD * HEADS
    pair_count = CLUSTERS // 2
    patterns = jnp.array([[TPD, TPD], [2 * TPD - 1, 1], [TPD + 1, TPD - 1]], dtype=jnp.int32)
    chosen = jax.random.randint(key_pattern, (pair_count,), 0, 3).at[0].set(1)
    turned = jax.random.randint(key_turn, (pair_count,), 0, 2)
    picked = patterns[chosen]
    columns = (jnp.arange(2)[None, :] + turned[:, None]) % 2
    cluster_size = jnp.take_along_axis(picked, columns, axis=1).reshape(spacing, HEADS)
    bounds = jnp.cumsum(cluster_size, axis=1)
    position = jnp.arange(members, dtype=jnp.int32)
    grouped = jnp.sum((position[None, :, None] >= bounds[:, None, :]).astype(jnp.int32), axis=2)
    orders = shuffled_rows(key_order, spacing, members)
    shuffled = jnp.take_along_axis(grouped, orders, axis=1)
    labels = shuffled_rows(key_label, spacing, HEADS)
    ranked = jnp.take_along_axis(labels, shuffled, axis=1)
    residue = jnp.arange(spacing, dtype=jnp.int32)[:, None]
    cluster = residue + spacing * ranked
    return cluster.T.reshape(NT).astype(jnp.int32)


def levels(key, dims, cuts, low, largest):
    level, own = 1.0, jax.random.fold_in(key, 6)
    for dim, shards_of in cuts:
        steps = jnp.exp(jax.random.uniform(jax.random.fold_in(own, dim), (shards_of,), jnp.float32, low / len(cuts), largest / len(cuts)))
        level = level * jnp.repeat(steps, dims[dim] // shards_of).reshape([-1 if axis == dim else 1 for axis in range(len(dims))])
    return level


def scatter_about(stream_key, shape, deviation, bound, cuts=(), held_as=jnp.bfloat16):
    result = jax.random.normal(stream_key, shape, jnp.float32) * deviation
    if len(cuts) > 0:
        result = levels(stream_key, shape, cuts, -0.22, 0.18) * result
    return jnp.clip(result, min=-bound, max=bound).astype(held_as)


def setup_inputs(seed: int = 0) -> dict:
    seeds = jax.random.split(jax.random.key(seed), 7)
    return {
        "section_input": scatter_about(seeds[0], (SECTIONS, TOKENS, D), 1.0, 6.0, ((0, 4), (1, 8))),
        "saved_input": scatter_about(seeds[1], (SECTIONS, TOKENS, D), 1.0, 6.0, ((0, 4), (1, 8))),
        "grad_output": scatter_about(seeds[2], (SECTIONS, TOKENS, D), 1.0, 6.0, ((0, 4), (1, 8))),
        "w_qkv": scatter_about(seeds[3], (SECTIONS, 3 * INNER, D), D ** -0.5, 0.1875, ((0, 4),)),
        "w_out": scatter_about(seeds[4], (SECTIONS, INNER, D), (INNER // 16) ** -0.5, 0.75, ((0, 4),)),
        "tile_cluster": draw_tile_cluster(jax.random.fold_in(seeds[6], 71), 0),
    }


EPSILON = 1e-05

def row_norm(values):
    return values * lax.rsqrt(lax.optimization_barrier(jnp.mean(values * values, axis=-1, keepdims=True)) + EPSILON)

def head_norm(values):
    shaped = values.reshape(values.shape[:-1] + (HEADS, HD))
    return row_norm(shaped).reshape(values.shape)

def attend(queries, key_rows, value_rows, live_keys):
    factor = queries.shape[-1] ** (-0.5)
    scores = jnp.dot(queries, key_rows.T, preferred_element_type=jnp.float32) * factor
    weights = jnp.where(live_keys[None, :], jnp.exp(scores), 0.0)
    softmax = weights / lax.optimization_barrier(jnp.sum(weights, axis=1, keepdims=True))
    soft_low = softmax.astype(jnp.bfloat16)
    return (softmax, soft_low, jnp.dot(soft_low, value_rows, preferred_element_type=jnp.float32))

def attend_forward(queries, key_rows, value_rows, live_keys):
    return (attend(queries, key_rows, value_rows, live_keys)[2],)

def attend_back(queries, key_rows, value_rows, grad_rows, live_keys):
    factor = queries.shape[-1] ** (-0.5)
    softmax, soft_low, outputs = attend(queries, key_rows, value_rows, live_keys)
    row_delta = lax.optimization_barrier(jnp.sum(grad_rows.astype(jnp.float32) * outputs, axis=1, keepdims=True))
    grad_soft = jnp.dot(grad_rows, value_rows.T, preferred_element_type=jnp.float32)
    grad_scores = (softmax * (grad_soft - row_delta)).astype(jnp.bfloat16)
    grad_queries = jnp.dot(grad_scores, key_rows, preferred_element_type=jnp.float32) * factor
    grad_keys = jnp.dot(grad_scores.T, queries, preferred_element_type=jnp.float32) * factor
    grad_values = jnp.dot(soft_low.T, grad_rows, preferred_element_type=jnp.float32)
    return (grad_queries, grad_keys, grad_values)

def by_cluster(tile_cluster, tensors, step, result_count):
    tile_ids = jnp.arange(NT, dtype=jnp.int32)
    lanes = jnp.arange(TILE, dtype=jnp.int32)
    slot_ids = jnp.arange(CAP, dtype=jnp.int32)
    in_axes = tuple((0 for tensor in tensors)) + (None,)

    def visit(totals, cluster):
        inside = tile_cluster == cluster
        members = jnp.argsort(jnp.where(inside, tile_ids, NT + tile_ids), stable=True)[:CAP].astype(jnp.int32)
        live_tiles = slot_ids < jnp.sum(inside.astype(jnp.int32))
        rows = (members[:, None] * TILE + lanes[None, :]).reshape(CAP * TILE)
        live_rows = jnp.repeat(live_tiles, TILE)
        pieces = []
        for tensor in tensors:
            picked = jnp.where(live_rows[:, None], tensor[rows], 0)
            pieces.append(picked.reshape(CAP * TILE, HEADS, HD).transpose(1, 0, 2))
        results = jax.vmap(step, in_axes=in_axes)(*pieces, live_rows)
        merged = tuple((total.at[rows].add(jnp.where(live_rows[:, None], part.transpose(1, 0, 2).reshape(CAP * TILE, INNER), 0.0)) for total, part in zip(totals, results)))
        return (merged, None)
    start = tuple((jnp.zeros((TOKENS, INNER), jnp.float32) for index in range(result_count)))
    totals, unused = lax.scan(visit, start, jnp.arange(CLUSTERS, dtype=jnp.int32))
    return totals

def split_heads(mixed):
    queries = head_norm(mixed[:, :INNER]).astype(jnp.bfloat16)
    key_rows = head_norm(mixed[:, INNER:2 * INNER]).astype(jnp.bfloat16)
    value_rows = mixed[:, 2 * INNER:].astype(jnp.bfloat16)
    return (queries, key_rows, value_rows)

def project(current, w_mix):
    normed = row_norm(current.astype(jnp.float32)).astype(jnp.bfloat16)
    return jnp.dot(normed, w_mix.T, preferred_element_type=jnp.float32)

def forward_section(current, w_mix, w_fin, tile_cluster):
    mixed = project(current, w_mix)
    queries, key_rows, value_rows = split_heads(mixed)
    totals = by_cluster(tile_cluster, (queries, key_rows, value_rows), attend_forward, 1)
    attention = totals[0].astype(jnp.bfloat16)
    return (current.astype(jnp.float32) + jnp.dot(attention, w_fin, preferred_element_type=jnp.float32)).astype(jnp.bfloat16)

def backward_section(stored, upstream, w_mix, w_fin, tile_cluster):
    mixed = project(stored, w_mix)
    queries, key_rows, value_rows = split_heads(mixed)
    grad_attention = jnp.dot(upstream, w_fin.T, preferred_element_type=jnp.float32).astype(jnp.bfloat16)
    totals = by_cluster(tile_cluster, (queries, key_rows, value_rows, grad_attention), attend_back, 3)
    grad_queries = totals[0].astype(jnp.bfloat16)
    grad_keys = totals[1].astype(jnp.bfloat16)
    grad_values = totals[2].astype(jnp.bfloat16)
    unused, pull_query = jax.vjp(head_norm, mixed[:, :INNER])
    unused, pull_key = jax.vjp(head_norm, mixed[:, INNER:2 * INNER])
    grad_mixed = jnp.concatenate([pull_query(grad_queries.astype(jnp.float32))[0], pull_key(grad_keys.astype(jnp.float32))[0], grad_values.astype(jnp.float32)], axis=1).astype(jnp.bfloat16)
    grad_normed = jnp.dot(grad_mixed, w_mix, preferred_element_type=jnp.float32)
    unused, pull_norm = jax.vjp(row_norm, stored.astype(jnp.float32))
    grad_norm_in = pull_norm(grad_normed)[0]
    return (upstream.astype(jnp.float32) + grad_norm_in).astype(jnp.bfloat16)

def reference(section_input, saved_input, grad_output, w_qkv, w_out, tile_cluster):
    forward_outs = []
    backward_outs = []
    for section in range(SECTIONS):
        forward_outs.append(forward_section(section_input[section], w_qkv[section], w_out[section], tile_cluster))
        backward_outs.append(backward_section(saved_input[section], grad_output[section], w_qkv[section], w_out[section], tile_cluster))
    blank = jnp.zeros((TOKENS, D), jnp.bfloat16)
    next_input = jnp.stack([blank] + forward_outs[:-1])
    grad_input = jnp.stack(backward_outs[1:] + [blank])
    return (next_input, grad_input)
```

```python
import functools

import jax
import jax.numpy as jnp
from jax import lax
from jax.experimental import pallas as pl
from jax.experimental.pallas import tpu as pltpu
from jax.sharding import PartitionSpec as P

HEADS = 8
HD = 128
TILE = 128
EPSILON = 1e-05
VMEM_LIMIT = 48 * 1024 * 1024
NT = (((1,), (1,)), ((), ()))
NN = (((1,), (0,)), ((), ()))
TN = (((0,), (0,)), ((), ()))


def dot(left, right, dims):
    return lax.dot_general(left, right, dims, preferred_element_type=jnp.float32)


def vmem():
    return pl.BlockSpec(memory_space=pltpu.VMEM)


def params():
    return pltpu.CompilerParams(vmem_limit_bytes=VMEM_LIMIT)


def rows_rsqrt(values):
    return lax.rsqrt(jnp.mean(values * values, axis=-1, keepdims=True) + EPSILON)


def project_kernel(parts, group, *refs):
    if parts == 4:
        x_ref, up_ref, w_ref, wo_ref, out_ref, scale_ref, normed = refs
    else:
        x_ref, w_ref, out_ref, normed = refs
    part, block = pl.program_id(0), pl.program_id(1)

    @pl.when((part == 0) & (block == 0))
    def _():
        x = x_ref[...].astype(jnp.float32)
        normed[...] = (x * rows_rsqrt(x)).astype(jnp.bfloat16)

    @pl.when(part < 3)
    def _():
        mixed = dot(normed[...], w_ref[...], NT)
        for j in range(group):
            u = mixed[:, j * HD : (j + 1) * HD]
            scale = jnp.where(part < 2, rows_rsqrt(u), 1.0)
            out_ref[j, 0] = (u * scale).astype(jnp.bfloat16)
            if parts == 4:
                lane = lax.broadcasted_iota(jnp.int32, (u.shape[0], HD), 1)
                column = part * HEADS + block * group + j

                @pl.when(part < 2)
                def _():
                    scale_ref[...] = jnp.where(lane == column, scale, scale_ref[...])

    if parts == 4:

        @pl.when(part == 3)
        def _():
            g = dot(up_ref[...], wo_ref[...], NT)
            for j in range(group):
                out_ref[j, 0] = g[:, j * HD : (j + 1) * HD].astype(jnp.bfloat16)


def project(x, w_rows, up=None, w_fin=None):
    tokens, width = x.shape
    group = 4
    blocks = HEADS // group
    parts = 3 if up is None else 4
    whole = pl.BlockSpec((tokens, width), lambda p, b: (0, 0))
    w_spec = pl.BlockSpec(
        (group * HD, width),
        lambda p, b: (jnp.where(p < 3, p * blocks + b, 3 * blocks - 1), 0),
    )
    wo_spec = pl.BlockSpec((group * HD, width), lambda p, b: (jnp.where(p < 3, 0, b), 0))
    out_spec = pl.BlockSpec((group, 1, tokens, HD), lambda p, b: (b, p, 0, 0))
    out = jax.ShapeDtypeStruct((HEADS, parts, tokens, HD), jnp.bfloat16)
    if up is None:
        operands, in_specs = (x, w_rows), [whole, w_spec]
        outs, out_specs = out, out_spec
    else:
        operands, in_specs = (x, up, w_rows, w_fin), [whole, whole, w_spec, wo_spec]
        outs = (out, jax.ShapeDtypeStruct((tokens, HD), jnp.float32))
        out_specs = (out_spec, pl.BlockSpec((tokens, HD), lambda p, b: (0, 0)))
    return pl.pallas_call(
        functools.partial(project_kernel, parts, group),
        grid=(parts, blocks),
        in_specs=in_specs,
        out_specs=out_specs,
        out_shape=outs,
        scratch_shapes=[pltpu.VMEM((tokens, width), jnp.bfloat16)],
        compiler_params=params(),
        cost_estimate=pl.CostEstimate(
            flops=2 * parts * tokens * width * HEADS * HD,
            bytes_accessed=2 * parts * width * HEADS * HD,
            transcendentals=0,
        ),
    )(*operands)


def forward_body(n, tiles, in_ref, out_ref):
    def load(c):
        return jnp.concatenate([in_ref[t // 2, c, t % 2] for t in tiles], axis=0)

    q, k, v = load(0), load(1), load(2)
    weights = jnp.exp(dot(q, k, NT) * (HD ** -0.5)).astype(jnp.bfloat16)
    wide = jnp.concatenate([v, jnp.ones_like(v)], axis=1)
    sums = dot(weights, wide, NN)
    result = (sums[:, :HD] / sums[:, HD:]).astype(jnp.bfloat16)
    for i, t in enumerate(tiles):
        out_ref[t // 2, 0, t % 2] = result[i * TILE : (i + 1) * TILE]


def backward_body(n, tiles, in_ref, out_ref):
    def load(c):
        return jnp.concatenate([in_ref[t // 2, c, t % 2] for t in tiles], axis=0)

    q, k, v, g = load(0), load(1), load(2), load(3)
    factor = HD ** -0.5
    weights = jnp.exp(dot(k, q, NT) * factor)
    softmax = weights * (1.0 / jnp.sum(weights, axis=0, keepdims=True))
    soft_low = softmax.astype(jnp.bfloat16)
    grad_soft = dot(v, g, NT)
    delta = jnp.sum(soft_low.astype(jnp.float32) * grad_soft, axis=0, keepdims=True)
    grad_scores = (softmax * (grad_soft - delta)).astype(jnp.bfloat16)
    results = (
        dot(grad_scores, k, TN) * factor,
        dot(grad_scores, q, NN) * factor,
        dot(soft_low, g, NN),
    )
    for c, result in enumerate(results):
        low = result.astype(jnp.bfloat16)
        for i, t in enumerate(tiles):
            out_ref[t // 2, c, t % 2] = low[i * TILE : (i + 1) * TILE]


def attend_kernel(body, clusters, capacity, spacing, cluster_ref, res_ref, in_ref, out_ref, count, member):
    tiles = in_ref.shape[0] * in_ref.shape[2]
    for c in range(clusters):
        count[c] = 0

    def enter(t, carry):
        c = cluster_ref[t * spacing + res_ref[0]] // spacing
        place = count[c]
        member[c * capacity + place] = t
        count[c] = place + 1
        return carry

    lax.fori_loop(0, tiles, enter, 0)

    def visit(c, carry):
        for n in range(1, capacity + 1):

            @pl.when(count[c] == n)
            def _():
                body(n, [member[c * capacity + i] for i in range(n)], in_ref, out_ref)

        return carry

    lax.fori_loop(0, clusters, visit, 0)


def attend(body, tile_cluster, residue, arrived, spacing, parts_out, flops):
    sources, parts, tokens, _ = arrived.shape
    tiled = arrived.reshape(sources * tokens // (2 * TILE), parts, 2, TILE, HD)
    tiles = 2 * tiled.shape[0]
    clusters = tiles // 2
    capacity = 3
    smem = pl.BlockSpec(memory_space=pltpu.SMEM)
    out = pl.pallas_call(
        functools.partial(attend_kernel, body, clusters, capacity, spacing),
        in_specs=[smem, smem, vmem()],
        out_specs=vmem(),
        out_shape=jax.ShapeDtypeStruct((tiled.shape[0], parts_out, 2, TILE, HD), jnp.bfloat16),
        scratch_shapes=[
            pltpu.SMEM((clusters,), jnp.int32),
            pltpu.SMEM((clusters * capacity,), jnp.int32),
        ],
        compiler_params=params(),
        cost_estimate=pl.CostEstimate(flops=flops, bytes_accessed=1 << 21, transcendentals=0),
    )(tile_cluster, residue, tiled)
    return out.reshape(tiled.shape[0], parts_out, 2 * TILE, HD)


def finish_kernel(att_ref, x_ref, w_ref, out_ref):
    att = jnp.concatenate([att_ref[h, 0] for h in range(HEADS)], axis=1)
    update = dot(att, w_ref[...], NN)
    out_ref[...] = (x_ref[...].astype(jnp.float32) + update).astype(jnp.bfloat16)


def finish(attention, current, w_fin):
    tokens, width = current.shape
    block = 256
    return pl.pallas_call(
        finish_kernel,
        grid=(width // block,),
        in_specs=[
            pl.BlockSpec((HEADS, 1, tokens, HD), lambda b: (0, 0, 0, 0)),
            pl.BlockSpec((tokens, block), lambda b: (0, b)),
            pl.BlockSpec((HEADS * HD, block), lambda b: (0, b)),
        ],
        out_specs=pl.BlockSpec((tokens, block), lambda b: (0, b)),
        out_shape=jax.ShapeDtypeStruct((tokens, width), jnp.bfloat16),
        compiler_params=params(),
        cost_estimate=pl.CostEstimate(flops=1 << 29, bytes_accessed=1 << 22, transcendentals=0),
    )(attention, current, w_fin)


def finish_back_kernel(group, grad_ref, kept_ref, scale_ref, x_ref, up_ref, w_ref, out_ref, total):
    part, block = pl.program_id(0), pl.program_id(1)
    blocks = pl.num_programs(1)
    pieces = []
    lane = lax.broadcasted_iota(jnp.int32, scale_ref.shape, 1)
    for j in range(group):
        g = grad_ref[j, 0].astype(jnp.float32)
        unit = kept_ref[j, 0].astype(jnp.float32)
        column = part * HEADS + block * group + j
        scale = jnp.sum(jnp.where(lane == column, scale_ref[...], 0.0), axis=1, keepdims=True)
        pulled = scale * (g - unit * jnp.mean(unit * g, axis=1, keepdims=True))
        pieces.append(jnp.where(part < 2, pulled, g).astype(jnp.bfloat16))
    product = dot(jnp.concatenate(pieces, axis=1), w_ref[...], NN)
    first = (part == 0) & (block == 0)

    @pl.when(first)
    def _():
        total[...] = product

    @pl.when(jnp.logical_not(first))
    def _():
        total[...] += product

    @pl.when((part == 2) & (block == blocks - 1))
    def _():
        x = x_ref[...].astype(jnp.float32)
        scale = rows_rsqrt(x)
        unit = x * scale
        g = total[...]
        pulled = scale * (g - unit * jnp.mean(unit * g, axis=1, keepdims=True))
        out_ref[...] = (up_ref[...].astype(jnp.float32) + pulled).astype(jnp.bfloat16)


def finish_back(grads, kept, scales, stored, upstream, w_rows):
    tokens, width = stored.shape
    group = 4
    blocks = HEADS // group
    whole = pl.BlockSpec((tokens, width), lambda p, b: (0, 0))
    heads = pl.BlockSpec((group, 1, tokens, HD), lambda p, b: (b, p, 0, 0))
    return pl.pallas_call(
        functools.partial(finish_back_kernel, group),
        grid=(3, blocks),
        in_specs=[
            heads,
            heads,
            pl.BlockSpec((tokens, HD), lambda p, b: (0, 0)),
            whole,
            whole,
            pl.BlockSpec((group * HD, width), lambda p, b: (p * blocks + b, 0)),
        ],
        out_specs=whole,
        out_shape=jax.ShapeDtypeStruct((tokens, width), jnp.bfloat16),
        scratch_shapes=[pltpu.VMEM((tokens, width), jnp.float32)],
        compiler_params=params(),
        cost_estimate=pl.CostEstimate(flops=3 << 29, bytes_accessed=1 << 23, transcendentals=0),
    )(grads, kept, scales, stored, upstream, w_rows)


def all_swap(blocks):
    return lax.all_to_all(blocks, "seq", split_axis=0, concat_axis=0, tiled=True)


def to_heads(headed, own, spacing):
    if spacing == 1:
        return all_swap(headed)
    heads, parts, tokens, _ = headed.shape
    held = tokens // TILE
    places = spacing // held
    tiled = headed.reshape(heads, parts, held, TILE, HD).transpose(0, 2, 1, 3, 4)
    padded = jnp.zeros((heads, places, held, parts, TILE, HD), headed.dtype)
    padded = lax.dynamic_update_slice_in_dim(padded, tiled[:, None], own % places, 1)
    arrived = all_swap(padded.reshape(heads * spacing, parts, TILE, HD))
    arrived = arrived.reshape(-1, places, parts, TILE, HD)
    mine = lax.dynamic_index_in_dim(arrived, own % spacing // held, 1, keepdims=False)
    paired = mine.reshape(-1, 2, parts, TILE, HD).transpose(0, 2, 1, 3, 4)
    return paired.reshape(-1, parts, 2 * TILE, HD)


def to_tokens(results, own, spacing, tokens):
    if spacing == 1:
        return all_swap(results)
    sources, parts, _, _ = results.shape
    held = tokens // TILE
    places = spacing // held
    tiled = results.reshape(sources, parts, 2, TILE, HD).transpose(0, 2, 1, 3, 4)
    tiled = tiled.reshape(-1, 1, parts, TILE, HD)
    padded = jnp.zeros((tiled.shape[0], places, parts, TILE, HD), results.dtype)
    padded = lax.dynamic_update_slice_in_dim(padded, tiled, own % spacing // held, 1)
    returned = all_swap(padded.reshape(-1, parts, TILE, HD))
    returned = returned.reshape(HEADS, places, held, parts, TILE, HD)
    mine = lax.dynamic_index_in_dim(returned, own % places, 1, keepdims=False)
    return mine.transpose(0, 2, 1, 3, 4).reshape(HEADS, parts, tokens, HD)


def passed_along(block, axis, distance):
    devices = range(lax.axis_size(axis))
    route = [(i - distance, i) for i in devices if i - distance in devices]
    return lax.ppermute(block, axis, route)


def per_device(section_input, saved_input, grad_output, w_qkv, w_out, tile_cluster):
    current, stored, upstream = section_input[0], saved_input[0], grad_output[0]
    w_rows, w_fin = w_qkv[0], w_out[0]
    tokens = current.shape[0]
    spacing = lax.axis_size("seq") // HEADS
    own = lax.axis_index("seq")
    residue = (own % spacing).astype(jnp.int32)[None]
    visit = functools.partial(attend, spacing=spacing)

    sent = project(current, w_rows)
    arrived = to_heads(sent, own, spacing)
    sent_back, scales = project(stored, w_rows, upstream, w_fin)
    arrived_back = to_heads(sent_back, own, spacing)
    outputs = visit(forward_body, tile_cluster, residue, arrived, parts_out=1, flops=1 << 30)
    returned = to_tokens(outputs, own, spacing, tokens)
    grads = visit(backward_body, tile_cluster, residue, arrived_back, parts_out=3, flops=3 << 30)
    returned_back = to_tokens(grads, own, spacing, tokens)
    result = finish(returned, current, w_fin)
    next_input = passed_along(result, "pipe", 1)
    grad_self = finish_back(returned_back, sent_back, scales, stored, upstream, w_rows)
    grad_input = passed_along(grad_self, "pipe", -1)
    return (next_input[None], grad_input[None])


def solution(mesh):
    return jax.shard_map(
        per_device,
        mesh=mesh,
        in_specs=(
            P("pipe", "seq", None),
            P("pipe", "seq", None),
            P("pipe", "seq", None),
            P("pipe", None, None),
            P("pipe", None, None),
            P(),
        ),
        out_specs=(P("pipe", "seq", None), P("pipe", "seq", None)),
        check_vma=False,
    )
```

```python
import functools

import jax
import jax.numpy as jnp
from jax import lax
from jax.experimental import pallas as pl
from jax.experimental.pallas import tpu as pltpu
from jax.sharding import PartitionSpec as P

HEADS = 8
HD = 128
TILE = 128
CAPACITY = 3
EPSILON = 1e-05
VMEM_LIMIT = 40 * 1024 * 1024
NT = (((1,), (1,)), ((), ()))
NN = (((1,), (0,)), ((), ()))
TN = (((0,), (0,)), ((), ()))
ANY = pl.BlockSpec(memory_space=pl.ANY)
SMEM = pl.BlockSpec(memory_space=pltpu.SMEM)
VMEM = pl.BlockSpec(memory_space=pltpu.VMEM)


def dot(left, right, dims):
    return lax.dot_general(left, right, dims, preferred_element_type=jnp.float32)


def low(values):
    return values.astype(jnp.bfloat16)


def high(values):
    return values.astype(jnp.float32)


def rows_rsqrt(values):
    return lax.rsqrt(jnp.mean(values * values, axis=-1, keepdims=True) + EPSILON)


def call(kernel, operands, in_specs, out_shape, scratch, flops, moved):
    many = isinstance(out_shape, tuple)
    return pl.pallas_call(
        kernel,
        in_specs=in_specs,
        out_specs=tuple(VMEM for _ in out_shape) if many else VMEM,
        out_shape=out_shape,
        scratch_shapes=scratch,
        compiler_params=pltpu.CompilerParams(vmem_limit_bytes=VMEM_LIMIT),
        cost_estimate=pl.CostEstimate(flops=flops, bytes_accessed=moved, transcendentals=0),
    )(*operands)


def fetch(source, target, sem):
    copy = pltpu.make_async_copy(source, target, sem)
    copy.start()
    return copy


def forward_cluster(tiles, kept, out):
    def load(c):
        return jnp.concatenate([kept[t, :, c * HD : (c + 1) * HD] for t in tiles], axis=0)

    q, k, v = load(0), load(1), load(2)
    weights = low(jnp.exp(dot(q, k, NT) * (HD ** -0.5)))
    wide = jnp.concatenate([v, jnp.ones_like(v)], axis=1)
    sums = dot(weights, wide, NN)
    result = low(sums[:, :HD] / sums[:, HD:])
    for i, t in enumerate(tiles):
        out[t] = result[i * TILE : (i + 1) * TILE]


def backward_cluster(tiles, kept, out, scales, grads):
    def load(c):
        return jnp.concatenate([kept[t, :, c * HD : (c + 1) * HD] for t in tiles], axis=0)

    def scale(c):
        return jnp.concatenate([scales[t, :, c * HD : (c + 1) * HD] for t in tiles], axis=0)

    q, k, v = load(0), load(1), load(2)
    g = jnp.concatenate([grads[t] for t in tiles], axis=0)
    factor = HD ** -0.5
    weights = jnp.exp(dot(k, q, NT) * factor)
    softmax = weights * (1.0 / jnp.sum(weights, axis=0, keepdims=True))
    soft_low = low(softmax)
    grad_soft = dot(v, g, NT)
    delta = jnp.sum(high(soft_low) * grad_soft, axis=0, keepdims=True)
    grad_scores = low(softmax * (grad_soft - delta))
    grad_values = low(dot(soft_low, g, NN))
    results = [grad_values]
    for c, unit, grad in (
        (1, k, dot(grad_scores, q, NN)),
        (0, q, dot(grad_scores, k, TN)),
    ):
        rounded = high(low(grad * factor))
        unit = high(unit)
        mean = jnp.mean(unit * rounded, axis=1, keepdims=True)
        results.append(low(scale(c) * (rounded - unit * mean)))
    for c, result in zip((2, 1, 0), results):
        for i, t in enumerate(tiles):
            out[t, :, c * HD : (c + 1) * HD] = result[i * TILE : (i + 1) * TILE]


def head_kernel(back, pieces, spacing, *refs):
    refs = list(refs)
    cluster_ref, info_ref = refs[:2]
    x_refs = refs[2 : 2 + len(pieces)]
    refs = refs[2 + len(pieces) :]
    g_refs = [refs.pop(0) for _ in range(HEADS if back else 0)]
    w_ref = refs.pop(0)
    out_refs = [refs.pop(0) for _ in range(HEADS)]
    xbuf, wbuf, turned, kept, out, count, member, xsem, wsem = refs[:9]
    flip, head, residue = info_ref[0], info_ref[1], info_ref[2]
    tiles = kept.shape[0]
    clusters = count.shape[0]

    weights = fetch(w_ref.at[:, head], wbuf, wsem)
    copies = []
    for i, (k, start, rows) in enumerate(pieces):
        copies.append(fetch(x_refs[i], xbuf.at[k, pl.ds(start, rows)], xsem.at[i]))
    if back:
        scales, grads, gsem = refs[9:]
        g_copies = []
        for k in range(HEADS):
            g_copies.append(fetch(g_refs[k], grads.at[pl.ds(2 * (flip ^ k), 2)], gsem.at[k]))

    for c in range(clusters):
        count[c] = 0

    def enter(t, carry):
        c = cluster_ref[t * spacing + residue] // spacing
        place = count[c]
        member[c * CAPACITY + place] = t
        count[c] = place + 1
        return carry

    lax.fori_loop(0, tiles, enter, 0)

    weights.wait()
    turned[...] = wbuf[...].reshape(3 * HD, -1).T

    def project(k, carry):
        for (slot, _, _), copy in zip(pieces, copies):
            pl.when(k == slot)(copy.wait)
        x = high(xbuf[k])
        mixed = dot(low(x * rows_rsqrt(x)), turned[...], NN)
        place = 2 * (flip ^ k)
        for c in range(3):
            u = mixed[:, c * HD : (c + 1) * HD]
            if c < 2:
                scale = rows_rsqrt(u)
                u = u * scale
            for j in range(2):
                kept[place + j, :, c * HD : (c + 1) * HD] = low(u[j * TILE : (j + 1) * TILE])
                if back and c < 2:
                    scales[place + j, :, c * HD : (c + 1) * HD] = jnp.broadcast_to(
                        scale[j * TILE : (j + 1) * TILE], (TILE, HD)
                    )
        return carry

    lax.fori_loop(0, HEADS, project, 0)
    if back:
        for copy in g_copies:
            copy.wait()

    def visit(c, carry):
        for n in range(1, CAPACITY + 1):

            @pl.when(count[c] == n)
            def _():
                held = [member[c * CAPACITY + i] for i in range(n)]
                if back:
                    backward_cluster(held, kept, out, scales, grads)
                else:
                    forward_cluster(held, kept, out)

        return carry

    lax.fori_loop(0, clusters, visit, 0)
    for k in range(HEADS):
        out_refs[k][...] = out[pl.ds(2 * (flip ^ k), 2)].reshape(out_refs[k].shape)


def head_work(info, tile_cluster, pieces, w_qkv, spacing, grads=None):
    back = grads is not None
    width = w_qkv.shape[1]
    tiles = 2 * HEADS
    wide = 3 * HD if back else HD
    tokens = tiles * TILE
    operands = [tile_cluster, info] + [array for _, _, array in pieces]
    if back:
        operands += [g.reshape(2, TILE, HD) for g in grads]
    operands.append(w_qkv.reshape(3, HEADS, HD, width))
    shapes = tuple((k, start, array.shape[0]) for k, start, array in pieces)
    scratch = [
        pltpu.VMEM((HEADS, 2 * TILE, width), jnp.bfloat16),
        pltpu.VMEM((3, HD, width), jnp.bfloat16),
        pltpu.VMEM((width, 3 * HD), jnp.bfloat16),
        pltpu.VMEM((tiles, TILE, 3 * HD), jnp.bfloat16),
        pltpu.VMEM((tiles, TILE, wide), jnp.bfloat16),
        pltpu.SMEM((tiles // 2,), jnp.int32),
        pltpu.SMEM((tiles // 2 * CAPACITY,), jnp.int32),
        pltpu.SemaphoreType.DMA((len(pieces),)),
        pltpu.SemaphoreType.DMA,
    ]
    if back:
        scratch += [
            pltpu.VMEM((tiles, TILE, 2 * HD), jnp.float32),
            pltpu.VMEM((tiles, TILE, HD), jnp.bfloat16),
            pltpu.SemaphoreType.DMA((HEADS,)),
        ]
    return call(
        functools.partial(head_kernel, back, shapes, spacing),
        operands,
        [SMEM, SMEM] + [ANY] * (len(operands) - 2),
        tuple(jax.ShapeDtypeStruct((2 * TILE, wide), jnp.bfloat16) for _ in range(HEADS)),
        scratch,
        2 * tokens * width * 3 * HD + tokens * 512 * HD * (14 if back else 4),
        2 * tokens * (width + 2 * wide),
    )


def spread_kernel(info_ref, up_ref, w_ref, *refs):
    out_refs, (up, rows, up_sem, sems) = refs[:HEADS], refs[HEADS:]
    flip = info_ref[0]
    up_copy = fetch(up_ref, up, up_sem)
    copies = [fetch(w_ref.at[flip ^ k], rows.at[k], sems.at[k]) for k in range(HEADS)]
    up_copy.wait()
    for k in range(0, HEADS, 2):
        copies[k].wait()
        copies[k + 1].wait()
        pair = rows[k : k + 2].reshape(2 * HD, -1)
        g = low(dot(up[...], pair, NT))
        out_refs[k][...] = g[:, :HD]
        out_refs[k + 1][...] = g[:, HD:]


def spread_grads(info, upstream, w_fin):
    tokens, width = upstream.shape
    return call(
        spread_kernel,
        [info, upstream, w_fin.reshape(HEADS, HD, width)],
        [SMEM, ANY, ANY],
        tuple(jax.ShapeDtypeStruct((tokens, HD), jnp.bfloat16) for _ in range(HEADS)),
        [
            pltpu.VMEM((tokens, width), jnp.bfloat16),
            pltpu.VMEM((HEADS, HD, width), jnp.bfloat16),
            pltpu.SemaphoreType.DMA,
            pltpu.SemaphoreType.DMA((HEADS,)),
        ],
        2 * tokens * width * HEADS * HD,
        2 * width * HEADS * HD,
    )


def finish_kernel(info_ref, *refs):
    att_refs, (x_ref, w_ref, out_ref, rows, sems) = refs[:HEADS], refs[HEADS:]
    flip = info_ref[0]
    copies = [fetch(w_ref.at[flip ^ k], rows.at[k], sems.at[k]) for k in range(HEADS)]
    att = jnp.concatenate([ref[...] for ref in att_refs], axis=1)
    for copy in copies:
        copy.wait()
    width = x_ref.shape[1]
    block = 256
    for start in range(0, width, block):
        columns = slice(start, start + block)
        w = rows[:, :, columns].reshape(HEADS * HD, block)
        out_ref[:, columns] = low(high(x_ref[:, columns]) + dot(att, w, NN))


def finish(info, attention, current, w_fin):
    tokens, width = current.shape
    return call(
        finish_kernel,
        [info, *attention, current, w_fin.reshape(HEADS, HD, width)],
        [SMEM] + [VMEM] * (HEADS + 1) + [ANY],
        jax.ShapeDtypeStruct((tokens, width), jnp.bfloat16),
        [
            pltpu.VMEM((HEADS, HD, width), jnp.bfloat16),
            pltpu.SemaphoreType.DMA((HEADS,)),
        ],
        2 * tokens * width * HEADS * HD,
        2 * width * HEADS * HD,
    )


def finish_back_kernel(info_ref, *refs):
    grad_refs, (x_ref, up_ref, w_ref, out_ref, rows, total, sems) = refs[:HEADS], refs[HEADS:]
    flip = info_ref[0]
    copies = [fetch(w_ref.at[:, flip ^ k], rows.at[k], sems.at[k]) for k in range(HEADS)]
    width = x_ref.shape[1]
    for k in range(0, HEADS, 2):
        copies[k].wait()
        copies[k + 1].wait()
        grads = jnp.concatenate([grad_refs[k][...], grad_refs[k + 1][...]], axis=1)
        product = dot(grads, rows[k : k + 2].reshape(6 * HD, width), NN)
        if k == 0:
            total[...] = product
        else:
            total[...] += product
    x = high(x_ref[...])
    scale = rows_rsqrt(x)
    unit = x * scale
    g = total[...]
    pulled = scale * (g - unit * jnp.mean(unit * g, axis=1, keepdims=True))
    out_ref[...] = low(high(up_ref[...]) + pulled)


def finish_back(info, grads, stored, upstream, w_qkv):
    tokens, width = stored.shape
    return call(
        finish_back_kernel,
        [info, *grads, stored, upstream, w_qkv.reshape(3, HEADS, HD, width)],
        [SMEM] + [VMEM] * (HEADS + 2) + [ANY],
        jax.ShapeDtypeStruct((tokens, width), jnp.bfloat16),
        [
            pltpu.VMEM((HEADS, 3, HD, width), jnp.bfloat16),
            pltpu.VMEM((tokens, width), jnp.float32),
            pltpu.SemaphoreType.DMA((HEADS,)),
        ],
        2 * tokens * width * 3 * HEADS * HD,
        6 * width * HEADS * HD,
    )


def partner(block, distance):
    route = [(i, i ^ distance) for i in range(lax.axis_size("seq"))]
    return lax.ppermute(block, "seq", route)


def gather_rows(x):
    half = x.shape[0] // 2
    over_x, over_y = partner(x, 2), partner(x, 4)
    top, bottom = partner(over_x[:half], 4), partner(over_y[half:], 2)
    pieces = [(0, 0, x), (2, 0, over_x), (4, 0, over_y), (6, 0, top), (6, half, bottom)]
    return pieces + [(k + 1, start, partner(block, 1)) for k, start, block in pieces]


def swap(blocks):
    moved = {k: partner(blocks[k], k) for k in (2, 4, 6, 3, 5, 7, 1)}
    return [blocks[0]] + [moved[k] for k in range(1, HEADS)]


def all_swap(blocks):
    return lax.all_to_all(blocks, "seq", split_axis=0, concat_axis=0, tiled=True)


def to_heads(blocks, own, spacing):
    heads, tokens, width = blocks.shape
    held = tokens // TILE
    places = spacing // held
    tiled = blocks.reshape(heads, 1, held, TILE, width)
    padded = jnp.zeros((heads, places, held, TILE, width), blocks.dtype)
    padded = lax.dynamic_update_slice_in_dim(padded, tiled, own % places, 1)
    arrived = all_swap(padded.reshape(heads * spacing, TILE, width))
    arrived = arrived.reshape(-1, places, TILE, width)
    mine = lax.dynamic_index_in_dim(arrived, own % spacing // held, 1, keepdims=False)
    return list(mine.reshape(HEADS, 2 * TILE, width))


def to_tokens(blocks, own, spacing, tokens):
    held = tokens // TILE
    places = spacing // held
    tiled = jnp.stack(blocks).reshape(2 * HEADS, 1, TILE, -1)
    padded = jnp.zeros((2 * HEADS, places, TILE, tiled.shape[3]), tiled.dtype)
    padded = lax.dynamic_update_slice_in_dim(padded, tiled, own % spacing // held, 1)
    returned = all_swap(padded.reshape(-1, TILE, tiled.shape[3]))
    returned = returned.reshape(HEADS, places, held * TILE, tiled.shape[3])
    return list(lax.dynamic_index_in_dim(returned, own % places, 1, keepdims=False))


def passed_along(block, axis, distance):
    devices = range(lax.axis_size(axis))
    route = [(i - distance, i) for i in devices if i - distance in devices]
    return lax.ppermute(block, axis, route)


def per_device(section_input, saved_input, grad_output, w_qkv, w_out, tile_cluster):
    current, stored, upstream = section_input[0], saved_input[0], grad_output[0]
    w_rows, w_fin = w_qkv[0], w_out[0]
    tokens = current.shape[0]
    spacing = lax.axis_size("seq") // HEADS
    own = lax.axis_index("seq").astype(jnp.int32)
    if spacing == 1:
        info = jnp.stack([own, own, jnp.zeros_like(own)])
        gather, spread, collect = gather_rows, swap, swap
    else:
        info = jnp.stack([jnp.zeros_like(own), own // spacing, own % spacing])

        def gather(x):
            copies = jnp.broadcast_to(x, (HEADS, *x.shape))
            return [(k, 0, b) for k, b in enumerate(to_heads(copies, own, spacing))]

        def spread(blocks):
            return to_heads(jnp.stack(blocks), own, spacing)

        def collect(blocks):
            return to_tokens(blocks, own, spacing, tokens)

    stored_pieces = gather(stored)
    grad_attention = spread(spread_grads(info, upstream, w_fin))
    current_pieces = gather(current)
    grads = head_work(info, tile_cluster, stored_pieces, w_rows, spacing, grad_attention)
    returned_grads = collect(grads)
    outputs = head_work(info, tile_cluster, current_pieces, w_rows, spacing)
    returned = collect(outputs)
    grad_self = finish_back(info, returned_grads, stored, upstream, w_rows)
    grad_input = passed_along(grad_self, "pipe", -1)
    result = finish(info, returned, current, w_fin)
    next_input = passed_along(result, "pipe", 1)
    return (next_input[None], grad_input[None])


def solution(mesh):
    return jax.shard_map(
        per_device,
        mesh=mesh,
        in_specs=(
            P("pipe", "seq", None),
            P("pipe", "seq", None),
            P("pipe", "seq", None),
            P("pipe", None, None),
            P("pipe", None, None),
            P(),
        ),
        out_specs=(P("pipe", "seq", None), P("pipe", "seq", None)),
        check_vma=False,
    )
```

```python
import functools

import jax
import jax.numpy as jnp
from jax import lax
from jax.experimental import pallas as pl
from jax.experimental.pallas import tpu as pltpu
from jax.sharding import PartitionSpec as P

HEADS = 8
HD = 128
TILE = 128
CAPACITY = 3
EPSILON = 1e-05
VMEM_LIMIT = 24 * 1024 * 1024
NT = (((1,), (1,)), ((), ()))
NN = (((1,), (0,)), ((), ()))
TN = (((0,), (0,)), ((), ()))
HBM = pl.BlockSpec(memory_space=pltpu.HBM)
SMEM = pl.BlockSpec(memory_space=pltpu.SMEM)
VMEM = pl.BlockSpec(memory_space=pltpu.VMEM)


def dot(left, right, dims):
    return lax.dot_general(left, right, dims, preferred_element_type=jnp.float32)


def low(values):
    return values.astype(jnp.bfloat16)


def high(values):
    return values.astype(jnp.float32)


def rows_rsqrt(values):
    return lax.rsqrt(jnp.mean(values * values, axis=-1, keepdims=True) + EPSILON)


def call(kernel, operands, in_specs, out_shape, scratch, flops, moved):
    many = isinstance(out_shape, tuple)
    return pl.pallas_call(
        kernel,
        in_specs=in_specs,
        out_specs=tuple(VMEM for _ in out_shape) if many else VMEM,
        out_shape=out_shape,
        scratch_shapes=scratch,
        compiler_params=pltpu.CompilerParams(vmem_limit_bytes=VMEM_LIMIT),
        cost_estimate=pl.CostEstimate(flops=flops, bytes_accessed=moved, transcendentals=0),
    )(*operands)


def fetch(source, target, sem):
    copy = pltpu.make_async_copy(source, target, sem)
    copy.start()
    return copy


def forward_cluster(tiles, kept, out):
    def load(c):
        return jnp.concatenate([kept[t, :, c * HD : (c + 1) * HD] for t in tiles], axis=0)

    q, k, v = load(0), load(1), load(2)
    weights = low(jnp.exp(dot(q, k, NT) * (HD ** -0.5)))
    wide = jnp.concatenate([v, jnp.ones_like(v)], axis=1)
    sums = dot(weights, wide, NN)
    result = low(sums[:, :HD] / sums[:, HD:])
    for i, t in enumerate(tiles):
        out[t] = result[i * TILE : (i + 1) * TILE]


def backward_cluster(tiles, kept, out, scales, grads):
    def load(c):
        return jnp.concatenate([kept[t, :, c * HD : (c + 1) * HD] for t in tiles], axis=0)

    def scale(c):
        return jnp.concatenate([scales[t, :, c * HD : (c + 1) * HD] for t in tiles], axis=0)

    q, k, v = load(0), load(1), load(2)
    g = jnp.concatenate([grads[t] for t in tiles], axis=0)
    factor = HD ** -0.5
    weights = jnp.exp(dot(k, q, NT) * factor)
    softmax = weights * (1.0 / jnp.sum(weights, axis=0, keepdims=True))
    soft_low = low(softmax)
    grad_soft = dot(v, g, NT)
    delta = jnp.sum(high(soft_low) * grad_soft, axis=0, keepdims=True)
    grad_scores = low(softmax * (grad_soft - delta))
    grad_values = low(dot(soft_low, g, NN))
    results = [grad_values]
    for c, unit, grad in (
        (1, k, dot(grad_scores, q, NN)),
        (0, q, dot(grad_scores, k, TN)),
    ):
        rounded = high(low(grad * factor))
        unit = high(unit)
        mean = jnp.mean(unit * rounded, axis=1, keepdims=True)
        results.append(low(scale(c) * (rounded - unit * mean)))
    for c, result in zip((2, 1, 0), results):
        for i, t in enumerate(tiles):
            out[t, :, c * HD : (c + 1) * HD] = result[i * TILE : (i + 1) * TILE]


def head_kernel(back, pieces, spacing, *refs):
    cluster_ref, info_ref = refs[:2]
    x_refs = refs[2 : 2 + len(pieces)]
    refs = refs[2 + len(pieces) :]
    if back:
        g_ref, refs = refs[0], refs[1:]
    w_ref, out, xbuf, wbuf, turned, kept, count, member, xsem, wsem = refs[:10]
    flip, head, residue = info_ref[0], info_ref[1], info_ref[2]
    tiles = kept.shape[0]
    clusters = count.shape[0]

    weights = fetch(w_ref.at[:, head], wbuf, wsem)
    copies = []
    for i, (k, start, rows) in enumerate(pieces):
        copies.append(fetch(x_refs[i], xbuf.at[k, pl.ds(start, rows)], xsem.at[i]))
    if back:
        scales, grads, gsem = refs[10:]
        g_copy = fetch(g_ref, grads, gsem)

    for c in range(clusters):
        count[c] = 0

    def enter(t, carry):
        c = cluster_ref[t * spacing + residue] // spacing
        place = count[c]
        member[c * CAPACITY + place] = t
        count[c] = place + 1
        return carry

    lax.fori_loop(0, tiles, enter, 0)

    weights.wait()
    turned[...] = wbuf[...].reshape(3 * HD, -1).T

    def project(k, carry):
        for (slot, _, _), copy in zip(pieces, copies):
            pl.when(k == slot)(copy.wait)
        normed = xbuf[k]
        if back:
            x = high(normed)
            normed = low(x * rows_rsqrt(x))
        mixed = dot(normed, turned[...], NN)
        place = 2 * (flip ^ k)
        for c in range(3):
            u = mixed[:, c * HD : (c + 1) * HD]
            if c < 2:
                scale = rows_rsqrt(u)
                u = u * scale
            for j in range(2):
                kept[place + j, :, c * HD : (c + 1) * HD] = low(u[j * TILE : (j + 1) * TILE])
                if back and c < 2:
                    scales[place + j, :, c * HD : (c + 1) * HD] = jnp.broadcast_to(
                        scale[j * TILE : (j + 1) * TILE], (TILE, HD)
                    )
        return carry

    lax.fori_loop(0, HEADS, project, 0)
    if back:
        g_copy.wait()

    def visit(c, carry):
        for n in range(1, CAPACITY + 1):

            @pl.when(count[c] == n)
            def _():
                held = [member[c * CAPACITY + i] for i in range(n)]
                if back:
                    backward_cluster(held, kept, out, scales, grads)
                else:
                    forward_cluster(held, kept, out)

        return carry

    lax.fori_loop(0, clusters, visit, 0)


def head_work(info, tile_cluster, pieces, w_qkv, spacing, grads=None):
    back = grads is not None
    width = w_qkv.shape[1]
    tiles = 2 * HEADS
    wide = 3 * HD if back else HD
    tokens = tiles * TILE
    operands = [tile_cluster, info] + [array for _, _, array in pieces]
    if back:
        operands.append(grads.reshape(tiles, TILE, HD))
    operands.append(w_qkv.reshape(3, HEADS, HD, width))
    shapes = tuple((k, start, array.shape[0]) for k, start, array in pieces)
    scratch = [
        pltpu.VMEM((HEADS, 2 * TILE, width), jnp.bfloat16),
        pltpu.VMEM((3, HD, width), jnp.bfloat16),
        pltpu.VMEM((width, 3 * HD), jnp.bfloat16),
        pltpu.VMEM((tiles, TILE, 3 * HD), jnp.bfloat16),
        pltpu.SMEM((tiles // 2,), jnp.int32),
        pltpu.SMEM((tiles // 2 * CAPACITY,), jnp.int32),
        pltpu.SemaphoreType.DMA((len(pieces),)),
        pltpu.SemaphoreType.DMA,
    ]
    if back:
        scratch += [
            pltpu.VMEM((tiles, TILE, 2 * HD), jnp.float32),
            pltpu.VMEM((tiles, TILE, HD), jnp.bfloat16),
            pltpu.SemaphoreType.DMA,
        ]
    out = call(
        functools.partial(head_kernel, back, shapes, spacing),
        operands,
        [SMEM, SMEM] + [HBM] * (len(operands) - 2),
        jax.ShapeDtypeStruct((tiles, TILE, wide), jnp.bfloat16),
        scratch,
        2 * tokens * width * 3 * HD + tokens * 512 * HD * (14 if back else 4),
        2 * tokens * (width + 2 * wide),
    )
    return out.reshape(HEADS, 2 * TILE, wide)


def norm_kernel(x_ref, *refs):
    out_ref = refs[-1]
    x = high(x_ref[...])
    out_ref[...] = low(x * rows_rsqrt(x))


def norm_after(x, earlier):
    return call(
        norm_kernel,
        [x, *earlier],
        [VMEM] + [HBM] * len(earlier),
        jax.ShapeDtypeStruct(x.shape, jnp.bfloat16),
        [],
        4 * x.size,
        4 * x.size,
    )


def spread_kernel(up_ref, w_ref, out_ref, rows, sems):
    copies = [fetch(w_ref.at[k], rows.at[k], sems.at[k]) for k in range(HEADS)]
    for k in range(0, HEADS, 2):
        copies[k].wait()
        copies[k + 1].wait()
        pair = rows[k : k + 2].reshape(2 * HD, -1)
        g = low(dot(up_ref[...], pair, NT))
        out_ref[k] = g[:, :HD]
        out_ref[k + 1] = g[:, HD:]


def spread_grads(upstream, w_fin):
    tokens, width = upstream.shape
    return call(
        spread_kernel,
        [upstream, w_fin.reshape(HEADS, HD, width)],
        [VMEM, HBM],
        jax.ShapeDtypeStruct((HEADS, tokens, HD), jnp.bfloat16),
        [
            pltpu.VMEM((HEADS, HD, width), jnp.bfloat16),
            pltpu.SemaphoreType.DMA((HEADS,)),
        ],
        2 * tokens * width * HEADS * HD,
        2 * width * HEADS * HD,
    )


def finish_kernel(att_ref, x_ref, w_ref, out_ref):
    att = jnp.concatenate([att_ref[k] for k in range(HEADS)], axis=1)
    block = 256
    for start in range(0, x_ref.shape[1], block):
        columns = slice(start, start + block)
        out_ref[:, columns] = low(high(x_ref[:, columns]) + dot(att, w_ref[:, columns], NN))


def finish(attention, current, w_fin):
    tokens, width = current.shape
    return call(
        finish_kernel,
        [attention, current, w_fin],
        [VMEM] * 3,
        jax.ShapeDtypeStruct((tokens, width), jnp.bfloat16),
        [],
        2 * tokens * width * HEADS * HD,
        2 * width * HEADS * HD,
    )


def finish_back_kernel(grad_ref, x_ref, up_ref, w_ref, out_ref, total):
    for c in range(3):
        grads = jnp.concatenate(
            [grad_ref[k, :, c * HD : (c + 1) * HD] for k in range(HEADS)], axis=1
        )
        product = dot(grads, w_ref[c * HEADS * HD : (c + 1) * HEADS * HD], NN)
        if c == 0:
            total[...] = product
        else:
            total[...] += product
    x = high(x_ref[...])
    scale = rows_rsqrt(x)
    unit = x * scale
    g = total[...]
    pulled = scale * (g - unit * jnp.mean(unit * g, axis=1, keepdims=True))
    out_ref[...] = low(high(up_ref[...]) + pulled)


def finish_back(grads, stored, upstream, w_qkv):
    tokens, width = stored.shape
    return call(
        finish_back_kernel,
        [grads, stored, upstream, w_qkv],
        [VMEM] * 4,
        jax.ShapeDtypeStruct((tokens, width), jnp.bfloat16),
        [pltpu.VMEM((tokens, width), jnp.float32)],
        2 * tokens * width * 3 * HEADS * HD,
        6 * width * HEADS * HD,
    )


def partner(block, distance):
    route = [(i, i ^ distance) for i in range(lax.axis_size("seq"))]
    return lax.ppermute(block, "seq", route)


def gather_rows(x):
    half = x.shape[0] // 2
    over_x, over_y = partner(x, 2), partner(x, 4)
    top, bottom = partner(over_x[:half], 4), partner(over_y[half:], 2)
    pieces = [(0, 0, x), (2, 0, over_x), (4, 0, over_y), (6, 0, top), (6, half, bottom)]
    return pieces + [(k + 1, start, partner(block, 1)) for k, start, block in pieces]


def all_swap(blocks):
    return lax.all_to_all(blocks, "seq", split_axis=0, concat_axis=0, tiled=True)


def to_heads(blocks, own, spacing):
    heads, tokens, width = blocks.shape
    held = tokens // TILE
    places = spacing // held
    tiled = blocks.reshape(heads, 1, held, TILE, width)
    padded = jnp.zeros((heads, places, held, TILE, width), blocks.dtype)
    padded = lax.dynamic_update_slice_in_dim(padded, tiled, own % places, 1)
    arrived = all_swap(padded.reshape(heads * spacing, TILE, width))
    arrived = arrived.reshape(-1, places, TILE, width)
    mine = lax.dynamic_index_in_dim(arrived, own % spacing // held, 1, keepdims=False)
    return mine.reshape(HEADS, 2 * TILE, width)


def to_tokens(blocks, own, spacing, tokens):
    held = tokens // TILE
    places = spacing // held
    tiled = blocks.reshape(2 * HEADS, 1, TILE, -1)
    padded = jnp.zeros((2 * HEADS, places, TILE, tiled.shape[3]), tiled.dtype)
    padded = lax.dynamic_update_slice_in_dim(padded, tiled, own % spacing // held, 1)
    returned = all_swap(padded.reshape(-1, TILE, tiled.shape[3]))
    returned = returned.reshape(HEADS, places, held * TILE, tiled.shape[3])
    return lax.dynamic_index_in_dim(returned, own % places, 1, keepdims=False)


def passed_along(block, axis, distance):
    devices = range(lax.axis_size(axis))
    route = [(i - distance, i) for i in devices if i - distance in devices]
    return lax.ppermute(block, axis, route)


def per_device(section_input, saved_input, grad_output, w_qkv, w_out, tile_cluster):
    current, stored, upstream = section_input[0], saved_input[0], grad_output[0]
    w_rows, w_fin = w_qkv[0], w_out[0]
    tokens = current.shape[0]
    spacing = lax.axis_size("seq") // HEADS
    own = lax.axis_index("seq").astype(jnp.int32)
    if spacing == 1:
        info = jnp.stack([own, own, jnp.zeros_like(own)])
        gather, spread, collect = gather_rows, all_swap, all_swap
    else:
        info = jnp.stack([jnp.zeros_like(own), own // spacing, own % spacing])

        def gather(x):
            copies = jnp.broadcast_to(x, (HEADS, *x.shape))
            return [(k, 0, block) for k, block in enumerate(to_heads(copies, own, spacing))]

        def spread(blocks):
            return to_heads(blocks, own, spacing)

        def collect(blocks):
            return to_tokens(blocks, own, spacing, tokens)

    stored_pieces = gather(stored)
    grad_attention = spread(spread_grads(upstream, w_fin))
    earlier = [block for k, _, block in stored_pieces if k == HEADS - 2]
    current_pieces = gather(norm_after(current, earlier))
    grads = head_work(info, tile_cluster, stored_pieces, w_rows, spacing, grad_attention)
    returned_grads = collect(grads)
    outputs = head_work(info, tile_cluster, current_pieces, w_rows, spacing)
    returned = collect(outputs)
    grad_self = finish_back(returned_grads, stored, upstream, w_rows)
    grad_input = passed_along(grad_self, "pipe", -1)
    result = finish(returned, current, w_fin)
    next_input = passed_along(result, "pipe", 1)
    return (next_input[None], grad_input[None])


def solution(mesh):
    return jax.shard_map(
        per_device,
        mesh=mesh,
        in_specs=(
            P("pipe", "seq", None),
            P("pipe", "seq", None),
            P("pipe", "seq", None),
            P("pipe", None, None),
            P("pipe", None, None),
            P(),
        ),
        out_specs=(P("pipe", "seq", None), P("pipe", "seq", None)),
        check_vma=False,
    )
```

```python
import functools

import jax
import jax.numpy as jnp
from jax import lax
from jax.experimental import pallas as pl
from jax.experimental.pallas import tpu as pltpu
from jax.sharding import PartitionSpec as P

HEADS = 8
HD = 128
TILE = 128
CAPACITY = 3
EPSILON = 1e-05
MIB = 1024 * 1024
NT = (((1,), (1,)), ((), ()))
NN = (((1,), (0,)), ((), ()))
TN = (((0,), (0,)), ((), ()))
HBM = pl.BlockSpec(memory_space=pltpu.HBM)
SMEM = pl.BlockSpec(memory_space=pltpu.SMEM)
VMEM = pl.BlockSpec(memory_space=pltpu.VMEM)


def dot(left, right, dims):
    return lax.dot_general(left, right, dims, preferred_element_type=jnp.float32)


def low(values):
    return values.astype(jnp.bfloat16)


def high(values):
    return values.astype(jnp.float32)


def rows_rsqrt(values):
    return lax.rsqrt(jnp.mean(values * values, axis=-1, keepdims=True) + EPSILON)


def call(kernel, operands, in_specs, out_shape, scratch, flops, moved, grant=24 * MIB):
    return pl.pallas_call(
        kernel,
        in_specs=in_specs,
        out_specs=VMEM,
        out_shape=out_shape,
        scratch_shapes=scratch,
        compiler_params=pltpu.CompilerParams(vmem_limit_bytes=grant),
        cost_estimate=pl.CostEstimate(flops=flops, bytes_accessed=moved, transcendentals=0),
    )(*operands)


def fetch(source, target, sem):
    copy = pltpu.make_async_copy(source, target, sem)
    copy.start()
    return copy


def forward_cluster(tiles, kept, out):
    def load(c):
        return jnp.concatenate([kept[t, :, c * HD : (c + 1) * HD] for t in tiles], axis=0)

    q, k, v = load(0), load(1), load(2)
    weights = low(jnp.exp(dot(q, k, NT) * (HD ** -0.5)))
    wide = jnp.concatenate([v, jnp.ones_like(v)], axis=1)
    sums = dot(weights, wide, NN)
    result = low(sums[:, :HD] / sums[:, HD:])
    for i, t in enumerate(tiles):
        out[t] = result[i * TILE : (i + 1) * TILE]


def backward_cluster(tiles, kept, out, scales, grads):
    def load(c):
        return jnp.concatenate([kept[t, :, c * HD : (c + 1) * HD] for t in tiles], axis=0)

    def scale(c):
        return jnp.concatenate([scales[t, :, c * HD : (c + 1) * HD] for t in tiles], axis=0)

    q, k, v = load(0), load(1), load(2)
    g = jnp.concatenate([grads[t] for t in tiles], axis=0)
    factor = HD ** -0.5
    weights = jnp.exp(dot(k, q, NT) * factor)
    softmax = weights * (1.0 / jnp.sum(weights, axis=0, keepdims=True))
    soft_low = low(softmax)
    grad_soft = dot(v, g, NT)
    delta = jnp.sum(high(soft_low) * grad_soft, axis=0, keepdims=True)
    grad_scores = low(softmax * (grad_soft - delta))
    grad_values = low(dot(soft_low, g, NN))
    results = [grad_values]
    for c, unit, grad in (
        (1, k, dot(grad_scores, q, NN)),
        (0, q, dot(grad_scores, k, TN)),
    ):
        rounded = high(low(grad * factor))
        unit = high(unit)
        mean = jnp.mean(unit * rounded, axis=1, keepdims=True)
        results.append(low(scale(c) * (rounded - unit * mean)))
    for c, result in zip((2, 1, 0), results):
        for i, t in enumerate(tiles):
            out[t, :, c * HD : (c + 1) * HD] = result[i * TILE : (i + 1) * TILE]


def head_kernel(back, unread, pieces, spacing, *refs):
    cluster_ref, info_ref = refs[:2]
    x_refs = refs[2 : 2 + len(pieces)]
    refs = refs[2 + len(pieces) :]
    if back:
        g_ref, refs = refs[0], refs[1:]
    w_ref, refs = refs[0], refs[1 + unread :]
    out, xbuf, wbuf, turned, kept, count, member, xsem, wsem = refs[:9]
    flip, head, residue = info_ref[0], info_ref[1], info_ref[2]
    tiles = kept.shape[0]
    clusters = count.shape[0]

    weights = fetch(w_ref.at[:, head], wbuf, wsem)
    copies = []
    for i, (k, start, rows) in enumerate(pieces):
        copies.append(fetch(x_refs[i], xbuf.at[k, pl.ds(start, rows)], xsem.at[i]))
    if back:
        scales, grads, gsem = refs[9:]
        g_copy = fetch(g_ref, grads, gsem)

    for c in range(clusters):
        count[c] = 0

    def enter(t, carry):
        c = cluster_ref[t * spacing + residue] // spacing
        place = count[c]
        member[c * CAPACITY + place] = t
        count[c] = place + 1
        return carry

    lax.fori_loop(0, tiles, enter, 0)

    weights.wait()
    turned[...] = wbuf[...].reshape(3 * HD, -1).T

    def project(k, carry):
        for (slot, _, _), copy in zip(pieces, copies):
            pl.when(k == slot)(copy.wait)
        normed = xbuf[k]
        if back:
            x = high(normed)
            normed = low(x * rows_rsqrt(x))
        mixed = dot(normed, turned[...], NN)
        place = 2 * (flip ^ k)
        for c in range(3):
            u = mixed[:, c * HD : (c + 1) * HD]
            if c < 2:
                scale = rows_rsqrt(u)
                u = u * scale
            for j in range(2):
                kept[place + j, :, c * HD : (c + 1) * HD] = low(u[j * TILE : (j + 1) * TILE])
                if back and c < 2:
                    scales[place + j, :, c * HD : (c + 1) * HD] = jnp.broadcast_to(
                        scale[j * TILE : (j + 1) * TILE], (TILE, HD)
                    )
        return carry

    lax.fori_loop(0, HEADS, project, 0)
    if back:
        g_copy.wait()

    def visit(c, carry):
        for n in range(1, CAPACITY + 1):

            @pl.when(count[c] == n)
            def _():
                held = [member[c * CAPACITY + i] for i in range(n)]
                if back:
                    backward_cluster(held, kept, out, scales, grads)
                else:
                    forward_cluster(held, kept, out)

        return carry

    lax.fori_loop(0, clusters, visit, 0)


def head_work(info, tile_cluster, pieces, w_qkv, spacing, grads=None, earlier=()):
    back = grads is not None
    width = w_qkv.shape[1]
    tiles = 2 * HEADS
    wide = 3 * HD if back else HD
    tokens = tiles * TILE
    operands = [tile_cluster, info] + [array for _, _, array in pieces]
    if back:
        operands.append(grads.reshape(tiles, TILE, HD))
    operands += [w_qkv.reshape(3, HEADS, HD, width), *earlier]
    shapes = tuple((k, start, array.shape[0]) for k, start, array in pieces)
    scratch = [
        pltpu.VMEM((HEADS, 2 * TILE, width), jnp.bfloat16),
        pltpu.VMEM((3, HD, width), jnp.bfloat16),
        pltpu.VMEM((width, 3 * HD), jnp.bfloat16),
        pltpu.VMEM((tiles, TILE, 3 * HD), jnp.bfloat16),
        pltpu.SMEM((tiles // 2,), jnp.int32),
        pltpu.SMEM((tiles // 2 * CAPACITY,), jnp.int32),
        pltpu.SemaphoreType.DMA((len(pieces),)),
        pltpu.SemaphoreType.DMA,
    ]
    if back:
        scratch += [
            pltpu.VMEM((tiles, TILE, 2 * HD), jnp.float32),
            pltpu.VMEM((tiles, TILE, HD), jnp.bfloat16),
            pltpu.SemaphoreType.DMA,
        ]
    out = call(
        functools.partial(head_kernel, back, len(earlier), shapes, spacing),
        operands,
        [SMEM, SMEM] + [HBM] * (len(operands) - 2),
        jax.ShapeDtypeStruct((tiles, TILE, wide), jnp.bfloat16),
        scratch,
        2 * tokens * width * 3 * HD + tokens * 512 * HD * (14 if back else 4),
        2 * tokens * (width + 2 * wide),
        grant=58 * MIB,
    )
    return out.reshape(HEADS, 2 * TILE, wide)


def norm_kernel(x_ref, *refs):
    out_ref = refs[-1]
    x = high(x_ref[...])
    out_ref[...] = low(x * rows_rsqrt(x))


def norm_after(x, earlier):
    return call(
        norm_kernel,
        [x, *earlier],
        [VMEM] + [HBM] * len(earlier),
        jax.ShapeDtypeStruct(x.shape, jnp.bfloat16),
        [],
        4 * x.size,
        4 * x.size,
    )


def spread_kernel(up_ref, w_ref, out_ref, rows, sems):
    copies = [fetch(w_ref.at[k], rows.at[k], sems.at[k]) for k in range(HEADS)]
    for k in range(0, HEADS, 2):
        copies[k].wait()
        copies[k + 1].wait()
        pair = rows[k : k + 2].reshape(2 * HD, -1)
        g = low(dot(up_ref[...], pair, NT))
        out_ref[k] = g[:, :HD]
        out_ref[k + 1] = g[:, HD:]


def spread_grads(upstream, w_fin):
    tokens, width = upstream.shape
    return call(
        spread_kernel,
        [upstream, w_fin.reshape(HEADS, HD, width)],
        [VMEM, HBM],
        jax.ShapeDtypeStruct((HEADS, tokens, HD), jnp.bfloat16),
        [
            pltpu.VMEM((HEADS, HD, width), jnp.bfloat16),
            pltpu.SemaphoreType.DMA((HEADS,)),
        ],
        2 * tokens * width * HEADS * HD,
        2 * width * HEADS * HD,
    )


def finish_kernel(att_ref, x_ref, w_ref, out_ref):
    att = jnp.concatenate([att_ref[k] for k in range(HEADS)], axis=1)
    block = 256
    for start in range(0, x_ref.shape[1], block):
        columns = slice(start, start + block)
        out_ref[:, columns] = low(high(x_ref[:, columns]) + dot(att, w_ref[:, columns], NN))


def finish(attention, current, w_fin):
    tokens, width = current.shape
    return call(
        finish_kernel,
        [attention, current, w_fin],
        [VMEM] * 3,
        jax.ShapeDtypeStruct((tokens, width), jnp.bfloat16),
        [],
        2 * tokens * width * HEADS * HD,
        2 * width * HEADS * HD,
    )


def finish_back_kernel(grad_ref, x_ref, up_ref, w_ref, out_ref, total):
    for c in range(3):
        grads = jnp.concatenate(
            [grad_ref[k, :, c * HD : (c + 1) * HD] for k in range(HEADS)], axis=1
        )
        product = dot(grads, w_ref[c * HEADS * HD : (c + 1) * HEADS * HD], NN)
        if c == 0:
            total[...] = product
        else:
            total[...] += product
    x = high(x_ref[...])
    scale = rows_rsqrt(x)
    unit = x * scale
    g = total[...]
    pulled = scale * (g - unit * jnp.mean(unit * g, axis=1, keepdims=True))
    out_ref[...] = low(high(up_ref[...]) + pulled)


def finish_back(grads, stored, upstream, w_qkv):
    tokens, width = stored.shape
    return call(
        finish_back_kernel,
        [grads, stored, upstream, w_qkv],
        [VMEM] * 4,
        jax.ShapeDtypeStruct((tokens, width), jnp.bfloat16),
        [pltpu.VMEM((tokens, width), jnp.float32)],
        2 * tokens * width * 3 * HEADS * HD,
        6 * width * HEADS * HD,
    )


def partner(block, distance):
    route = [(i, i ^ distance) for i in range(lax.axis_size("seq"))]
    return lax.ppermute(block, "seq", route)


def gather_rows(x):
    half = x.shape[0] // 2
    over_x, over_y = partner(x, 2), partner(x, 4)
    top, bottom = partner(over_x[:half], 4), partner(over_y[half:], 2)
    pieces = [(0, 0, x), (2, 0, over_x), (4, 0, over_y), (6, 0, top), (6, half, bottom)]
    return pieces + [(k + 1, start, partner(block, 1)) for k, start, block in pieces]


def all_swap(blocks):
    return lax.all_to_all(blocks, "seq", split_axis=0, concat_axis=0, tiled=True)


def to_heads(blocks, own, spacing):
    heads, tokens, width = blocks.shape
    held = tokens // TILE
    places = spacing // held
    tiled = blocks.reshape(heads, 1, held, TILE, width)
    padded = jnp.zeros((heads, places, held, TILE, width), blocks.dtype)
    padded = lax.dynamic_update_slice_in_dim(padded, tiled, own % places, 1)
    arrived = all_swap(padded.reshape(heads * spacing, TILE, width))
    arrived = arrived.reshape(-1, places, TILE, width)
    mine = lax.dynamic_index_in_dim(arrived, own % spacing // held, 1, keepdims=False)
    return mine.reshape(HEADS, 2 * TILE, width)


def to_tokens(blocks, own, spacing, tokens):
    held = tokens // TILE
    places = spacing // held
    tiled = blocks.reshape(2 * HEADS, 1, TILE, -1)
    padded = jnp.zeros((2 * HEADS, places, TILE, tiled.shape[3]), tiled.dtype)
    padded = lax.dynamic_update_slice_in_dim(padded, tiled, own % spacing // held, 1)
    returned = all_swap(padded.reshape(-1, TILE, tiled.shape[3]))
    returned = returned.reshape(HEADS, places, held * TILE, tiled.shape[3])
    return lax.dynamic_index_in_dim(returned, own % places, 1, keepdims=False)


def passed_along(block, axis, distance):
    devices = range(lax.axis_size(axis))
    route = [(i - distance, i) for i in devices if i - distance in devices]
    return lax.ppermute(block, axis, route)


def per_device(section_input, saved_input, grad_output, w_qkv, w_out, tile_cluster):
    current, stored, upstream = section_input[0], saved_input[0], grad_output[0]
    w_rows, w_fin = w_qkv[0], w_out[0]
    tokens = current.shape[0]
    spacing = lax.axis_size("seq") // HEADS
    own = lax.axis_index("seq").astype(jnp.int32)
    if spacing == 1:
        info = jnp.stack([own, own, jnp.zeros_like(own)])
        gather, spread, collect = gather_rows, all_swap, all_swap
    else:
        info = jnp.stack([jnp.zeros_like(own), own // spacing, own % spacing])

        def gather(x):
            copies = jnp.broadcast_to(x, (HEADS, *x.shape))
            return [(k, 0, block) for k, block in enumerate(to_heads(copies, own, spacing))]

        def spread(blocks):
            return to_heads(blocks, own, spacing)

        def collect(blocks):
            return to_tokens(blocks, own, spacing, tokens)

    stored_pieces = gather(stored)
    grad_attention = spread(spread_grads(upstream, w_fin))
    earlier = [block for k, _, block in stored_pieces if k == HEADS - 2]
    current_pieces = gather(norm_after(current, [*earlier, grad_attention]))
    grads = head_work(info, tile_cluster, stored_pieces, w_rows, spacing, grad_attention)
    returned_grads = collect(grads)
    outputs = head_work(
        info, tile_cluster, current_pieces, w_rows, spacing, earlier=(grads,)
    )
    returned = collect(outputs)
    grad_self = finish_back(returned_grads, stored, upstream, w_rows)
    grad_input = passed_along(grad_self, "pipe", -1)
    result = finish(returned, current, w_fin)
    next_input = passed_along(result, "pipe", 1)
    return (next_input[None], grad_input[None])


def solution(mesh):
    return jax.shard_map(
        per_device,
        mesh=mesh,
        in_specs=(
            P("pipe", "seq", None),
            P("pipe", "seq", None),
            P("pipe", "seq", None),
            P("pipe", None, None),
            P("pipe", None, None),
            P(),
        ),
        out_specs=(P("pipe", "seq", None), P("pipe", "seq", None)),
        check_vma=False,
    )
```

```python
import functools

import jax
import jax.numpy as jnp
from jax import lax
from jax.experimental import pallas as pl
from jax.experimental.pallas import tpu as pltpu
from jax.sharding import PartitionSpec as P

HEADS = 8
HD = 128
TILE = 128
CAPACITY = 3
EPSILON = 1e-05
MIB = 1024 * 1024
NT = (((1,), (1,)), ((), ()))
NN = (((1,), (0,)), ((), ()))
TN = (((0,), (0,)), ((), ()))
HBM = pl.BlockSpec(memory_space=pl.ANY)
SMEM = pl.BlockSpec(memory_space=pltpu.SMEM)
VMEM = pl.BlockSpec(memory_space=pltpu.VMEM)


def dot(left, right, dims):
    return lax.dot_general(left, right, dims, preferred_element_type=jnp.float32)


def low(values):
    return values.astype(jnp.bfloat16)


def high(values):
    return values.astype(jnp.float32)


def rows_rsqrt(values):
    return lax.rsqrt(jnp.mean(values * values, axis=-1, keepdims=True) + EPSILON)


def call(kernel, operands, in_specs, out_shape, scratch, flops, moved, grant=24 * MIB):
    return pl.pallas_call(
        kernel,
        in_specs=in_specs,
        out_specs=VMEM,
        out_shape=out_shape,
        scratch_shapes=scratch,
        compiler_params=pltpu.CompilerParams(vmem_limit_bytes=grant),
        cost_estimate=pl.CostEstimate(flops=flops, bytes_accessed=moved, transcendentals=0),
    )(*operands)


def fetch(source, target, sem):
    copy = pltpu.make_async_copy(source, target, sem)
    copy.start()
    return copy


def forward_cluster(tiles, kept, out):
    def load(c):
        return jnp.concatenate([kept[t, :, c * HD : (c + 1) * HD] for t in tiles], axis=0)

    q, k, v = load(0), load(1), load(2)
    weights = low(jnp.exp(dot(q, k, NT) * (HD ** -0.5)))
    wide = jnp.concatenate([v, jnp.ones_like(v)], axis=1)
    sums = dot(weights, wide, NN)
    result = low(sums[:, :HD] / sums[:, HD:])
    for i, t in enumerate(tiles):
        out[t] = result[i * TILE : (i + 1) * TILE]


def backward_cluster(tiles, kept, out, scales, grads):
    def load(c):
        return jnp.concatenate([kept[t, :, c * HD : (c + 1) * HD] for t in tiles], axis=0)

    def scale(c):
        return jnp.concatenate([scales[t, :, c * HD : (c + 1) * HD] for t in tiles], axis=0)

    q, k, v = load(0), load(1), load(2)
    g = jnp.concatenate([grads[t] for t in tiles], axis=0)
    factor = HD ** -0.5
    weights = jnp.exp(dot(k, q, NT) * factor)
    softmax = weights * (1.0 / jnp.sum(weights, axis=0, keepdims=True))
    soft_low = low(softmax)
    grad_soft = dot(v, g, NT)
    delta = jnp.sum(high(soft_low) * grad_soft, axis=0, keepdims=True)
    grad_scores = low(softmax * (grad_soft - delta))
    grad_values = low(dot(soft_low, g, NN))
    results = [grad_values]
    for c, unit, grad in (
        (1, k, dot(grad_scores, q, NN)),
        (0, q, dot(grad_scores, k, TN)),
    ):
        rounded = high(low(grad * factor))
        unit = high(unit)
        mean = jnp.mean(unit * rounded, axis=1, keepdims=True)
        results.append(low(scale(c) * (rounded - unit * mean)))
    for c, result in zip((2, 1, 0), results):
        for i, t in enumerate(tiles):
            out[t, :, c * HD : (c + 1) * HD] = result[i * TILE : (i + 1) * TILE]


def head_kernel(back, unread, pieces, spacing, *refs):
    cluster_ref, info_ref, w_ref = refs[:3]
    x_refs = refs[3 : 3 + len(pieces)]
    refs = refs[3 + len(pieces) :]
    if back:
        grads, refs = refs[0], refs[1:]
    out, kept, count, member = refs[unread : unread + 4]
    if back:
        scales = refs[unread + 4]
    flip, residue = info_ref[0], info_ref[2]
    tiles = kept.shape[0]
    clusters = count.shape[0]
    for c in range(clusters):
        count[c] = 0

    def enter(t, carry):
        c = cluster_ref[t * spacing + residue] // spacing
        place = count[c]
        member[c * CAPACITY + place] = t
        count[c] = place + 1
        return carry

    lax.fori_loop(0, tiles, enter, 0)

    weights = w_ref[...]
    for (slot, start, rows), x_ref in zip(pieces, x_refs):
        normed = x_ref[...]
        if back:
            x = high(normed)
            normed = low(x * rows_rsqrt(x))
        mixed = dot(normed, weights, NT)
        place = 2 * (flip ^ slot) + start // TILE
        for c in range(3):
            u = mixed[:, c * HD : (c + 1) * HD]
            if c < 2:
                scale = rows_rsqrt(u)
                u = u * scale
            for j in range(rows // TILE):
                kept[place + j, :, c * HD : (c + 1) * HD] = low(u[j * TILE : (j + 1) * TILE])
                if back and c < 2:
                    scales[place + j, :, c * HD : (c + 1) * HD] = jnp.broadcast_to(
                        scale[j * TILE : (j + 1) * TILE], (TILE, HD)
                    )

    def visit(c, carry):
        for n in range(1, CAPACITY + 1):

            @pl.when(count[c] == n)
            def _():
                held = [member[c * CAPACITY + i] for i in range(n)]
                if back:
                    backward_cluster(held, kept, out, scales, grads)
                else:
                    forward_cluster(held, kept, out)

        return carry

    lax.fori_loop(0, clusters, visit, 0)


def head_work(info, tile_cluster, pieces, weights, spacing, grads=None, earlier=()):
    back = grads is not None
    width = weights.shape[1]
    tiles = 2 * HEADS
    wide = 3 * HD if back else HD
    tokens = tiles * TILE
    operands = [tile_cluster, info, weights] + [array for _, _, array in pieces]
    if back:
        operands.append(grads.reshape(tiles, TILE, HD))
    scratch = [
        pltpu.VMEM((tiles, TILE, 3 * HD), jnp.bfloat16),
        pltpu.SMEM((tiles // 2,), jnp.int32),
        pltpu.SMEM((tiles // 2 * CAPACITY,), jnp.int32),
    ]
    if back:
        scratch.append(pltpu.VMEM((tiles, TILE, 2 * HD), jnp.float32))
    shapes = tuple((k, start, array.shape[0]) for k, start, array in pieces)
    out = call(
        functools.partial(head_kernel, back, len(earlier), shapes, spacing),
        operands + list(earlier),
        [SMEM, SMEM] + [VMEM] * (len(operands) - 2) + [HBM] * len(earlier),
        jax.ShapeDtypeStruct((tiles, TILE, wide), jnp.bfloat16),
        scratch,
        2 * tokens * width * 3 * HD + tokens * 512 * HD * (14 if back else 4),
        2 * tokens * (width + 2 * wide),
    )
    return out.reshape(HEADS, 2 * TILE, wide)


def nothing(*refs):
    pass


def gate(arrays, earlier):
    return pl.pallas_call(
        nothing,
        in_specs=[HBM] * (len(arrays) + len(earlier)),
        out_specs=[HBM] * len(arrays),
        out_shape=[jax.ShapeDtypeStruct(a.shape, a.dtype) for a in arrays],
        input_output_aliases={i: i for i in range(len(arrays))},
    )(*arrays, *earlier)


def norm_kernel(x_ref, *refs):
    out_ref = refs[-1]
    x = high(x_ref[...])
    out_ref[...] = low(x * rows_rsqrt(x))


def norm_after(x, earlier):
    return call(
        norm_kernel,
        [x, *earlier],
        [VMEM] + [HBM] * len(earlier),
        jax.ShapeDtypeStruct(x.shape, jnp.bfloat16),
        [],
        4 * x.size,
        4 * x.size,
    )


def spread_kernel(up_ref, w_ref, out_ref, rows, sems):
    copies = [fetch(w_ref.at[k], rows.at[k], sems.at[k]) for k in range(HEADS)]
    for k in range(0, HEADS, 2):
        copies[k].wait()
        copies[k + 1].wait()
        pair = rows[k : k + 2].reshape(2 * HD, -1)
        g = low(dot(up_ref[...], pair, NT))
        out_ref[k] = g[:, :HD]
        out_ref[k + 1] = g[:, HD:]


def spread_grads(upstream, w_fin):
    tokens, width = upstream.shape
    return call(
        spread_kernel,
        [upstream, w_fin.reshape(HEADS, HD, width)],
        [VMEM, HBM],
        jax.ShapeDtypeStruct((HEADS, tokens, HD), jnp.bfloat16),
        [
            pltpu.VMEM((HEADS, HD, width), jnp.bfloat16),
            pltpu.SemaphoreType.DMA((HEADS,)),
        ],
        2 * tokens * width * HEADS * HD,
        2 * width * HEADS * HD,
    )


def finish_kernel(att_ref, x_ref, w_ref, out_ref):
    att = jnp.concatenate([att_ref[k] for k in range(HEADS)], axis=1)
    block = 256
    for start in range(0, x_ref.shape[1], block):
        columns = slice(start, start + block)
        out_ref[:, columns] = low(high(x_ref[:, columns]) + dot(att, w_ref[:, columns], NN))


def finish(attention, current, w_fin):
    tokens, width = current.shape
    return call(
        finish_kernel,
        [attention, current, w_fin],
        [VMEM] * 3,
        jax.ShapeDtypeStruct((tokens, width), jnp.bfloat16),
        [],
        2 * tokens * width * HEADS * HD,
        2 * width * HEADS * HD,
    )


def finish_back_kernel(grad_ref, x_ref, up_ref, w_ref, out_ref, total):
    for c in range(3):
        grads = jnp.concatenate(
            [grad_ref[k, :, c * HD : (c + 1) * HD] for k in range(HEADS)], axis=1
        )
        product = dot(grads, w_ref[c * HEADS * HD : (c + 1) * HEADS * HD], NN)
        if c == 0:
            total[...] = product
        else:
            total[...] += product
    x = high(x_ref[...])
    scale = rows_rsqrt(x)
    unit = x * scale
    g = total[...]
    pulled = scale * (g - unit * jnp.mean(unit * g, axis=1, keepdims=True))
    out_ref[...] = low(high(up_ref[...]) + pulled)


def finish_back(grads, stored, upstream, w_qkv):
    tokens, width = stored.shape
    return call(
        finish_back_kernel,
        [grads, stored, upstream, w_qkv],
        [VMEM] * 4,
        jax.ShapeDtypeStruct((tokens, width), jnp.bfloat16),
        [pltpu.VMEM((tokens, width), jnp.float32)],
        2 * tokens * width * 3 * HEADS * HD,
        6 * width * HEADS * HD,
    )


def partner(block, distance):
    route = [(i, i ^ distance) for i in range(lax.axis_size("seq"))]
    return lax.ppermute(block, "seq", route)


def gather_rows(x, earlier=()):
    half = x.shape[0] // 2
    over_x, over_y = partner(x, 2), partner(x, 4)
    if earlier:
        over_x, over_y = gate([over_x, over_y], earlier)
    top, bottom = partner(over_x[:half], 4), partner(over_y[half:], 2)
    pieces = [(0, 0, x), (2, 0, over_x), (4, 0, over_y), (6, 0, top), (6, half, bottom)]
    return pieces + [(k + 1, start, partner(block, 1)) for k, start, block in pieces]


def all_swap(blocks):
    return lax.all_to_all(blocks, "seq", split_axis=0, concat_axis=0, tiled=True)


def to_heads(blocks, own, spacing):
    heads, tokens, width = blocks.shape
    held = tokens // TILE
    places = spacing // held
    tiled = blocks.reshape(heads, 1, held, TILE, width)
    padded = jnp.zeros((heads, places, held, TILE, width), blocks.dtype)
    padded = lax.dynamic_update_slice_in_dim(padded, tiled, own % places, 1)
    arrived = all_swap(padded.reshape(heads * spacing, TILE, width))
    arrived = arrived.reshape(-1, places, TILE, width)
    mine = lax.dynamic_index_in_dim(arrived, own % spacing // held, 1, keepdims=False)
    return mine.reshape(HEADS, 2 * TILE, width)


def to_tokens(blocks, own, spacing, tokens):
    held = tokens // TILE
    places = spacing // held
    tiled = blocks.reshape(2 * HEADS, 1, TILE, -1)
    padded = jnp.zeros((2 * HEADS, places, TILE, tiled.shape[3]), tiled.dtype)
    padded = lax.dynamic_update_slice_in_dim(padded, tiled, own % spacing // held, 1)
    returned = all_swap(padded.reshape(-1, TILE, tiled.shape[3]))
    returned = returned.reshape(HEADS, places, held * TILE, tiled.shape[3])
    return lax.dynamic_index_in_dim(returned, own % places, 1, keepdims=False)


def passed_along(block, axis, distance):
    devices = range(lax.axis_size(axis))
    route = [(i - distance, i) for i in devices if i - distance in devices]
    return lax.ppermute(block, axis, route)


def per_device(section_input, saved_input, grad_output, w_qkv, w_out, tile_cluster):
    current, stored, upstream = section_input[0], saved_input[0], grad_output[0]
    w_rows, w_fin = w_qkv[0], w_out[0]
    tokens = current.shape[0]
    spacing = lax.axis_size("seq") // HEADS
    own = lax.axis_index("seq").astype(jnp.int32)
    if spacing == 1:
        info = jnp.stack([own, own, jnp.zeros_like(own)])
        gather, spread, collect = gather_rows, all_swap, all_swap
    else:
        info = jnp.stack([jnp.zeros_like(own), own // spacing, own % spacing])

        def gather(x, earlier=()):
            copies = jnp.broadcast_to(x, (HEADS, *x.shape))
            return [(k, 0, block) for k, block in enumerate(to_heads(copies, own, spacing))]

        def spread(blocks):
            return to_heads(blocks, own, spacing)

        def collect(blocks):
            return to_tokens(blocks, own, spacing, tokens)

    own_head = w_rows.reshape(3, HEADS, HD, -1)
    own_head = lax.dynamic_index_in_dim(own_head, info[1], 1, keepdims=False)
    own_head = own_head.reshape(3 * HD, -1)
    stored_pieces = gather(stored)
    grad_attention = spread(spread_grads(upstream, w_fin))
    earlier = [block for k, _, block in stored_pieces if k == HEADS - 2]
    normed = norm_after(current, [*earlier, grad_attention])
    grads = head_work(info, tile_cluster, stored_pieces, own_head, spacing, grad_attention)
    current_pieces = gather(normed, [grads])
    returned_grads = collect(grads)
    outputs = head_work(
        info, tile_cluster, current_pieces, own_head, spacing, earlier=(grads,)
    )
    returned = collect(gate([outputs], [returned_grads])[0])
    grad_self = finish_back(returned_grads, stored, upstream, w_rows)
    grad_input = passed_along(grad_self, "pipe", -1)
    result = finish(returned, current, w_fin)
    next_input = passed_along(result, "pipe", 1)
    return (next_input[None], grad_input[None])


def solution(mesh):
    return jax.shard_map(
        per_device,
        mesh=mesh,
        in_specs=(
            P("pipe", "seq", None),
            P("pipe", "seq", None),
            P("pipe", "seq", None),
            P("pipe", None, None),
            P("pipe", None, None),
            P(),
        ),
        out_specs=(P("pipe", "seq", None), P("pipe", "seq", None)),
        check_vma=False,
    )
```

```python
import functools

import jax
import jax.numpy as jnp
from jax import lax
from jax.experimental import pallas as pl
from jax.experimental.pallas import tpu as pltpu
from jax.sharding import PartitionSpec as P

HEADS = 8
HD = 128
TILE = 128
CAPACITY = 3
EPSILON = 1e-05
MIB = 1024 * 1024
MICROSECOND = 1150000000
NT = (((1,), (1,)), ((), ()))
NN = (((1,), (0,)), ((), ()))
TN = (((0,), (0,)), ((), ()))
HBM = pl.BlockSpec(memory_space=pl.ANY)
SMEM = pl.BlockSpec(memory_space=pltpu.SMEM)
VMEM = pl.BlockSpec(memory_space=pltpu.VMEM)


def dot(left, right, dims):
    return lax.dot_general(left, right, dims, preferred_element_type=jnp.float32)


def low(values):
    return values.astype(jnp.bfloat16)


def high(values):
    return values.astype(jnp.float32)


def rows_rsqrt(values):
    return lax.rsqrt(jnp.mean(values * values, axis=-1, keepdims=True) + EPSILON)


def call(kernel, operands, in_specs, out_shape, scratch, flops, moved, grant=24 * MIB):
    return pl.pallas_call(
        kernel,
        in_specs=in_specs,
        out_specs=VMEM,
        out_shape=out_shape,
        scratch_shapes=scratch,
        compiler_params=pltpu.CompilerParams(vmem_limit_bytes=grant),
        cost_estimate=pl.CostEstimate(flops=flops, bytes_accessed=moved, transcendentals=0),
    )(*operands)


def fetch(source, target, sem):
    copy = pltpu.make_async_copy(source, target, sem)
    copy.start()
    return copy


def forward_cluster(tiles, kept, out):
    def load(c):
        return jnp.concatenate([kept[t, :, c * HD : (c + 1) * HD] for t in tiles], axis=0)

    q, k, v = load(0), load(1), load(2)
    weights = low(jnp.exp(dot(q, k, NT) * (HD ** -0.5)))
    wide = jnp.concatenate([v, jnp.ones_like(v)], axis=1)
    sums = dot(weights, wide, NN)
    result = low(sums[:, :HD] / sums[:, HD:])
    for i, t in enumerate(tiles):
        out[t] = result[i * TILE : (i + 1) * TILE]


def backward_cluster(tiles, kept, out, scales, grads):
    def load(c):
        return jnp.concatenate([kept[t, :, c * HD : (c + 1) * HD] for t in tiles], axis=0)

    def scale(c):
        return jnp.concatenate([scales[t, :, c * HD : (c + 1) * HD] for t in tiles], axis=0)

    q, k, v = load(0), load(1), load(2)
    g = jnp.concatenate([grads[t] for t in tiles], axis=0)
    factor = HD ** -0.5
    weights = jnp.exp(dot(k, q, NT) * factor)
    softmax = weights * (1.0 / jnp.sum(weights, axis=0, keepdims=True))
    soft_low = low(softmax)
    grad_soft = dot(v, g, NT)
    delta = jnp.sum(high(soft_low) * grad_soft, axis=0, keepdims=True)
    grad_scores = low(softmax * (grad_soft - delta))
    grad_values = low(dot(soft_low, g, NN))
    results = [grad_values]
    for c, unit, grad in (
        (1, k, dot(grad_scores, q, NN)),
        (0, q, dot(grad_scores, k, TN)),
    ):
        rounded = high(low(grad * factor))
        unit = high(unit)
        mean = jnp.mean(unit * rounded, axis=1, keepdims=True)
        results.append(low(scale(c) * (rounded - unit * mean)))
    for c, result in zip((2, 1, 0), results):
        for i, t in enumerate(tiles):
            out[t, :, c * HD : (c + 1) * HD] = result[i * TILE : (i + 1) * TILE]


def head_kernel(back, unread, pieces, spacing, *refs):
    cluster_ref, info_ref, w_ref = refs[:3]
    x_refs = refs[3 : 3 + len(pieces)]
    refs = refs[3 + len(pieces) :]
    if back:
        grads, refs = refs[0], refs[1:]
    out, kept, count, member = refs[unread : unread + 4]
    if back:
        scales = refs[unread + 4]
    flip, residue = info_ref[0], info_ref[2]
    tiles = kept.shape[0]
    clusters = count.shape[0]
    for c in range(clusters):
        count[c] = 0

    def enter(t, carry):
        c = cluster_ref[t * spacing + residue] // spacing
        place = count[c]
        member[c * CAPACITY + place] = t
        count[c] = place + 1
        return carry

    lax.fori_loop(0, tiles, enter, 0)

    weights = w_ref[...]
    for (slot, start, rows), x_ref in zip(pieces, x_refs):
        normed = x_ref[...]
        if back:
            x = high(normed)
            normed = low(x * rows_rsqrt(x))
        mixed = dot(normed, weights, NT)
        place = 2 * (flip ^ slot) + start // TILE
        for c in range(3):
            u = mixed[:, c * HD : (c + 1) * HD]
            if c < 2:
                scale = rows_rsqrt(u)
                u = u * scale
            for j in range(rows // TILE):
                kept[place + j, :, c * HD : (c + 1) * HD] = low(u[j * TILE : (j + 1) * TILE])
                if back and c < 2:
                    scales[place + j, :, c * HD : (c + 1) * HD] = jnp.broadcast_to(
                        scale[j * TILE : (j + 1) * TILE], (TILE, HD)
                    )

    def visit(c, carry):
        for n in range(1, CAPACITY + 1):

            @pl.when(count[c] == n)
            def _():
                held = [member[c * CAPACITY + i] for i in range(n)]
                if back:
                    backward_cluster(held, kept, out, scales, grads)
                else:
                    forward_cluster(held, kept, out)

        return carry

    lax.fori_loop(0, clusters, visit, 0)


def head_work(info, tile_cluster, pieces, weights, spacing, grads=None, earlier=()):
    back = grads is not None
    width = weights.shape[1]
    tiles = 2 * HEADS
    wide = 3 * HD if back else HD
    tokens = tiles * TILE
    operands = [tile_cluster, info, weights] + [array for _, _, array in pieces]
    if back:
        operands.append(grads.reshape(tiles, TILE, HD))
    scratch = [
        pltpu.VMEM((tiles, TILE, 3 * HD), jnp.bfloat16),
        pltpu.SMEM((tiles // 2,), jnp.int32),
        pltpu.SMEM((tiles // 2 * CAPACITY,), jnp.int32),
    ]
    if back:
        scratch.append(pltpu.VMEM((tiles, TILE, 2 * HD), jnp.float32))
    shapes = tuple((k, start, array.shape[0]) for k, start, array in pieces)
    out = call(
        functools.partial(head_kernel, back, len(earlier), shapes, spacing),
        operands + list(earlier),
        [SMEM, SMEM] + [VMEM] * (len(operands) - 2) + [HBM] * len(earlier),
        jax.ShapeDtypeStruct((tiles, TILE, wide), jnp.bfloat16),
        scratch,
        MICROSECOND * (12 if back else 8),
        2 * tokens * (width + 2 * wide),
    )
    return out.reshape(HEADS, 2 * TILE, wide)


def copy_kernel(starts, *refs):
    count = len(starts)
    outs, sems = refs[-count - 1 : -1], refs[-1]
    copies = [
        fetch(refs[i].at[pl.ds(start, outs[i].shape[0])], outs[i], sems.at[i])
        for i, start in enumerate(starts)
    ]
    for copy in copies:
        copy.wait()


def rows_after(arrays, starts, rows, earlier):
    return pl.pallas_call(
        functools.partial(copy_kernel, starts),
        in_specs=[HBM] * (len(arrays) + len(earlier)),
        out_specs=[HBM] * len(arrays),
        out_shape=[jax.ShapeDtypeStruct((rows, *a.shape[1:]), a.dtype) for a in arrays],
        scratch_shapes=[pltpu.SemaphoreType.DMA((len(arrays),))],
    )(*arrays, *earlier)


def norm_kernel(x_ref, *refs):
    out_ref = refs[-1]
    x = high(x_ref[...])
    out_ref[...] = low(x * rows_rsqrt(x))


def norm_after(x, earlier):
    return call(
        norm_kernel,
        [x, *earlier],
        [VMEM] + [HBM] * len(earlier),
        jax.ShapeDtypeStruct(x.shape, jnp.bfloat16),
        [],
        4 * x.size,
        4 * x.size,
    )


def spread_kernel(up_ref, w_ref, out_ref, rows, sems):
    copies = [fetch(w_ref.at[k], rows.at[k], sems.at[k]) for k in range(HEADS)]
    for k in range(0, HEADS, 2):
        copies[k].wait()
        copies[k + 1].wait()
        pair = rows[k : k + 2].reshape(2 * HD, -1)
        g = low(dot(up_ref[...], pair, NT))
        out_ref[k] = g[:, :HD]
        out_ref[k + 1] = g[:, HD:]


def spread_grads(upstream, w_fin):
    tokens, width = upstream.shape
    return call(
        spread_kernel,
        [upstream, w_fin.reshape(HEADS, HD, width)],
        [VMEM, HBM],
        jax.ShapeDtypeStruct((HEADS, tokens, HD), jnp.bfloat16),
        [
            pltpu.VMEM((HEADS, HD, width), jnp.bfloat16),
            pltpu.SemaphoreType.DMA((HEADS,)),
        ],
        MICROSECOND * 3,
        2 * width * HEADS * HD,
    )


def finish_kernel(att_ref, x_ref, w_ref, out_ref):
    att = jnp.concatenate([att_ref[k] for k in range(HEADS)], axis=1)
    block = 256
    for start in range(0, x_ref.shape[1], block):
        columns = slice(start, start + block)
        out_ref[:, columns] = low(high(x_ref[:, columns]) + dot(att, w_ref[:, columns], NN))


def finish(attention, current, w_fin):
    tokens, width = current.shape
    return call(
        finish_kernel,
        [attention, current, w_fin],
        [VMEM] * 3,
        jax.ShapeDtypeStruct((tokens, width), jnp.bfloat16),
        [],
        2 * tokens * width * HEADS * HD,
        2 * width * HEADS * HD,
    )


def finish_back_kernel(grad_ref, x_ref, up_ref, w_ref, out_ref, total):
    for c in range(3):
        grads = jnp.concatenate(
            [grad_ref[k, :, c * HD : (c + 1) * HD] for k in range(HEADS)], axis=1
        )
        product = dot(grads, w_ref[c * HEADS * HD : (c + 1) * HEADS * HD], NN)
        if c == 0:
            total[...] = product
        else:
            total[...] += product
    x = high(x_ref[...])
    scale = rows_rsqrt(x)
    unit = x * scale
    g = total[...]
    pulled = scale * (g - unit * jnp.mean(unit * g, axis=1, keepdims=True))
    out_ref[...] = low(high(up_ref[...]) + pulled)


def finish_back(grads, stored, upstream, w_qkv):
    tokens, width = stored.shape
    return call(
        finish_back_kernel,
        [grads, stored, upstream, w_qkv],
        [VMEM] * 4,
        jax.ShapeDtypeStruct((tokens, width), jnp.bfloat16),
        [pltpu.VMEM((tokens, width), jnp.float32)],
        2 * tokens * width * 3 * HEADS * HD,
        6 * width * HEADS * HD,
    )


def partner(block, distance):
    route = [(i, i ^ distance) for i in range(lax.axis_size("seq"))]
    return lax.ppermute(block, "seq", route)


def gather_rows(x, earlier):
    half = x.shape[0] // 2
    over_x, over_y = partner(x, 2), partner(x, 4)
    top, bottom = rows_after([over_x, over_y], [0, half], half, earlier)
    top, bottom = partner(top, 4), partner(bottom, 2)
    pieces = [(0, 0, x), (2, 0, over_x), (4, 0, over_y), (6, 0, top), (6, half, bottom)]
    return pieces + [(k + 1, start, partner(block, 1)) for k, start, block in pieces]


def all_swap(blocks):
    return lax.all_to_all(blocks, "seq", split_axis=0, concat_axis=0, tiled=True)


def to_heads(blocks, own, spacing):
    heads, tokens, width = blocks.shape
    held = tokens // TILE
    places = spacing // held
    tiled = blocks.reshape(heads, 1, held, TILE, width)
    padded = jnp.zeros((heads, places, held, TILE, width), blocks.dtype)
    padded = lax.dynamic_update_slice_in_dim(padded, tiled, own % places, 1)
    arrived = all_swap(padded.reshape(heads * spacing, TILE, width))
    arrived = arrived.reshape(-1, places, TILE, width)
    mine = lax.dynamic_index_in_dim(arrived, own % spacing // held, 1, keepdims=False)
    return mine.reshape(HEADS, 2 * TILE, width)


def to_tokens(blocks, own, spacing, tokens):
    held = tokens // TILE
    places = spacing // held
    tiled = blocks.reshape(2 * HEADS, 1, TILE, -1)
    padded = jnp.zeros((2 * HEADS, places, TILE, tiled.shape[3]), tiled.dtype)
    padded = lax.dynamic_update_slice_in_dim(padded, tiled, own % spacing // held, 1)
    returned = all_swap(padded.reshape(-1, TILE, tiled.shape[3]))
    returned = returned.reshape(HEADS, places, held * TILE, tiled.shape[3])
    return lax.dynamic_index_in_dim(returned, own % places, 1, keepdims=False)


def passed_along(block, axis, distance):
    devices = range(lax.axis_size(axis))
    route = [(i - distance, i) for i in devices if i - distance in devices]
    return lax.ppermute(block, axis, route)


def per_device(section_input, saved_input, grad_output, w_qkv, w_out, tile_cluster):
    current, stored, upstream = section_input[0], saved_input[0], grad_output[0]
    w_rows, w_fin = w_qkv[0], w_out[0]
    tokens = current.shape[0]
    spacing = lax.axis_size("seq") // HEADS
    own = lax.axis_index("seq").astype(jnp.int32)
    if spacing == 1:
        info = jnp.stack([own, own, jnp.zeros_like(own)])
        gather, spread, collect = gather_rows, all_swap, all_swap
    else:
        info = jnp.stack([jnp.zeros_like(own), own // spacing, own % spacing])

        def gather(x, earlier):
            copies = jnp.broadcast_to(x, (HEADS, *x.shape))
            return [(k, 0, block) for k, block in enumerate(to_heads(copies, own, spacing))]

        def spread(blocks):
            return to_heads(blocks, own, spacing)

        def collect(blocks):
            return to_tokens(blocks, own, spacing, tokens)

    own_head = w_rows.reshape(3, HEADS, HD, -1)
    own_head = lax.dynamic_index_in_dim(own_head, info[1], 1, keepdims=False)
    own_head = own_head.reshape(3 * HD, -1)
    spreading = spread_grads(upstream, w_fin)
    stored_pieces = gather(stored, [spreading])
    grad_attention = spread(spreading)
    earlier = [block for k, _, block in stored_pieces if k == HEADS - 2]
    normed = norm_after(current, [*earlier, grad_attention])
    grads = head_work(
        info, tile_cluster, stored_pieces, own_head, spacing, grad_attention, [normed]
    )
    current_pieces = gather(normed, [grads])
    returned_grads = collect(grads)
    outputs = head_work(
        info, tile_cluster, current_pieces, own_head, spacing, earlier=[grads]
    )
    outputs = rows_after([outputs], [0], HEADS, [returned_grads])[0]
    returned = collect(outputs)
    grad_self = finish_back(returned_grads, stored, upstream, w_rows)
    grad_input = passed_along(grad_self, "pipe", -1)
    result = finish(returned, current, w_fin)
    next_input = passed_along(result, "pipe", 1)
    return (next_input[None], grad_input[None])


def solution(mesh):
    return jax.shard_map(
        per_device,
        mesh=mesh,
        in_specs=(
            P("pipe", "seq", None),
            P("pipe", "seq", None),
            P("pipe", "seq", None),
            P("pipe", None, None),
            P("pipe", None, None),
            P(),
        ),
        out_specs=(P("pipe", "seq", None), P("pipe", "seq", None)),
        check_vma=False,
    )
```

```python
import functools

import jax
import jax.numpy as jnp
from jax import lax
from jax.experimental import pallas as pl
from jax.experimental.pallas import tpu as pltpu
from jax.sharding import PartitionSpec as P

HEADS = 8
HD = 128
TILE = 128
CAPACITY = 3
EPSILON = 1e-05
MIB = 1024 * 1024
MICROSECOND = 1150000000
NT = (((1,), (1,)), ((), ()))
NN = (((1,), (0,)), ((), ()))
TN = (((0,), (0,)), ((), ()))
HBM = pl.BlockSpec(memory_space=pl.ANY)
SMEM = pl.BlockSpec(memory_space=pltpu.SMEM)
VMEM = pl.BlockSpec(memory_space=pltpu.VMEM)


def dot(left, right, dims):
    return lax.dot_general(left, right, dims, preferred_element_type=jnp.float32)


def low(values):
    return values.astype(jnp.bfloat16)


def high(values):
    return values.astype(jnp.float32)


def rows_rsqrt(values):
    return lax.rsqrt(jnp.mean(values * values, axis=-1, keepdims=True) + EPSILON)


def call(kernel, operands, in_specs, out_shape, scratch, flops, moved, grant=24 * MIB):
    return pl.pallas_call(
        kernel,
        in_specs=in_specs,
        out_specs=VMEM,
        out_shape=out_shape,
        scratch_shapes=scratch,
        compiler_params=pltpu.CompilerParams(vmem_limit_bytes=grant),
        cost_estimate=pl.CostEstimate(flops=flops, bytes_accessed=moved, transcendentals=0),
    )(*operands)


def fetch(source, target, sem):
    copy = pltpu.make_async_copy(source, target, sem)
    copy.start()
    return copy


def forward_cluster(tiles, kept, out):
    def load(c):
        return jnp.concatenate([kept[t, :, c * HD : (c + 1) * HD] for t in tiles], axis=0)

    q, k, v = load(0), load(1), load(2)
    weights = low(jnp.exp(dot(q, k, NT) * (HD ** -0.5)))
    wide = jnp.concatenate([v, jnp.ones_like(v)], axis=1)
    sums = dot(weights, wide, NN)
    result = low(sums[:, :HD] / sums[:, HD:])
    for i, t in enumerate(tiles):
        out[t] = result[i * TILE : (i + 1) * TILE]


def backward_cluster(tiles, kept, out, scales, grads):
    def load(c):
        return jnp.concatenate([kept[t, :, c * HD : (c + 1) * HD] for t in tiles], axis=0)

    def scale(c):
        return jnp.concatenate([scales[t, :, c * HD : (c + 1) * HD] for t in tiles], axis=0)

    q, k, v = load(0), load(1), load(2)
    g = jnp.concatenate([grads[t] for t in tiles], axis=0)
    factor = HD ** -0.5
    weights = jnp.exp(dot(k, q, NT) * factor)
    softmax = weights * (1.0 / jnp.sum(weights, axis=0, keepdims=True))
    soft_low = low(softmax)
    grad_soft = dot(v, g, NT)
    delta = jnp.sum(high(soft_low) * grad_soft, axis=0, keepdims=True)
    grad_scores = low(softmax * (grad_soft - delta))
    grad_values = low(dot(soft_low, g, NN))
    results = [grad_values]
    for c, unit, grad in (
        (1, k, dot(grad_scores, q, NN)),
        (0, q, dot(grad_scores, k, TN)),
    ):
        rounded = high(low(grad * factor))
        unit = high(unit)
        mean = jnp.mean(unit * rounded, axis=1, keepdims=True)
        results.append(low(scale(c) * (rounded - unit * mean)))
    for c, result in zip((2, 1, 0), results):
        for i, t in enumerate(tiles):
            out[t, :, c * HD : (c + 1) * HD] = result[i * TILE : (i + 1) * TILE]


def head_kernel(back, unread, pieces, spacing, *refs):
    cluster_ref, info_ref, w_ref = refs[:3]
    x_refs = refs[3 : 3 + len(pieces)]
    refs = refs[3 + len(pieces) :]
    if back:
        grads, refs = refs[0], refs[1:]
    out, kept, count, member = refs[unread : unread + 4]
    if back:
        scales = refs[unread + 4]
    flip, residue = info_ref[0], info_ref[2]
    tiles = kept.shape[0]
    clusters = count.shape[0]
    for c in range(clusters):
        count[c] = 0

    def enter(t, carry):
        c = cluster_ref[t * spacing + residue] // spacing
        place = count[c]
        member[c * CAPACITY + place] = t
        count[c] = place + 1
        return carry

    lax.fori_loop(0, tiles, enter, 0)

    weights = w_ref[...]
    for (slot, start, rows), x_ref in zip(pieces, x_refs):
        normed = x_ref[...]
        if back:
            x = high(normed)
            normed = low(x * rows_rsqrt(x))
        mixed = dot(normed, weights, NT)
        place = 2 * (flip ^ slot) + start // TILE
        for c in range(3):
            u = mixed[:, c * HD : (c + 1) * HD]
            if c < 2:
                scale = rows_rsqrt(u)
                u = u * scale
            for j in range(rows // TILE):
                kept[place + j, :, c * HD : (c + 1) * HD] = low(u[j * TILE : (j + 1) * TILE])
                if back and c < 2:
                    scales[place + j, :, c * HD : (c + 1) * HD] = jnp.broadcast_to(
                        scale[j * TILE : (j + 1) * TILE], (TILE, HD)
                    )

    def visit(c, carry):
        for n in range(1, CAPACITY + 1):

            @pl.when(count[c] == n)
            def _():
                held = [member[c * CAPACITY + i] for i in range(n)]
                if back:
                    backward_cluster(held, kept, out, scales, grads)
                else:
                    forward_cluster(held, kept, out)

        return carry

    lax.fori_loop(0, clusters, visit, 0)


def head_work(info, tile_cluster, pieces, weights, spacing, grads=None, earlier=()):
    back = grads is not None
    width = weights.shape[1]
    tiles = 2 * HEADS
    wide = 3 * HD if back else HD
    tokens = tiles * TILE
    operands = [tile_cluster, info, weights] + [array for _, _, array in pieces]
    if back:
        operands.append(grads.reshape(tiles, TILE, HD))
    scratch = [
        pltpu.VMEM((tiles, TILE, 3 * HD), jnp.bfloat16),
        pltpu.SMEM((tiles // 2,), jnp.int32),
        pltpu.SMEM((tiles // 2 * CAPACITY,), jnp.int32),
    ]
    if back:
        scratch.append(pltpu.VMEM((tiles, TILE, 2 * HD), jnp.float32))
    shapes = tuple((k, start, array.shape[0]) for k, start, array in pieces)
    out = call(
        functools.partial(head_kernel, back, len(earlier), shapes, spacing),
        operands + list(earlier),
        [SMEM, SMEM] + [VMEM] * (len(operands) - 2) + [HBM] * len(earlier),
        jax.ShapeDtypeStruct((tiles, TILE, wide), jnp.bfloat16),
        scratch,
        MICROSECOND * (12 if back else 8),
        2 * tokens * (width + 2 * wide),
    )
    return out.reshape(HEADS, 2 * TILE, wide)


def copy_kernel(starts, *refs):
    count = len(starts)
    outs, sems = refs[-count - 1 : -1], refs[-1]
    copies = [
        fetch(refs[i].at[pl.ds(start, outs[i].shape[0])], outs[i], sems.at[i])
        for i, start in enumerate(starts)
    ]
    for copy in copies:
        copy.wait()


def rows_after(arrays, starts, rows, earlier):
    return pl.pallas_call(
        functools.partial(copy_kernel, starts),
        in_specs=[HBM] * (len(arrays) + len(earlier)),
        out_specs=[VMEM] * len(arrays),
        out_shape=[jax.ShapeDtypeStruct((rows, *a.shape[1:]), a.dtype) for a in arrays],
        scratch_shapes=[pltpu.SemaphoreType.DMA((len(arrays),))],
    )(*arrays, *earlier)


def norm_kernel(x_ref, *refs):
    out_ref = refs[-1]
    x = high(x_ref[...])
    out_ref[...] = low(x * rows_rsqrt(x))


def norm_after(x, earlier):
    return call(
        norm_kernel,
        [x, *earlier],
        [VMEM] + [HBM] * len(earlier),
        jax.ShapeDtypeStruct(x.shape, jnp.bfloat16),
        [],
        4 * x.size,
        4 * x.size,
    )


def spread_kernel(up_ref, w_ref, out_ref, rows, sems):
    copies = [fetch(w_ref.at[k], rows.at[k], sems.at[k]) for k in range(HEADS)]
    for k in range(0, HEADS, 2):
        copies[k].wait()
        copies[k + 1].wait()
        pair = rows[k : k + 2].reshape(2 * HD, -1)
        g = low(dot(up_ref[...], pair, NT))
        out_ref[k] = g[:, :HD]
        out_ref[k + 1] = g[:, HD:]


def spread_grads(upstream, w_fin):
    tokens, width = upstream.shape
    return call(
        spread_kernel,
        [upstream, w_fin.reshape(HEADS, HD, width)],
        [VMEM, HBM],
        jax.ShapeDtypeStruct((HEADS, tokens, HD), jnp.bfloat16),
        [
            pltpu.VMEM((HEADS, HD, width), jnp.bfloat16),
            pltpu.SemaphoreType.DMA((HEADS,)),
        ],
        MICROSECOND * 3,
        2 * width * HEADS * HD,
    )


def finish_kernel(att_ref, x_ref, w_ref, out_ref):
    att = jnp.concatenate([att_ref[k] for k in range(HEADS)], axis=1)
    block = 256
    for start in range(0, x_ref.shape[1], block):
        columns = slice(start, start + block)
        out_ref[:, columns] = low(high(x_ref[:, columns]) + dot(att, w_ref[:, columns], NN))


def finish(attention, current, w_fin):
    tokens, width = current.shape
    return call(
        finish_kernel,
        [attention, current, w_fin],
        [VMEM] * 3,
        jax.ShapeDtypeStruct((tokens, width), jnp.bfloat16),
        [],
        2 * tokens * width * HEADS * HD,
        2 * width * HEADS * HD,
    )


def finish_back_kernel(grad_ref, x_ref, up_ref, w_ref, out_ref, total):
    for c in range(3):
        grads = jnp.concatenate(
            [grad_ref[k, :, c * HD : (c + 1) * HD] for k in range(HEADS)], axis=1
        )
        product = dot(grads, w_ref[c * HEADS * HD : (c + 1) * HEADS * HD], NN)
        if c == 0:
            total[...] = product
        else:
            total[...] += product
    x = high(x_ref[...])
    scale = rows_rsqrt(x)
    unit = x * scale
    g = total[...]
    pulled = scale * (g - unit * jnp.mean(unit * g, axis=1, keepdims=True))
    out_ref[...] = low(high(up_ref[...]) + pulled)


def finish_back(grads, stored, upstream, w_qkv):
    tokens, width = stored.shape
    return call(
        finish_back_kernel,
        [grads, stored, upstream, w_qkv],
        [VMEM] * 4,
        jax.ShapeDtypeStruct((tokens, width), jnp.bfloat16),
        [pltpu.VMEM((tokens, width), jnp.float32)],
        2 * tokens * width * 3 * HEADS * HD,
        6 * width * HEADS * HD,
    )


def partner(block, distance):
    route = [(i, i ^ distance) for i in range(lax.axis_size("seq"))]
    return lax.ppermute(block, "seq", route)


def gather_rows(x, earlier):
    half = x.shape[0] // 2
    over_x, over_y = partner(x, 2), partner(x, 4)
    top, bottom = rows_after([over_x, over_y], [0, half], half, earlier)
    top, bottom = partner(top, 4), partner(bottom, 2)
    pieces = [(0, 0, x), (2, 0, over_x), (4, 0, over_y), (6, 0, top), (6, half, bottom)]
    return pieces + [(k + 1, start, partner(block, 1)) for k, start, block in pieces]


def all_swap(blocks):
    return lax.all_to_all(blocks, "seq", split_axis=0, concat_axis=0, tiled=True)


def to_heads(blocks, own, spacing):
    heads, tokens, width = blocks.shape
    held = tokens // TILE
    places = spacing // held
    tiled = blocks.reshape(heads, 1, held, TILE, width)
    padded = jnp.zeros((heads, places, held, TILE, width), blocks.dtype)
    padded = lax.dynamic_update_slice_in_dim(padded, tiled, own % places, 1)
    arrived = all_swap(padded.reshape(heads * spacing, TILE, width))
    arrived = arrived.reshape(-1, places, TILE, width)
    mine = lax.dynamic_index_in_dim(arrived, own % spacing // held, 1, keepdims=False)
    return mine.reshape(HEADS, 2 * TILE, width)


def to_tokens(blocks, own, spacing, tokens):
    held = tokens // TILE
    places = spacing // held
    tiled = blocks.reshape(2 * HEADS, 1, TILE, -1)
    padded = jnp.zeros((2 * HEADS, places, TILE, tiled.shape[3]), tiled.dtype)
    padded = lax.dynamic_update_slice_in_dim(padded, tiled, own % spacing // held, 1)
    returned = all_swap(padded.reshape(-1, TILE, tiled.shape[3]))
    returned = returned.reshape(HEADS, places, held * TILE, tiled.shape[3])
    return lax.dynamic_index_in_dim(returned, own % places, 1, keepdims=False)


def passed_along(block, axis, distance):
    devices = range(lax.axis_size(axis))
    route = [(i - distance, i) for i in devices if i - distance in devices]
    return lax.ppermute(block, axis, route)


def per_device(section_input, saved_input, grad_output, w_qkv, w_out, tile_cluster):
    current, stored, upstream = section_input[0], saved_input[0], grad_output[0]
    w_rows, w_fin = w_qkv[0], w_out[0]
    tokens = current.shape[0]
    spacing = lax.axis_size("seq") // HEADS
    own = lax.axis_index("seq").astype(jnp.int32)
    if spacing == 1:
        info = jnp.stack([own, own, jnp.zeros_like(own)])
        gather, spread, collect = gather_rows, all_swap, all_swap
    else:
        info = jnp.stack([jnp.zeros_like(own), own // spacing, own % spacing])

        def gather(x, earlier):
            copies = jnp.broadcast_to(x, (HEADS, *x.shape))
            return [(k, 0, block) for k, block in enumerate(to_heads(copies, own, spacing))]

        def spread(blocks):
            return to_heads(blocks, own, spacing)

        def collect(blocks):
            return to_tokens(blocks, own, spacing, tokens)

    own_head = w_rows.reshape(3, HEADS, HD, -1)
    own_head = lax.dynamic_index_in_dim(own_head, info[1], 1, keepdims=False)
    own_head = own_head.reshape(3 * HD, -1)
    spreading = spread_grads(upstream, w_fin)
    stored_pieces = gather(stored, [spreading])
    grad_attention = spread(spreading)
    earlier = [block for k, _, block in stored_pieces if k == HEADS - 2]
    normed = norm_after(current, [*earlier, grad_attention])
    grads = head_work(
        info, tile_cluster, stored_pieces, own_head, spacing, grad_attention, [normed]
    )
    current_pieces = gather(normed, [grads])
    returned_grads = collect(grads)
    outputs = head_work(
        info, tile_cluster, current_pieces, own_head, spacing, earlier=[grads]
    )
    outputs = rows_after([outputs], [0], HEADS, [returned_grads])[0]
    returned = collect(outputs)
    grad_self = finish_back(returned_grads, stored, upstream, w_rows)
    grad_input = passed_along(grad_self, "pipe", -1)
    result = finish(returned, current, w_fin)
    next_input = passed_along(result, "pipe", 1)
    return (next_input[None], grad_input[None])


def solution(mesh):
    return jax.shard_map(
        per_device,
        mesh=mesh,
        in_specs=(
            P("pipe", "seq", None),
            P("pipe", "seq", None),
            P("pipe", "seq", None),
            P("pipe", None, None),
            P("pipe", None, None),
            P(),
        ),
        out_specs=(P("pipe", "seq", None), P("pipe", "seq", None)),
        check_vma=False,
    )
```

```python
import functools

import jax
import jax.numpy as jnp
from jax import lax
from jax.experimental import pallas as pl
from jax.experimental.pallas import tpu as pltpu
from jax.sharding import PartitionSpec as P

HEADS = 8
HD = 128
TILE = 128
CAPACITY = 3
EPSILON = 1e-05
MIB = 1024 * 1024
MICROSECOND = 1150000000
NT = (((1,), (1,)), ((), ()))
NN = (((1,), (0,)), ((), ()))
TN = (((0,), (0,)), ((), ()))
HBM = pl.BlockSpec(memory_space=pl.ANY)
SMEM = pl.BlockSpec(memory_space=pltpu.SMEM)
VMEM = pl.BlockSpec(memory_space=pltpu.VMEM)


def dot(left, right, dims):
    return lax.dot_general(left, right, dims, preferred_element_type=jnp.float32)


def low(values):
    return values.astype(jnp.bfloat16)


def high(values):
    return values.astype(jnp.float32)


def rows_rsqrt(values):
    return lax.rsqrt(jnp.mean(values * values, axis=-1, keepdims=True) + EPSILON)


def call(kernel, operands, in_specs, out_shape, scratch, flops, moved, grant=24 * MIB):
    return pl.pallas_call(
        kernel,
        in_specs=in_specs,
        out_specs=[VMEM] * len(out_shape) if isinstance(out_shape, list) else VMEM,
        out_shape=out_shape,
        scratch_shapes=scratch,
        compiler_params=pltpu.CompilerParams(vmem_limit_bytes=grant),
        cost_estimate=pl.CostEstimate(flops=flops, bytes_accessed=moved, transcendentals=0),
    )(*operands)


def fetch(source, target, sem):
    copy = pltpu.make_async_copy(source, target, sem)
    copy.start()
    return copy


def forward_cluster(tiles, kept, out):
    def load(c):
        return jnp.concatenate([kept[t, :, c * HD : (c + 1) * HD] for t in tiles], axis=0)

    q, k, v = load(0), load(1), load(2)
    weights = low(jnp.exp(dot(q, k, NT) * (HD ** -0.5)))
    wide = jnp.concatenate([v, jnp.ones_like(v)], axis=1)
    sums = dot(weights, wide, NN)
    result = low(sums[:, :HD] / sums[:, HD:])
    for i, t in enumerate(tiles):
        out[t] = result[i * TILE : (i + 1) * TILE]


def backward_cluster(tiles, kept, out, scales, grads):
    def load(c):
        return jnp.concatenate([kept[t, :, c * HD : (c + 1) * HD] for t in tiles], axis=0)

    def scale(c):
        return jnp.concatenate([scales[t, :, c * HD : (c + 1) * HD] for t in tiles], axis=0)

    q, k, v = load(0), load(1), load(2)
    g = jnp.concatenate([grads[t] for t in tiles], axis=0)
    factor = HD ** -0.5
    weights = jnp.exp(dot(k, q, NT) * factor)
    softmax = weights * (1.0 / jnp.sum(weights, axis=0, keepdims=True))
    soft_low = low(softmax)
    grad_soft = dot(v, g, NT)
    delta = jnp.sum(high(soft_low) * grad_soft, axis=0, keepdims=True)
    grad_scores = low(softmax * (grad_soft - delta))
    grad_values = low(dot(soft_low, g, NN))
    results = [grad_values]
    for c, unit, grad in (
        (1, k, dot(grad_scores, q, NN)),
        (0, q, dot(grad_scores, k, TN)),
    ):
        rounded = high(low(grad * factor))
        unit = high(unit)
        mean = jnp.mean(unit * rounded, axis=1, keepdims=True)
        results.append(low(scale(c) * (rounded - unit * mean)))
    for c, result in zip((2, 1, 0), results):
        for i, t in enumerate(tiles):
            half = pl.ds(t % 2 * TILE, TILE)
            out[t // 2, half, c * HD : (c + 1) * HD] = result[i * TILE : (i + 1) * TILE]


def head_kernel(back, unread, pieces, spacing, *refs):
    cluster_ref, info_ref, w_ref = refs[:3]
    x_refs = refs[3 : 3 + len(pieces)]
    refs = refs[3 + len(pieces) :]
    if back:
        grads, refs = refs[0], refs[1:]
    refs = refs[unread:]
    if back:
        out, kept, count, member, scales = refs
    else:
        out_refs, (kept, count, member, out) = refs[:HEADS], refs[HEADS:]
    flip, residue = info_ref[0], info_ref[2]
    tiles = kept.shape[0]
    clusters = count.shape[0]
    for c in range(clusters):
        count[c] = 0

    def enter(t, carry):
        c = cluster_ref[t * spacing + residue] // spacing
        place = count[c]
        member[c * CAPACITY + place] = t
        count[c] = place + 1
        return carry

    lax.fori_loop(0, tiles, enter, 0)

    weights = w_ref[...]
    for (slot, start, rows), x_ref in zip(pieces, x_refs):
        normed = x_ref[...]
        if back:
            x = high(normed)
            normed = low(x * rows_rsqrt(x))
        mixed = dot(normed, weights, NT)
        place = 2 * (flip ^ slot) + start // TILE
        for c in range(3):
            u = mixed[:, c * HD : (c + 1) * HD]
            if c < 2:
                scale = rows_rsqrt(u)
                u = u * scale
            for j in range(rows // TILE):
                kept[place + j, :, c * HD : (c + 1) * HD] = low(u[j * TILE : (j + 1) * TILE])
                if back and c < 2:
                    scales[place + j, :, c * HD : (c + 1) * HD] = jnp.broadcast_to(
                        scale[j * TILE : (j + 1) * TILE], (TILE, HD)
                    )

    def visit(c, carry):
        for n in range(1, CAPACITY + 1):

            @pl.when(count[c] == n)
            def _():
                held = [member[c * CAPACITY + i] for i in range(n)]
                if back:
                    backward_cluster(held, kept, out, scales, grads)
                else:
                    forward_cluster(held, kept, out)

        return carry

    lax.fori_loop(0, clusters, visit, 0)
    if not back:
        for k in range(HEADS):
            out_refs[k][...] = out[pl.ds(2 * (flip ^ k), 2)].reshape(out_refs[k].shape)


def head_work(info, tile_cluster, pieces, weights, spacing, grads=None, earlier=()):
    back = grads is not None
    width = weights.shape[1]
    tiles = 2 * HEADS
    wide = 3 * HD if back else HD
    tokens = tiles * TILE
    operands = [tile_cluster, info, weights] + [array for _, _, array in pieces]
    if back:
        operands.append(grads.reshape(tiles, TILE, HD))
    scratch = [
        pltpu.VMEM((tiles, TILE, 3 * HD), jnp.bfloat16),
        pltpu.SMEM((tiles // 2,), jnp.int32),
        pltpu.SMEM((tiles // 2 * CAPACITY,), jnp.int32),
    ]
    if back:
        scratch.append(pltpu.VMEM((tiles, TILE, 2 * HD), jnp.float32))
        shape = jax.ShapeDtypeStruct((HEADS, 2 * TILE, wide), jnp.bfloat16)
    else:
        scratch.append(pltpu.VMEM((tiles, TILE, HD), jnp.bfloat16))
        shape = [jax.ShapeDtypeStruct((2 * TILE, HD), jnp.bfloat16) for _ in range(HEADS)]
    shapes = tuple((k, start, array.shape[0]) for k, start, array in pieces)
    return call(
        functools.partial(head_kernel, back, len(earlier), shapes, spacing),
        operands + list(earlier),
        [SMEM, SMEM] + [VMEM] * (len(operands) - 2) + [HBM] * len(earlier),
        shape,
        scratch,
        MICROSECOND * (12 if back else 8),
        2 * tokens * (width + 2 * wide),
    )

def copy_kernel(starts, *refs):
    count = len(starts)
    outs, sems = refs[-count - 1 : -1], refs[-1]
    copies = [
        fetch(refs[i].at[pl.ds(start, outs[i].shape[0])], outs[i], sems.at[i])
        for i, start in enumerate(starts)
    ]
    for copy in copies:
        copy.wait()


def rows_after(arrays, starts, rows, earlier):
    rows = [rows] * len(arrays) if isinstance(rows, int) else rows
    return pl.pallas_call(
        functools.partial(copy_kernel, starts),
        in_specs=[HBM] * (len(arrays) + len(earlier)),
        out_specs=[VMEM] * len(arrays),
        out_shape=[jax.ShapeDtypeStruct((n, *a.shape[1:]), a.dtype) for n, a in zip(rows, arrays)],
        scratch_shapes=[pltpu.SemaphoreType.DMA((len(arrays),))],
        compiler_params=pltpu.CompilerParams(vmem_limit_bytes=24 * MIB),
        cost_estimate=pl.CostEstimate(flops=MICROSECOND, bytes_accessed=0, transcendentals=0),
    )(*arrays, *earlier)


def norm_kernel(x_ref, *refs):
    out_ref = refs[-1]
    x = high(x_ref[...])
    out_ref[...] = low(x * rows_rsqrt(x))


def norm_after(x, earlier):
    return call(
        norm_kernel,
        [x, *earlier],
        [VMEM] + [HBM] * len(earlier),
        jax.ShapeDtypeStruct(x.shape, jnp.bfloat16),
        [],
        4 * x.size,
        4 * x.size,
    )


def spread_kernel(up_ref, w_ref, out_ref, rows, sems):
    copies = [fetch(w_ref.at[k], rows.at[k], sems.at[k]) for k in range(HEADS)]
    for k in range(0, HEADS, 2):
        copies[k].wait()
        copies[k + 1].wait()
        pair = rows[k : k + 2].reshape(2 * HD, -1)
        g = low(dot(up_ref[...], pair, NT))
        out_ref[k] = g[:, :HD]
        out_ref[k + 1] = g[:, HD:]


def spread_grads(upstream, w_fin):
    tokens, width = upstream.shape
    return call(
        spread_kernel,
        [upstream, w_fin.reshape(HEADS, HD, width)],
        [VMEM, HBM],
        jax.ShapeDtypeStruct((HEADS, tokens, HD), jnp.bfloat16),
        [
            pltpu.VMEM((HEADS, HD, width), jnp.bfloat16),
            pltpu.SemaphoreType.DMA((HEADS,)),
        ],
        MICROSECOND * 3,
        2 * width * HEADS * HD,
    )


def finish_kernel(info_ref, *refs):
    att_refs, (x_ref, w_ref, out_ref) = refs[:HEADS], refs[HEADS:]
    flip = info_ref[0]
    att = jnp.concatenate([ref[...] for ref in att_refs], axis=1)
    block = 256
    for start in range(0, x_ref.shape[1], block):
        columns = slice(start, start + block)
        w = jnp.concatenate([w_ref[flip ^ k, :, columns] for k in range(HEADS)], axis=0)
        out_ref[:, columns] = low(high(x_ref[:, columns]) + dot(att, w, NN))


def finish(info, attention, current, w_fin):
    tokens, width = current.shape
    return call(
        finish_kernel,
        [info, *attention, current, w_fin.reshape(HEADS, HD, width)],
        [SMEM] + [VMEM] * (HEADS + 2),
        jax.ShapeDtypeStruct((tokens, width), jnp.bfloat16),
        [],
        2 * tokens * width * HEADS * HD,
        2 * width * HEADS * HD,
    )


def finish_back_kernel(grad_ref, x_ref, up_ref, w_ref, out_ref, total):
    for c in range(3):
        grads = jnp.concatenate(
            [grad_ref[k, :, c * HD : (c + 1) * HD] for k in range(HEADS)], axis=1
        )
        product = dot(grads, w_ref[c * HEADS * HD : (c + 1) * HEADS * HD], NN)
        if c == 0:
            total[...] = product
        else:
            total[...] += product
    x = high(x_ref[...])
    scale = rows_rsqrt(x)
    unit = x * scale
    g = total[...]
    pulled = scale * (g - unit * jnp.mean(unit * g, axis=1, keepdims=True))
    out_ref[...] = low(high(up_ref[...]) + pulled)


def finish_back(grads, stored, upstream, w_qkv):
    tokens, width = stored.shape
    return call(
        finish_back_kernel,
        [grads, stored, upstream, w_qkv],
        [VMEM] * 4,
        jax.ShapeDtypeStruct((tokens, width), jnp.bfloat16),
        [pltpu.VMEM((tokens, width), jnp.float32)],
        2 * tokens * width * 3 * HEADS * HD,
        6 * width * HEADS * HD,
    )


def partner(block, distance):
    route = [(i, i ^ distance) for i in range(lax.axis_size("seq"))]
    return lax.ppermute(block, "seq", route)


def gather_rows(x, earlier):
    half = x.shape[0] // 2
    over_x, over_y = partner(x, 2), partner(x, 4)
    if earlier:
        top, bottom = rows_after([over_x, over_y], [0, half], half, earlier)
    else:
        top, bottom = over_x[:half], over_y[half:]
    top, bottom = partner(top, 4), partner(bottom, 2)
    pieces = [(0, 0, x), (2, 0, over_x), (4, 0, over_y), (6, 0, top), (6, half, bottom)]
    return pieces + [(k + 1, start, partner(block, 1)) for k, start, block in pieces]


def swap(blocks):
    moved = {k: partner(blocks[k], k) for k in (2, 4, 6, 3, 5, 7, 1)}
    return [blocks[0]] + [moved[k] for k in range(1, HEADS)]


def all_swap(blocks):
    return lax.all_to_all(blocks, "seq", split_axis=0, concat_axis=0, tiled=True)


def to_heads(blocks, own, spacing):
    heads, tokens, width = blocks.shape
    held = tokens // TILE
    places = spacing // held
    tiled = blocks.reshape(heads, 1, held, TILE, width)
    padded = jnp.zeros((heads, places, held, TILE, width), blocks.dtype)
    padded = lax.dynamic_update_slice_in_dim(padded, tiled, own % places, 1)
    arrived = all_swap(padded.reshape(heads * spacing, TILE, width))
    arrived = arrived.reshape(-1, places, TILE, width)
    mine = lax.dynamic_index_in_dim(arrived, own % spacing // held, 1, keepdims=False)
    return mine.reshape(HEADS, 2 * TILE, width)


def to_tokens(blocks, own, spacing, tokens):
    held = tokens // TILE
    places = spacing // held
    tiled = blocks.reshape(2 * HEADS, 1, TILE, -1)
    padded = jnp.zeros((2 * HEADS, places, TILE, tiled.shape[3]), tiled.dtype)
    padded = lax.dynamic_update_slice_in_dim(padded, tiled, own % spacing // held, 1)
    returned = all_swap(padded.reshape(-1, TILE, tiled.shape[3]))
    returned = returned.reshape(HEADS, places, held * TILE, tiled.shape[3])
    return lax.dynamic_index_in_dim(returned, own % places, 1, keepdims=False)


def passed_along(block, axis, distance):
    devices = range(lax.axis_size(axis))
    route = [(i - distance, i) for i in devices if i - distance in devices]
    return lax.ppermute(block, axis, route)


def per_device(section_input, saved_input, grad_output, w_qkv, w_out, tile_cluster):
    current, stored, upstream = section_input[0], saved_input[0], grad_output[0]
    w_rows, w_fin = w_qkv[0], w_out[0]
    tokens = current.shape[0]
    spacing = lax.axis_size("seq") // HEADS
    own = lax.axis_index("seq").astype(jnp.int32)
    if spacing == 1:
        info = jnp.stack([own, own, jnp.zeros_like(own)])
        gather, spread, collect, collect_each = gather_rows, all_swap, all_swap, swap
    else:
        info = jnp.stack([jnp.zeros_like(own), own // spacing, own % spacing])

        def gather(x, earlier):
            copies = jnp.broadcast_to(x, (HEADS, *x.shape))
            return [(k, 0, block) for k, block in enumerate(to_heads(copies, own, spacing))]

        def spread(blocks):
            return to_heads(blocks, own, spacing)

        def collect(blocks):
            return to_tokens(blocks, own, spacing, tokens)

        def collect_each(blocks):
            return list(collect(jnp.stack(blocks)))

    own_head = w_rows.reshape(3, HEADS, HD, -1)
    own_head = lax.dynamic_index_in_dim(own_head, info[1], 1, keepdims=False)
    own_head = own_head.reshape(3 * HD, -1)
    spreading = spread_grads(upstream, w_fin)
    stored_pieces = gather(stored, [])
    grad_attention = spread(spreading)
    earlier = [block for k, _, block in stored_pieces if k == HEADS - 2]
    normed = norm_after(current, [*earlier, grad_attention])
    grads = head_work(
        info, tile_cluster, stored_pieces, own_head, spacing, grad_attention, [normed]
    )
    current_pieces = gather(normed, [grads])
    returned_grads = collect(grads)
    outputs = head_work(
        info, tile_cluster, current_pieces, own_head, spacing, earlier=[grads]
    )
    returned = collect_each(outputs)
    near = [stored, upstream, w_rows]
    near = rows_after(near, [0] * 3, [a.shape[0] for a in near], outputs[:1])
    grad_self = finish_back(returned_grads, *near)
    grad_input = passed_along(grad_self, "pipe", -1)
    result = finish(info, returned, current, w_fin)
    next_input = passed_along(result, "pipe", 1)
    return (next_input[None], grad_input[None])


def solution(mesh):
    return jax.shard_map(
        per_device,
        mesh=mesh,
        in_specs=(
            P("pipe", "seq", None),
            P("pipe", "seq", None),
            P("pipe", "seq", None),
            P("pipe", None, None),
            P("pipe", None, None),
            P(),
        ),
        out_specs=(P("pipe", "seq", None), P("pipe", "seq", None)),
        check_vma=False,
    )
```

```python
import functools

import jax
import jax.numpy as jnp
from jax import lax
from jax.experimental import pallas as pl
from jax.experimental.pallas import tpu as pltpu
from jax.sharding import PartitionSpec as P

HEADS = 8
HD = 128
TILE = 128
CAPACITY = 3
EPSILON = 1e-05
MIB = 1024 * 1024
MICROSECOND = 1150000000
NT = (((1,), (1,)), ((), ()))
NN = (((1,), (0,)), ((), ()))
TN = (((0,), (0,)), ((), ()))
HBM = pl.BlockSpec(memory_space=pl.ANY)
SMEM = pl.BlockSpec(memory_space=pltpu.SMEM)
VMEM = pl.BlockSpec(memory_space=pltpu.VMEM)


def dot(left, right, dims):
    return lax.dot_general(left, right, dims, preferred_element_type=jnp.float32)


def low(values):
    return values.astype(jnp.bfloat16)


def high(values):
    return values.astype(jnp.float32)


def rows_rsqrt(values):
    return lax.rsqrt(jnp.mean(values * values, axis=-1, keepdims=True) + EPSILON)


def call(kernel, operands, in_specs, out_shape, scratch, flops, moved, grant=24 * MIB):
    return pl.pallas_call(
        kernel,
        in_specs=in_specs,
        out_specs=[VMEM] * len(out_shape) if isinstance(out_shape, list) else VMEM,
        out_shape=out_shape,
        scratch_shapes=scratch,
        compiler_params=pltpu.CompilerParams(vmem_limit_bytes=grant),
        cost_estimate=pl.CostEstimate(flops=flops, bytes_accessed=moved, transcendentals=0),
    )(*operands)


def fetch(source, target, sem):
    copy = pltpu.make_async_copy(source, target, sem)
    copy.start()
    return copy


def forward_cluster(tiles, kept, out):
    def load(c):
        return jnp.concatenate([kept[t, :, c * HD : (c + 1) * HD] for t in tiles], axis=0)

    q, k, v = load(0), load(1), load(2)
    weights = low(jnp.exp(dot(q, k, NT) * (HD ** -0.5)))
    wide = jnp.concatenate([v, jnp.ones_like(v)], axis=1)
    sums = dot(weights, wide, NN)
    result = low(sums[:, :HD] / sums[:, HD:])
    for i, t in enumerate(tiles):
        out[t] = result[i * TILE : (i + 1) * TILE]


def backward_cluster(tiles, kept, out, scales, grads):
    def load(c):
        return jnp.concatenate([kept[t, :, c * HD : (c + 1) * HD] for t in tiles], axis=0)

    def scale(c):
        return jnp.concatenate([scales[t, :, c * HD : (c + 1) * HD] for t in tiles], axis=0)

    q, k, v = load(0), load(1), load(2)
    g = jnp.concatenate([grads[t] for t in tiles], axis=0)
    factor = HD ** -0.5
    weights = jnp.exp(dot(k, q, NT) * factor)
    softmax = weights * (1.0 / jnp.sum(weights, axis=0, keepdims=True))
    soft_low = low(softmax)
    grad_soft = dot(v, g, NT)
    delta = jnp.sum(high(soft_low) * grad_soft, axis=0, keepdims=True)
    grad_scores = low(softmax * (grad_soft - delta))
    grad_values = low(dot(soft_low, g, NN))
    results = [grad_values]
    for c, unit, grad in (
        (1, k, dot(grad_scores, q, NN)),
        (0, q, dot(grad_scores, k, TN)),
    ):
        rounded = high(low(grad * factor))
        unit = high(unit)
        mean = jnp.mean(unit * rounded, axis=1, keepdims=True)
        results.append(low(scale(c) * (rounded - unit * mean)))
    for c, result in zip((2, 1, 0), results):
        for i, t in enumerate(tiles):
            half = pl.ds(t % 2 * TILE, TILE)
            out[t // 2, half, c * HD : (c + 1) * HD] = result[i * TILE : (i + 1) * TILE]


def head_kernel(back, unread, pieces, spacing, *refs):
    cluster_ref, info_ref, w_ref = refs[:3]
    x_refs = refs[3 : 3 + len(pieces)]
    refs = refs[3 + len(pieces) :]
    if back:
        grads, refs = refs[0], refs[1:]
    refs = refs[unread:]
    if back:
        out, kept, count, member, scales = refs
    else:
        out_refs, (kept, count, member, out) = refs[:HEADS], refs[HEADS:]
    flip, residue = info_ref[0], info_ref[2]
    tiles = kept.shape[0]
    clusters = count.shape[0]
    for c in range(clusters):
        count[c] = 0

    def enter(t, carry):
        c = cluster_ref[t * spacing + residue] // spacing
        place = count[c]
        member[c * CAPACITY + place] = t
        count[c] = place + 1
        return carry

    lax.fori_loop(0, tiles, enter, 0)

    weights = w_ref[...]
    for (slot, start, rows), x_ref in zip(pieces, x_refs):
        normed = x_ref[...]
        if back:
            x = high(normed)
            normed = low(x * rows_rsqrt(x))
        mixed = dot(normed, weights, NT)
        place = 2 * (flip ^ slot) + start // TILE
        for c in range(3):
            u = mixed[:, c * HD : (c + 1) * HD]
            if c < 2:
                scale = rows_rsqrt(u)
                u = u * scale
            for j in range(rows // TILE):
                kept[place + j, :, c * HD : (c + 1) * HD] = low(u[j * TILE : (j + 1) * TILE])
                if back and c < 2:
                    scales[place + j, :, c * HD : (c + 1) * HD] = jnp.broadcast_to(
                        scale[j * TILE : (j + 1) * TILE], (TILE, HD)
                    )

    def visit(c, carry):
        for n in range(1, CAPACITY + 1):

            @pl.when(count[c] == n)
            def _():
                held = [member[c * CAPACITY + i] for i in range(n)]
                if back:
                    backward_cluster(held, kept, out, scales, grads)
                else:
                    forward_cluster(held, kept, out)

        return carry

    lax.fori_loop(0, clusters, visit, 0)
    if not back:
        for k in range(HEADS):
            out_refs[k][...] = out[pl.ds(2 * (flip ^ k), 2)].reshape(out_refs[k].shape)


def head_work(info, tile_cluster, pieces, weights, spacing, grads=None, earlier=()):
    back = grads is not None
    width = weights.shape[1]
    tiles = 2 * HEADS
    wide = 3 * HD if back else HD
    tokens = tiles * TILE
    operands = [tile_cluster, info, weights] + [array for _, _, array in pieces]
    if back:
        operands.append(grads.reshape(tiles, TILE, HD))
    scratch = [
        pltpu.VMEM((tiles, TILE, 3 * HD), jnp.bfloat16),
        pltpu.SMEM((tiles // 2,), jnp.int32),
        pltpu.SMEM((tiles // 2 * CAPACITY,), jnp.int32),
    ]
    if back:
        scratch.append(pltpu.VMEM((tiles, TILE, 2 * HD), jnp.float32))
        shape = jax.ShapeDtypeStruct((HEADS, 2 * TILE, wide), jnp.bfloat16)
    else:
        scratch.append(pltpu.VMEM((tiles, TILE, HD), jnp.bfloat16))
        shape = [jax.ShapeDtypeStruct((2 * TILE, HD), jnp.bfloat16) for _ in range(HEADS)]
    shapes = tuple((k, start, array.shape[0]) for k, start, array in pieces)
    return call(
        functools.partial(head_kernel, back, len(earlier), shapes, spacing),
        operands + list(earlier),
        [SMEM, SMEM] + [VMEM] * (len(operands) - 2) + [HBM] * len(earlier),
        shape,
        scratch,
        MICROSECOND * (12 if back else 8),
        2 * tokens * (width + 2 * wide),
    )

def copy_kernel(starts, *refs):
    count = len(starts)
    outs, sems = refs[-count - 1 : -1], refs[-1]
    copies = [
        fetch(refs[i].at[pl.ds(start, outs[i].shape[0])], outs[i], sems.at[i])
        for i, start in enumerate(starts)
    ]
    for copy in copies:
        copy.wait()


def rows_after(arrays, starts, rows, earlier):
    return pl.pallas_call(
        functools.partial(copy_kernel, starts),
        in_specs=[HBM] * (len(arrays) + len(earlier)),
        out_specs=[VMEM] * len(arrays),
        out_shape=[jax.ShapeDtypeStruct((rows, *a.shape[1:]), a.dtype) for a in arrays],
        scratch_shapes=[pltpu.SemaphoreType.DMA((len(arrays),))],
        compiler_params=pltpu.CompilerParams(vmem_limit_bytes=24 * MIB),
        cost_estimate=pl.CostEstimate(flops=MICROSECOND, bytes_accessed=0, transcendentals=0),
    )(*arrays, *earlier)


def norm_kernel(x_ref, *refs):
    out_ref = refs[-1]
    x = high(x_ref[...])
    out_ref[...] = low(x * rows_rsqrt(x))


def norm_after(x, earlier):
    return call(
        norm_kernel,
        [x, *earlier],
        [VMEM] + [HBM] * len(earlier),
        jax.ShapeDtypeStruct(x.shape, jnp.bfloat16),
        [],
        4 * x.size,
        4 * x.size,
    )


def spread_kernel(up_ref, w_ref, out_ref, rows, sems):
    copies = [fetch(w_ref.at[k], rows.at[k], sems.at[k]) for k in range(HEADS)]
    for k in range(0, HEADS, 2):
        copies[k].wait()
        copies[k + 1].wait()
        pair = rows[k : k + 2].reshape(2 * HD, -1)
        g = low(dot(up_ref[...], pair, NT))
        out_ref[k] = g[:, :HD]
        out_ref[k + 1] = g[:, HD:]


def spread_grads(upstream, w_fin):
    tokens, width = upstream.shape
    return call(
        spread_kernel,
        [upstream, w_fin.reshape(HEADS, HD, width)],
        [VMEM, HBM],
        jax.ShapeDtypeStruct((HEADS, tokens, HD), jnp.bfloat16),
        [
            pltpu.VMEM((HEADS, HD, width), jnp.bfloat16),
            pltpu.SemaphoreType.DMA((HEADS,)),
        ],
        MICROSECOND * 3,
        2 * width * HEADS * HD,
    )


def finish_kernel(info_ref, *refs):
    att_refs, (x_ref, w_ref, out_ref) = refs[:HEADS], refs[HEADS:]
    flip = info_ref[0]
    att = jnp.concatenate([ref[...] for ref in att_refs], axis=1)
    block = 256
    for start in range(0, x_ref.shape[1], block):
        columns = slice(start, start + block)
        w = jnp.concatenate([w_ref[flip ^ k, :, columns] for k in range(HEADS)], axis=0)
        out_ref[:, columns] = low(high(x_ref[:, columns]) + dot(att, w, NN))


def finish(info, attention, current, w_fin):
    tokens, width = current.shape
    return call(
        finish_kernel,
        [info, *attention, current, w_fin.reshape(HEADS, HD, width)],
        [SMEM] + [VMEM] * (HEADS + 2),
        jax.ShapeDtypeStruct((tokens, width), jnp.bfloat16),
        [],
        2 * tokens * width * HEADS * HD,
        2 * width * HEADS * HD,
    )


def finish_back_kernel(grad_ref, x_ref, up_ref, w_ref, out_ref, grads, x, up, rows, total, sems):
    chunks = rows.shape[0]
    depth = rows.shape[1]
    held = depth // HD
    copies = [fetch(grad_ref, grads, sems.at[0])]
    copies += [
        fetch(w_ref.at[pl.ds(i * depth, depth)], rows.at[i], sems.at[1 + i]) for i in range(chunks)
    ]
    copies.append(fetch(x_ref, x, sems.at[1 + chunks]))
    copies.append(fetch(up_ref, up, sems.at[2 + chunks]))
    copies[0].wait()
    for i in range(chunks):
        c, first = i * held // HEADS, i * held % HEADS
        columns = slice(c * HD, (c + 1) * HD)
        block = jnp.concatenate([grads[first + j, :, columns] for j in range(held)], axis=1)
        copies[1 + i].wait()
        product = dot(block, rows[i], NN)
        if i == 0:
            total[...] = product
        else:
            total[...] += product
    copies[1 + chunks].wait()
    copies[2 + chunks].wait()
    stored = high(x[...])
    scale = rows_rsqrt(stored)
    unit = stored * scale
    g = total[...]
    pulled = scale * (g - unit * jnp.mean(unit * g, axis=1, keepdims=True))
    out_ref[...] = low(high(up[...]) + pulled)


def finish_back(grads, stored, upstream, w_qkv):
    tokens, width = stored.shape
    chunks = 6
    return call(
        finish_back_kernel,
        [grads, stored, upstream, w_qkv],
        [HBM] * 4,
        jax.ShapeDtypeStruct((tokens, width), jnp.bfloat16),
        [
            pltpu.VMEM(grads.shape, jnp.bfloat16),
            pltpu.VMEM((tokens, width), jnp.bfloat16),
            pltpu.VMEM((tokens, width), jnp.bfloat16),
            pltpu.VMEM((chunks, w_qkv.shape[0] // chunks, width), jnp.bfloat16),
            pltpu.VMEM((tokens, width), jnp.float32),
            pltpu.SemaphoreType.DMA((chunks + 3,)),
        ],
        MICROSECOND * 5,
        6 * width * HEADS * HD,
        grant=58 * MIB,
    )


def partner(block, distance):
    route = [(i, i ^ distance) for i in range(lax.axis_size("seq"))]
    return lax.ppermute(block, "seq", route)


def gather_rows(x, earlier):
    half = x.shape[0] // 2
    top, bottom = x[:half], x[half:]
    x_top, y_bottom = partner(top, 2), partner(bottom, 4)
    x_bottom, y_top = partner(bottom, 2), partner(top, 4)
    relay_top, relay_bottom = x_top, y_bottom
    if earlier:
        relay_top, relay_bottom = rows_after([x_top, y_bottom], [0, 0], half, earlier)
    far_top, far_bottom = partner(relay_top, 4), partner(relay_bottom, 2)
    pieces = [(0, 0, x), (2, 0, x_top), (4, half, y_bottom), (2, half, x_bottom)]
    pieces += [(4, 0, y_top), (6, 0, far_top), (6, half, far_bottom)]
    return pieces + [(k + 1, start, partner(block, 1)) for k, start, block in pieces]


def swap(blocks):
    moved = {k: partner(blocks[k], k) for k in (2, 4, 6, 3, 5, 7, 1)}
    return [blocks[0]] + [moved[k] for k in range(1, HEADS)]


def all_swap(blocks):
    return lax.all_to_all(blocks, "seq", split_axis=0, concat_axis=0, tiled=True)


def to_heads(blocks, own, spacing):
    heads, tokens, width = blocks.shape
    held = tokens // TILE
    places = spacing // held
    tiled = blocks.reshape(heads, 1, held, TILE, width)
    padded = jnp.zeros((heads, places, held, TILE, width), blocks.dtype)
    padded = lax.dynamic_update_slice_in_dim(padded, tiled, own % places, 1)
    arrived = all_swap(padded.reshape(heads * spacing, TILE, width))
    arrived = arrived.reshape(-1, places, TILE, width)
    mine = lax.dynamic_index_in_dim(arrived, own % spacing // held, 1, keepdims=False)
    return mine.reshape(HEADS, 2 * TILE, width)


def to_tokens(blocks, own, spacing, tokens):
    held = tokens // TILE
    places = spacing // held
    tiled = blocks.reshape(2 * HEADS, 1, TILE, -1)
    padded = jnp.zeros((2 * HEADS, places, TILE, tiled.shape[3]), tiled.dtype)
    padded = lax.dynamic_update_slice_in_dim(padded, tiled, own % spacing // held, 1)
    returned = all_swap(padded.reshape(-1, TILE, tiled.shape[3]))
    returned = returned.reshape(HEADS, places, held * TILE, tiled.shape[3])
    return lax.dynamic_index_in_dim(returned, own % places, 1, keepdims=False)


def passed_along(block, axis, distance):
    devices = range(lax.axis_size(axis))
    route = [(i - distance, i) for i in devices if i - distance in devices]
    return lax.ppermute(block, axis, route)


def per_device(section_input, saved_input, grad_output, w_qkv, w_out, tile_cluster):
    current, stored, upstream = section_input[0], saved_input[0], grad_output[0]
    w_rows, w_fin = w_qkv[0], w_out[0]
    tokens = current.shape[0]
    spacing = lax.axis_size("seq") // HEADS
    own = lax.axis_index("seq").astype(jnp.int32)
    if spacing == 1:
        info = jnp.stack([own, own, jnp.zeros_like(own)])
        gather, spread, collect, collect_each = gather_rows, all_swap, all_swap, swap
    else:
        info = jnp.stack([jnp.zeros_like(own), own // spacing, own % spacing])

        def gather(x, earlier):
            copies = jnp.broadcast_to(x, (HEADS, *x.shape))
            return [(k, 0, block) for k, block in enumerate(to_heads(copies, own, spacing))]

        def spread(blocks):
            return to_heads(blocks, own, spacing)

        def collect(blocks):
            return to_tokens(blocks, own, spacing, tokens)

        def collect_each(blocks):
            return list(collect(jnp.stack(blocks)))

    own_head = w_rows.reshape(3, HEADS, HD, -1)
    own_head = lax.dynamic_index_in_dim(own_head, info[1], 1, keepdims=False)
    own_head = own_head.reshape(3 * HD, -1)
    spreading = spread_grads(upstream, w_fin)
    stored_pieces = gather(stored, [])
    grad_attention = spread(spreading)
    earlier = [block for k, _, block in stored_pieces if k == HEADS - 2]
    normed = norm_after(current, [*earlier, grad_attention])
    grads = head_work(
        info, tile_cluster, stored_pieces, own_head, spacing, grad_attention, [normed]
    )
    current_pieces = gather(normed, [grads])
    returned_grads = collect(grads)
    outputs = head_work(
        info, tile_cluster, current_pieces, own_head, spacing, earlier=[grads]
    )
    returned = collect_each(outputs)
    grad_self = finish_back(returned_grads, stored, upstream, w_rows)
    grad_input = passed_along(grad_self, "pipe", -1)
    result = finish(info, returned, current, w_fin)
    next_input = passed_along(result, "pipe", 1)
    return (next_input[None], grad_input[None])


def solution(mesh):
    return jax.shard_map(
        per_device,
        mesh=mesh,
        in_specs=(
            P("pipe", "seq", None),
            P("pipe", "seq", None),
            P("pipe", "seq", None),
            P("pipe", None, None),
            P("pipe", None, None),
            P(),
        ),
        out_specs=(P("pipe", "seq", None), P("pipe", "seq", None)),
        check_vma=False,
    )
```

```python
import functools

import jax
import jax.numpy as jnp
from jax import lax
from jax.experimental import pallas as pl
from jax.experimental.pallas import tpu as pltpu
from jax.sharding import PartitionSpec as P

HEADS = 8
HD = 128
TILE = 128
CAPACITY = 3
EPSILON = 1e-05
MIB = 1024 * 1024
MICROSECOND = 1150000000
NT = (((1,), (1,)), ((), ()))
NN = (((1,), (0,)), ((), ()))
TN = (((0,), (0,)), ((), ()))
HBM = pl.BlockSpec(memory_space=pl.ANY)
SMEM = pl.BlockSpec(memory_space=pltpu.SMEM)
VMEM = pl.BlockSpec(memory_space=pltpu.VMEM)


def dot(left, right, dims):
    return lax.dot_general(left, right, dims, preferred_element_type=jnp.float32)


def low(values):
    return values.astype(jnp.bfloat16)


def high(values):
    return values.astype(jnp.float32)


def rows_rsqrt(values):
    return lax.rsqrt(jnp.mean(values * values, axis=-1, keepdims=True) + EPSILON)


def call(kernel, operands, in_specs, out_shape, scratch, flops, moved, grant=24 * MIB):
    return pl.pallas_call(
        kernel,
        in_specs=in_specs,
        out_specs=[VMEM] * len(out_shape) if isinstance(out_shape, list) else VMEM,
        out_shape=out_shape,
        scratch_shapes=scratch,
        compiler_params=pltpu.CompilerParams(vmem_limit_bytes=grant),
        cost_estimate=pl.CostEstimate(flops=flops, bytes_accessed=moved, transcendentals=0),
    )(*operands)


def fetch(source, target, sem):
    copy = pltpu.make_async_copy(source, target, sem)
    copy.start()
    return copy


def forward_cluster(tiles, kept, out):
    def load(c):
        return jnp.concatenate([kept[t, :, c * HD : (c + 1) * HD] for t in tiles], axis=0)

    q, k, v = load(0), load(1), load(2)
    weights = low(jnp.exp(dot(q, k, NT) * (HD ** -0.5)))
    wide = jnp.concatenate([v, jnp.ones_like(v)], axis=1)
    sums = dot(weights, wide, NN)
    result = low(sums[:, :HD] / sums[:, HD:])
    for i, t in enumerate(tiles):
        out[t] = result[i * TILE : (i + 1) * TILE]


def backward_cluster(tiles, kept, out, scales, grads):
    def load(c):
        return jnp.concatenate([kept[t, :, c * HD : (c + 1) * HD] for t in tiles], axis=0)

    def scale(c):
        return jnp.concatenate([scales[t, :, c * HD : (c + 1) * HD] for t in tiles], axis=0)

    q, k, v = load(0), load(1), load(2)
    g = jnp.concatenate([grads[t] for t in tiles], axis=0)
    factor = HD ** -0.5
    weights = jnp.exp(dot(k, q, NT) * factor)
    softmax = weights * (1.0 / jnp.sum(weights, axis=0, keepdims=True))
    soft_low = low(softmax)
    grad_soft = dot(v, g, NT)
    delta = jnp.sum(high(soft_low) * grad_soft, axis=0, keepdims=True)
    grad_scores = low(softmax * (grad_soft - delta))
    grad_values = low(dot(soft_low, g, NN))
    results = [grad_values]
    for c, unit, grad in (
        (1, k, dot(grad_scores, q, NN)),
        (0, q, dot(grad_scores, k, TN)),
    ):
        rounded = high(low(grad * factor))
        unit = high(unit)
        mean = jnp.mean(unit * rounded, axis=1, keepdims=True)
        results.append(low(scale(c) * (rounded - unit * mean)))
    for c, result in zip((2, 1, 0), results):
        for i, t in enumerate(tiles):
            out[t, :, c * HD : (c + 1) * HD] = result[i * TILE : (i + 1) * TILE]


def head_kernel(back, unread, pieces, spacing, *refs):
    cluster_ref, info_ref, w_ref = refs[:3]
    x_refs = refs[3 : 3 + len(pieces)]
    refs = refs[3 + len(pieces) :]
    if back:
        grads, refs = refs[0], refs[1:]
    refs = refs[unread:]
    out_refs, (kept, out, count, member) = refs[:HEADS], refs[HEADS : HEADS + 4]
    if back:
        scales = refs[HEADS + 4]
    flip, residue = info_ref[0], info_ref[2]
    tiles = kept.shape[0]
    clusters = count.shape[0]
    for c in range(clusters):
        count[c] = 0

    def enter(t, carry):
        c = cluster_ref[t * spacing + residue] // spacing
        place = count[c]
        member[c * CAPACITY + place] = t
        count[c] = place + 1
        return carry

    lax.fori_loop(0, tiles, enter, 0)

    weights = w_ref[...]
    for (slot, start, rows), x_ref in zip(pieces, x_refs):
        normed = x_ref[...]
        if back:
            x = high(normed)
            normed = low(x * rows_rsqrt(x))
        mixed = dot(normed, weights, NT)
        place = 2 * (flip ^ slot) + start // TILE
        for c in range(3):
            u = mixed[:, c * HD : (c + 1) * HD]
            if c < 2:
                scale = rows_rsqrt(u)
                u = u * scale
            for j in range(rows // TILE):
                kept[place + j, :, c * HD : (c + 1) * HD] = low(u[j * TILE : (j + 1) * TILE])
                if back and c < 2:
                    scales[place + j, :, c * HD : (c + 1) * HD] = jnp.broadcast_to(
                        scale[j * TILE : (j + 1) * TILE], (TILE, HD)
                    )

    def visit(c, carry):
        for n in range(1, CAPACITY + 1):

            @pl.when(count[c] == n)
            def _():
                held = [member[c * CAPACITY + i] for i in range(n)]
                if back:
                    backward_cluster(held, kept, out, scales, grads)
                else:
                    forward_cluster(held, kept, out)

        return carry

    lax.fori_loop(0, clusters, visit, 0)
    for k in range(HEADS):
        out_refs[k][...] = out[pl.ds(2 * (flip ^ k), 2)].reshape(out_refs[k].shape)


def head_work(info, tile_cluster, pieces, weights, spacing, grads=None, earlier=()):
    back = grads is not None
    width = weights.shape[1]
    tiles = 2 * HEADS
    wide = 3 * HD if back else HD
    tokens = tiles * TILE
    operands = [tile_cluster, info, weights] + [array for _, _, array in pieces]
    if back:
        operands.append(grads.reshape(tiles, TILE, HD))
    scratch = [
        pltpu.VMEM((tiles, TILE, 3 * HD), jnp.bfloat16),
        pltpu.VMEM((tiles, TILE, wide), jnp.bfloat16),
        pltpu.SMEM((tiles // 2,), jnp.int32),
        pltpu.SMEM((tiles // 2 * CAPACITY,), jnp.int32),
    ]
    if back:
        scratch.append(pltpu.VMEM((tiles, TILE, 2 * HD), jnp.float32))
    shapes = tuple((k, start, array.shape[0]) for k, start, array in pieces)
    return call(
        functools.partial(head_kernel, back, len(earlier), shapes, spacing),
        operands + list(earlier),
        [SMEM, SMEM] + [VMEM] * (len(operands) - 2) + [HBM] * len(earlier),
        [jax.ShapeDtypeStruct((2 * TILE, wide), jnp.bfloat16) for _ in range(HEADS)],
        scratch,
        MICROSECOND * (12 if back else 8),
        2 * tokens * (width + 2 * wide),
    )

def copy_kernel(starts, *refs):
    count = len(starts)
    outs, sems = refs[-count - 1 : -1], refs[-1]
    copies = [
        fetch(refs[i].at[pl.ds(start, outs[i].shape[0])], outs[i], sems.at[i])
        for i, start in enumerate(starts)
    ]
    for copy in copies:
        copy.wait()


def rows_after(arrays, starts, rows, earlier):
    return pl.pallas_call(
        functools.partial(copy_kernel, starts),
        in_specs=[HBM] * (len(arrays) + len(earlier)),
        out_specs=[VMEM] * len(arrays),
        out_shape=[jax.ShapeDtypeStruct((rows, *a.shape[1:]), a.dtype) for a in arrays],
        scratch_shapes=[pltpu.SemaphoreType.DMA((len(arrays),))],
        compiler_params=pltpu.CompilerParams(vmem_limit_bytes=24 * MIB),
        cost_estimate=pl.CostEstimate(flops=MICROSECOND, bytes_accessed=0, transcendentals=0),
    )(*arrays, *earlier)


def norm_kernel(x_ref, *refs):
    out_ref = refs[-1]
    x = high(x_ref[...])
    out_ref[...] = low(x * rows_rsqrt(x))


def norm_after(x, earlier):
    return call(
        norm_kernel,
        [x, *earlier],
        [VMEM] + [HBM] * len(earlier),
        jax.ShapeDtypeStruct(x.shape, jnp.bfloat16),
        [],
        4 * x.size,
        4 * x.size,
    )


def spread_kernel(up_ref, w_ref, out_ref, rows, sems):
    copies = [fetch(w_ref.at[k], rows.at[k], sems.at[k]) for k in range(HEADS)]
    for k in range(0, HEADS, 2):
        copies[k].wait()
        copies[k + 1].wait()
        pair = rows[k : k + 2].reshape(2 * HD, -1)
        g = low(dot(up_ref[...], pair, NT))
        out_ref[k] = g[:, :HD]
        out_ref[k + 1] = g[:, HD:]


def spread_grads(upstream, w_fin):
    tokens, width = upstream.shape
    return call(
        spread_kernel,
        [upstream, w_fin.reshape(HEADS, HD, width)],
        [VMEM, HBM],
        jax.ShapeDtypeStruct((HEADS, tokens, HD), jnp.bfloat16),
        [
            pltpu.VMEM((HEADS, HD, width), jnp.bfloat16),
            pltpu.SemaphoreType.DMA((HEADS,)),
        ],
        MICROSECOND * 3,
        2 * width * HEADS * HD,
    )


def finish_kernel(unread, info_ref, *refs):
    att_refs, refs = refs[:HEADS], refs[HEADS:]
    x_ref, w_ref, (out_ref, att) = refs[0], refs[1], refs[2 + unread :]
    flip = info_ref[0]
    for k in range(HEADS):
        att[flip ^ k] = att_refs[k][...]
    whole = jnp.concatenate([att[k] for k in range(HEADS)], axis=1)
    block = 256
    for start in range(0, x_ref.shape[1], block):
        columns = slice(start, start + block)
        out_ref[:, columns] = low(high(x_ref[:, columns]) + dot(whole, w_ref[:, columns], NN))


def finish(info, attention, current, w_fin, earlier):
    tokens, width = current.shape
    return call(
        functools.partial(finish_kernel, len(earlier)),
        [info, *attention, current, w_fin, *earlier],
        [SMEM] + [VMEM] * (HEADS + 2) + [HBM] * len(earlier),
        jax.ShapeDtypeStruct((tokens, width), jnp.bfloat16),
        [pltpu.VMEM((HEADS, tokens, HD), jnp.bfloat16)],
        MICROSECOND,
        2 * width * HEADS * HD,
    )


def finish_back_kernel(info_ref, *refs):
    grad_refs, (x_ref, up_ref, w_ref, out_ref, grads, total) = refs[:HEADS], refs[HEADS:]
    flip = info_ref[0]
    for k in range(HEADS):
        grads[flip ^ k] = grad_refs[k][...]
    for c in range(3):
        columns = slice(c * HD, (c + 1) * HD)
        block = jnp.concatenate([grads[k, :, columns] for k in range(HEADS)], axis=1)
        product = dot(block, w_ref[c * HEADS * HD : (c + 1) * HEADS * HD], NN)
        if c == 0:
            total[...] = product
        else:
            total[...] += product
    x = high(x_ref[...])
    scale = rows_rsqrt(x)
    unit = x * scale
    g = total[...]
    pulled = scale * (g - unit * jnp.mean(unit * g, axis=1, keepdims=True))
    out_ref[...] = low(high(up_ref[...]) + pulled)


def finish_back(info, grads, stored, upstream, w_qkv):
    tokens, width = stored.shape
    return call(
        finish_back_kernel,
        [info, *grads, stored, upstream, w_qkv],
        [SMEM] + [VMEM] * (HEADS + 3),
        jax.ShapeDtypeStruct((tokens, width), jnp.bfloat16),
        [
            pltpu.VMEM((HEADS, tokens, 3 * HD), jnp.bfloat16),
            pltpu.VMEM((tokens, width), jnp.float32),
        ],
        MICROSECOND * 3,
        6 * width * HEADS * HD,
    )


def partner(block, distance):
    route = [(i, i ^ distance) for i in range(lax.axis_size("seq"))]
    return lax.ppermute(block, "seq", route)


def gather_rows(x, earlier):
    half = x.shape[0] // 2
    if earlier:
        over_x, over_y = partner(x, 2), partner(x, 4)
        relay_top, relay_bottom = rows_after([over_x, over_y], [0, half], half, earlier)
        pieces = [(0, 0, x), (2, 0, over_x), (4, 0, over_y)]
    else:
        top, bottom = x[:half], x[half:]
        relay_top, relay_bottom = partner(top, 2), partner(bottom, 4)
        pieces = [(0, 0, x), (2, 0, relay_top), (4, half, relay_bottom)]
        pieces += [(2, half, partner(bottom, 2)), (4, 0, partner(top, 4))]
    far_top, far_bottom = partner(relay_top, 4), partner(relay_bottom, 2)
    pieces += [(6, 0, far_top), (6, half, far_bottom)]
    return pieces + [(k + 1, start, partner(block, 1)) for k, start, block in pieces]


def swap(blocks):
    moved = {k: partner(blocks[k], k) for k in (2, 4, 6, 3, 5, 7, 1)}
    return [blocks[0]] + [moved[k] for k in range(1, HEADS)]


def all_swap(blocks):
    return lax.all_to_all(blocks, "seq", split_axis=0, concat_axis=0, tiled=True)


def to_heads(blocks, own, spacing):
    heads, tokens, width = blocks.shape
    held = tokens // TILE
    places = spacing // held
    tiled = blocks.reshape(heads, 1, held, TILE, width)
    padded = jnp.zeros((heads, places, held, TILE, width), blocks.dtype)
    padded = lax.dynamic_update_slice_in_dim(padded, tiled, own % places, 1)
    arrived = all_swap(padded.reshape(heads * spacing, TILE, width))
    arrived = arrived.reshape(-1, places, TILE, width)
    mine = lax.dynamic_index_in_dim(arrived, own % spacing // held, 1, keepdims=False)
    return mine.reshape(HEADS, 2 * TILE, width)


def to_tokens(blocks, own, spacing, tokens):
    held = tokens // TILE
    places = spacing // held
    tiled = blocks.reshape(2 * HEADS, 1, TILE, -1)
    padded = jnp.zeros((2 * HEADS, places, TILE, tiled.shape[3]), tiled.dtype)
    padded = lax.dynamic_update_slice_in_dim(padded, tiled, own % spacing // held, 1)
    returned = all_swap(padded.reshape(-1, TILE, tiled.shape[3]))
    returned = returned.reshape(HEADS, places, held * TILE, tiled.shape[3])
    return lax.dynamic_index_in_dim(returned, own % places, 1, keepdims=False)


def passed_along(block, axis, distance):
    devices = range(lax.axis_size(axis))
    route = [(i - distance, i) for i in devices if i - distance in devices]
    return lax.ppermute(block, axis, route)


def per_device(section_input, saved_input, grad_output, w_qkv, w_out, tile_cluster):
    current, stored, upstream = section_input[0], saved_input[0], grad_output[0]
    w_rows, w_fin = w_qkv[0], w_out[0]
    tokens = current.shape[0]
    spacing = lax.axis_size("seq") // HEADS
    own = lax.axis_index("seq").astype(jnp.int32)
    if spacing == 1:
        info = jnp.stack([own, own, jnp.zeros_like(own)])
        gather, spread, collect = gather_rows, all_swap, swap
    else:
        info = jnp.stack([jnp.zeros_like(own), own // spacing, own % spacing])

        def gather(x, earlier):
            copies = jnp.broadcast_to(x, (HEADS, *x.shape))
            return [(k, 0, block) for k, block in enumerate(to_heads(copies, own, spacing))]

        def spread(blocks):
            return to_heads(blocks, own, spacing)

        def collect(blocks):
            return list(to_tokens(jnp.stack(blocks), own, spacing, tokens))

    own_head = w_rows.reshape(3, HEADS, HD, -1)
    own_head = lax.dynamic_index_in_dim(own_head, info[1], 1, keepdims=False)
    own_head = own_head.reshape(3 * HD, -1)
    spreading = spread_grads(upstream, w_fin)
    stored_pieces = gather(stored, [])
    grad_attention = spread(spreading)
    earlier = [block for k, _, block in stored_pieces if k == HEADS - 2]
    normed = norm_after(current, [*earlier, grad_attention])
    grads = head_work(
        info, tile_cluster, stored_pieces, own_head, spacing, grad_attention, [normed]
    )
    current_pieces = gather(normed, grads[:1])
    returned_grads = collect(grads)
    outputs = head_work(
        info, tile_cluster, current_pieces, own_head, spacing, earlier=grads[:1]
    )
    returned = collect(outputs)
    grad_self = finish_back(info, returned_grads, stored, upstream, w_rows)
    grad_input = passed_along(grad_self, "pipe", -1)
    result = finish(info, returned, current, w_fin, [grad_self])
    next_input = passed_along(result, "pipe", 1)
    return (next_input[None], grad_input[None])


def solution(mesh):
    return jax.shard_map(
        per_device,
        mesh=mesh,
        in_specs=(
            P("pipe", "seq", None),
            P("pipe", "seq", None),
            P("pipe", "seq", None),
            P("pipe", None, None),
            P("pipe", None, None),
            P(),
        ),
        out_specs=(P("pipe", "seq", None), P("pipe", "seq", None)),
        check_vma=False,
    )
```

```python
import functools

import jax
import jax.numpy as jnp
from jax import lax
from jax.experimental import pallas as pl
from jax.experimental.pallas import tpu as pltpu
from jax.sharding import PartitionSpec as P

HEADS = 8
HD = 128
TILE = 128
CAPACITY = 3
EPSILON = 1e-05
MIB = 1024 * 1024
MICROSECOND = 1150000000
NT = (((1,), (1,)), ((), ()))
NN = (((1,), (0,)), ((), ()))
TN = (((0,), (0,)), ((), ()))
HBM = pl.BlockSpec(memory_space=pl.ANY)
SMEM = pl.BlockSpec(memory_space=pltpu.SMEM)
VMEM = pl.BlockSpec(memory_space=pltpu.VMEM)


def dot(left, right, dims):
    return lax.dot_general(left, right, dims, preferred_element_type=jnp.float32)


def low(values):
    return values.astype(jnp.bfloat16)


def high(values):
    return values.astype(jnp.float32)


def rows_rsqrt(values):
    return lax.rsqrt(jnp.mean(values * values, axis=-1, keepdims=True) + EPSILON)


def call(kernel, operands, in_specs, out_shape, scratch, flops, moved, grant=24 * MIB):
    return pl.pallas_call(
        kernel,
        in_specs=in_specs,
        out_specs=[VMEM] * len(out_shape) if isinstance(out_shape, list) else VMEM,
        out_shape=out_shape,
        scratch_shapes=scratch,
        compiler_params=pltpu.CompilerParams(vmem_limit_bytes=grant),
        cost_estimate=pl.CostEstimate(flops=flops, bytes_accessed=moved, transcendentals=0),
    )(*operands)


def fetch(source, target, sem):
    copy = pltpu.make_async_copy(source, target, sem)
    copy.start()
    return copy


def forward_cluster(tiles, kept, out):
    def load(c):
        return jnp.concatenate([kept[t, :, c * HD : (c + 1) * HD] for t in tiles], axis=0)

    q, k, v = load(0), load(1), load(2)
    weights = low(jnp.exp(dot(q, k, NT) * (HD ** -0.5)))
    wide = jnp.concatenate([v, jnp.ones_like(v)], axis=1)
    sums = dot(weights, wide, NN)
    result = low(sums[:, :HD] / sums[:, HD:])
    for i, t in enumerate(tiles):
        out[t] = result[i * TILE : (i + 1) * TILE]


def backward_cluster(tiles, kept, out, scales, grads):
    def load(c):
        return jnp.concatenate([kept[t, :, c * HD : (c + 1) * HD] for t in tiles], axis=0)

    def scale(c):
        column = c * HD // 2
        return jnp.concatenate([scales[t, :, column : column + 1] for t in tiles], axis=0)

    q, k, v = load(0), load(1), load(2)
    g = jnp.concatenate([grads[t] for t in tiles], axis=0)
    factor = HD ** -0.5
    weights = jnp.exp(dot(k, q, NT) * factor)
    softmax = weights * (1.0 / jnp.sum(weights, axis=0, keepdims=True))
    soft_low = low(softmax)
    grad_soft = dot(v, g, NT)
    delta = jnp.sum(high(soft_low) * grad_soft, axis=0, keepdims=True)
    grad_scores = low(softmax * (grad_soft - delta))
    grad_values = low(dot(soft_low, g, NN))
    results = [grad_values]
    for c, unit, grad in (
        (1, k, dot(grad_scores, q, NN)),
        (0, q, dot(grad_scores, k, TN)),
    ):
        rounded = high(low(grad * factor))
        unit = high(unit)
        mean = jnp.mean(unit * rounded, axis=1, keepdims=True)
        results.append(low(scale(c) * (rounded - unit * mean)))
    for c, result in zip((2, 1, 0), results):
        for i, t in enumerate(tiles):
            out[t, :, c * HD : (c + 1) * HD] = result[i * TILE : (i + 1) * TILE]


def project_rows(back, flip, pieces, x_refs, w_ref, kept, scales):
    weights = w_ref[...]
    for (slot, start, rows), x_ref in zip(pieces, x_refs):
        normed = x_ref[...]
        if back:
            x = high(normed)
            normed = low(x * rows_rsqrt(x))
        mixed = dot(normed, weights, NT)
        q, k, v = (mixed[:, c * HD : (c + 1) * HD] for c in range(3))
        q_scale, k_scale = rows_rsqrt(q), rows_rsqrt(k)
        whole = low(jnp.concatenate([q * q_scale, k * k_scale, v], axis=1))
        if back:
            lane = lax.broadcasted_iota(jnp.int32, q.shape, 1)
            both = jnp.where(lane < HD // 2, q_scale, k_scale)
        place = 2 * (flip ^ slot) + start // TILE
        for j in range(rows // TILE):
            kept[place + j] = whole[j * TILE : (j + 1) * TILE]
            if back:
                scales[place + j] = both[j * TILE : (j + 1) * TILE]


def visit_clusters(cluster_ref, residue, spacing, count, member, body):
    clusters = count.shape[0]
    for c in range(clusters):
        count[c] = 0

    def enter(t, carry):
        c = cluster_ref[t * spacing + residue] // spacing
        place = count[c]
        member[c * CAPACITY + place] = t
        count[c] = place + 1
        return carry

    lax.fori_loop(0, 2 * clusters, enter, 0)

    def visit(c, carry):
        for n in range(1, CAPACITY + 1):

            @pl.when(count[c] == n)
            def _():
                body([member[c * CAPACITY + i] for i in range(n)])

        return carry

    lax.fori_loop(0, clusters, visit, 0)


def forward_kernel(pieces, unread, spacing, cluster_ref, info_ref, w_ref, *refs):
    x_refs, refs = refs[: len(pieces)], refs[len(pieces) + unread :]
    out_refs, (kept, out, count, member) = refs[:HEADS], refs[HEADS:]
    flip, residue = info_ref[0], info_ref[2]
    project_rows(False, flip, pieces, x_refs, w_ref, kept, None)
    visit_clusters(
        cluster_ref, residue, spacing, count, member, lambda held: forward_cluster(held, kept, out)
    )
    for k in range(HEADS):
        out_refs[k][...] = out[pl.ds(2 * (flip ^ k), 2)].reshape(out_refs[k].shape)


def project_kernel(pieces, unread, info_ref, w_ref, *refs):
    x_refs, (kept, scales) = refs[: len(pieces)], refs[len(pieces) + unread :]
    project_rows(True, info_ref[0], pieces, x_refs, w_ref, kept, scales)


def backward_kernel(spacing, cluster_ref, info_ref, kept, scales, grads, out, count, member):
    visit_clusters(
        cluster_ref,
        info_ref[2],
        spacing,
        count,
        member,
        lambda held: backward_cluster(held, kept, out, scales, grads),
    )


def tables(tiles):
    return [
        pltpu.SMEM((tiles // 2,), jnp.int32),
        pltpu.SMEM((tiles // 2 * CAPACITY,), jnp.int32),
    ]


def head_forward(info, tile_cluster, pieces, weights, spacing, earlier):
    width = weights.shape[1]
    tiles = 2 * HEADS
    arrays = [array for _, _, array in pieces]
    shapes = tuple((k, start, array.shape[0]) for k, start, array in pieces)
    return call(
        functools.partial(forward_kernel, shapes, len(earlier), spacing),
        [tile_cluster, info, weights, *arrays, *earlier],
        [SMEM, SMEM] + [VMEM] * (1 + len(arrays)) + [HBM] * len(earlier),
        [jax.ShapeDtypeStruct((2 * TILE, HD), jnp.bfloat16) for _ in range(HEADS)],
        [
            pltpu.VMEM((tiles, TILE, 3 * HD), jnp.bfloat16),
            pltpu.VMEM((tiles, TILE, HD), jnp.bfloat16),
            *tables(tiles),
        ],
        MICROSECOND * 8,
        2 * tiles * TILE * width,
    )


def head_project(info, pieces, weights, earlier):
    width = weights.shape[1]
    tiles = 2 * HEADS
    arrays = [array for _, _, array in pieces]
    shapes = tuple((k, start, array.shape[0]) for k, start, array in pieces)
    return call(
        functools.partial(project_kernel, shapes, len(earlier)),
        [info, weights, *arrays, *earlier],
        [SMEM] + [VMEM] * (1 + len(arrays)) + [HBM] * len(earlier),
        [
            jax.ShapeDtypeStruct((tiles, TILE, 3 * HD), jnp.bfloat16),
            jax.ShapeDtypeStruct((tiles, TILE, HD), jnp.float32),
        ],
        [],
        MICROSECOND * 5,
        2 * tiles * TILE * width,
    )


def head_backward(info, tile_cluster, kept, scales, grads, spacing):
    tiles = kept.shape[0]
    out = call(
        functools.partial(backward_kernel, spacing),
        [tile_cluster, info, kept, scales, grads.reshape(tiles, TILE, HD)],
        [SMEM, SMEM] + [VMEM] * 3,
        jax.ShapeDtypeStruct((tiles, TILE, 3 * HD), jnp.bfloat16),
        tables(tiles),
        MICROSECOND * 7,
        2 * tiles * TILE * 8 * HD,
    )
    return out.reshape(HEADS, 2 * TILE, 3 * HD)


def copy_kernel(starts, *refs):
    count = len(starts)
    outs, sems = refs[-count - 1 : -1], refs[-1]
    copies = [
        fetch(refs[i].at[pl.ds(start, outs[i].shape[0])], outs[i], sems.at[i])
        for i, start in enumerate(starts)
    ]
    for copy in copies:
        copy.wait()


def rows_after(arrays, starts, rows, earlier):
    return pl.pallas_call(
        functools.partial(copy_kernel, starts),
        in_specs=[HBM] * (len(arrays) + len(earlier)),
        out_specs=[VMEM] * len(arrays),
        out_shape=[jax.ShapeDtypeStruct((rows, *a.shape[1:]), a.dtype) for a in arrays],
        scratch_shapes=[pltpu.SemaphoreType.DMA((len(arrays),))],
        compiler_params=pltpu.CompilerParams(vmem_limit_bytes=24 * MIB),
        cost_estimate=pl.CostEstimate(flops=MICROSECOND, bytes_accessed=0, transcendentals=0),
    )(*arrays, *earlier)


def norm_kernel(x_ref, *refs):
    out_ref = refs[-1]
    x = high(x_ref[...])
    out_ref[...] = low(x * rows_rsqrt(x))


def norm_after(x, earlier):
    return call(
        norm_kernel,
        [x, *earlier],
        [VMEM] + [HBM] * len(earlier),
        jax.ShapeDtypeStruct(x.shape, jnp.bfloat16),
        [],
        4 * x.size,
        4 * x.size,
    )


def spread_kernel(up_ref, w_ref, out_ref, rows, sems):
    copies = [fetch(w_ref.at[k], rows.at[k], sems.at[k]) for k in range(HEADS)]
    for k in range(0, HEADS, 2):
        copies[k].wait()
        copies[k + 1].wait()
        pair = rows[k : k + 2].reshape(2 * HD, -1)
        g = low(dot(up_ref[...], pair, NT))
        out_ref[k] = g[:, :HD]
        out_ref[k + 1] = g[:, HD:]


def spread_grads(upstream, w_fin):
    tokens, width = upstream.shape
    return call(
        spread_kernel,
        [upstream, w_fin.reshape(HEADS, HD, width)],
        [VMEM, HBM],
        jax.ShapeDtypeStruct((HEADS, tokens, HD), jnp.bfloat16),
        [
            pltpu.VMEM((HEADS, HD, width), jnp.bfloat16),
            pltpu.SemaphoreType.DMA((HEADS,)),
        ],
        MICROSECOND * 3,
        2 * width * HEADS * HD,
    )


def finish_kernel(unread, info_ref, *refs):
    att_refs, refs = refs[:HEADS], refs[HEADS:]
    x_ref, w_ref, (out_ref, att) = refs[0], refs[1], refs[2 + unread :]
    flip = info_ref[0]
    for k in range(HEADS):
        att[flip ^ k] = att_refs[k][...]
    whole = jnp.concatenate([att[k] for k in range(HEADS)], axis=1)
    block = 256
    for start in range(0, x_ref.shape[1], block):
        columns = slice(start, start + block)
        out_ref[:, columns] = low(high(x_ref[:, columns]) + dot(whole, w_ref[:, columns], NN))


def finish(info, attention, current, w_fin, earlier):
    tokens, width = current.shape
    return call(
        functools.partial(finish_kernel, len(earlier)),
        [info, *attention, current, w_fin, *earlier],
        [SMEM] + [VMEM] * (HEADS + 2) + [HBM] * len(earlier),
        jax.ShapeDtypeStruct((tokens, width), jnp.bfloat16),
        [pltpu.VMEM((HEADS, tokens, HD), jnp.bfloat16)],
        MICROSECOND,
        2 * width * HEADS * HD,
    )


def finish_back_kernel(grad_ref, x_ref, up_ref, w_ref, out_ref, grads, x, up, rows, total, sems):
    chunks = rows.shape[0]
    depth = rows.shape[1]
    held = depth // HD
    copies = [fetch(grad_ref, grads, sems.at[0])]
    copies += [
        fetch(w_ref.at[pl.ds(i * depth, depth)], rows.at[i], sems.at[1 + i]) for i in range(chunks)
    ]
    copies.append(fetch(x_ref, x, sems.at[1 + chunks]))
    copies.append(fetch(up_ref, up, sems.at[2 + chunks]))
    copies[0].wait()
    for i in range(chunks):
        c, first = i * held // HEADS, i * held % HEADS
        columns = slice(c * HD, (c + 1) * HD)
        block = jnp.concatenate([grads[first + j, :, columns] for j in range(held)], axis=1)
        copies[1 + i].wait()
        product = dot(block, rows[i], NN)
        if i == 0:
            total[...] = product
        else:
            total[...] += product
    copies[1 + chunks].wait()
    copies[2 + chunks].wait()
    stored = high(x[...])
    scale = rows_rsqrt(stored)
    unit = stored * scale
    g = total[...]
    pulled = scale * (g - unit * jnp.mean(unit * g, axis=1, keepdims=True))
    out_ref[...] = low(high(up[...]) + pulled)


def finish_back(grads, stored, upstream, w_qkv):
    tokens, width = stored.shape
    chunks = 6
    return call(
        finish_back_kernel,
        [grads, stored, upstream, w_qkv],
        [HBM] * 4,
        jax.ShapeDtypeStruct((tokens, width), jnp.bfloat16),
        [
            pltpu.VMEM(grads.shape, jnp.bfloat16),
            pltpu.VMEM((tokens, width), jnp.bfloat16),
            pltpu.VMEM((tokens, width), jnp.bfloat16),
            pltpu.VMEM((chunks, w_qkv.shape[0] // chunks, width), jnp.bfloat16),
            pltpu.VMEM((tokens, width), jnp.float32),
            pltpu.SemaphoreType.DMA((chunks + 3,)),
        ],
        MICROSECOND * 5,
        6 * width * HEADS * HD,
        grant=58 * MIB,
    )


def partner(block, distance):
    route = [(i, i ^ distance) for i in range(lax.axis_size("seq"))]
    return lax.ppermute(block, "seq", route)


def gather_rows(x, top_after, bottom_after):
    half = x.shape[0] // 2
    top, bottom = x[:half], x[half:]
    relay_top, relay_bottom = partner(top, 2), partner(bottom, 4)
    pieces = [(0, 0, x), (2, 0, relay_top), (4, half, relay_bottom)]
    pieces += [(2, half, partner(bottom, 2)), (4, 0, partner(top, 4))]
    if top_after:
        relay_top, relay_bottom = rows_after([relay_top, relay_bottom], [0, 0], half, top_after)
    else:
        relay_bottom = rows_after([relay_bottom], [0], half, bottom_after)[0]
    far_top, far_bottom = partner(relay_top, 4), partner(relay_bottom, 2)
    pieces += [(6, 0, far_top), (6, half, far_bottom)]
    return pieces + [(k + 1, start, partner(block, 1)) for k, start, block in pieces]


def swap(blocks):
    moved = {k: partner(blocks[k], k) for k in (2, 4, 6, 3, 5, 7, 1)}
    return [blocks[0]] + [moved[k] for k in range(1, HEADS)]


def all_swap(blocks):
    return lax.all_to_all(blocks, "seq", split_axis=0, concat_axis=0, tiled=True)


def to_heads(blocks, own, spacing):
    heads, tokens, width = blocks.shape
    held = tokens // TILE
    places = spacing // held
    tiled = blocks.reshape(heads, 1, held, TILE, width)
    padded = jnp.zeros((heads, places, held, TILE, width), blocks.dtype)
    padded = lax.dynamic_update_slice_in_dim(padded, tiled, own % places, 1)
    arrived = all_swap(padded.reshape(heads * spacing, TILE, width))
    arrived = arrived.reshape(-1, places, TILE, width)
    mine = lax.dynamic_index_in_dim(arrived, own % spacing // held, 1, keepdims=False)
    return mine.reshape(HEADS, 2 * TILE, width)


def to_tokens(blocks, own, spacing, tokens):
    held = tokens // TILE
    places = spacing // held
    tiled = blocks.reshape(2 * HEADS, 1, TILE, -1)
    padded = jnp.zeros((2 * HEADS, places, TILE, tiled.shape[3]), tiled.dtype)
    padded = lax.dynamic_update_slice_in_dim(padded, tiled, own % spacing // held, 1)
    returned = all_swap(padded.reshape(-1, TILE, tiled.shape[3]))
    returned = returned.reshape(HEADS, places, held * TILE, tiled.shape[3])
    return lax.dynamic_index_in_dim(returned, own % places, 1, keepdims=False)


def passed_along(block, axis, distance):
    devices = range(lax.axis_size(axis))
    route = [(i - distance, i) for i in devices if i - distance in devices]
    return lax.ppermute(block, axis, route)


def per_device(section_input, saved_input, grad_output, w_qkv, w_out, tile_cluster):
    current, stored, upstream = section_input[0], saved_input[0], grad_output[0]
    w_rows, w_fin = w_qkv[0], w_out[0]
    tokens = current.shape[0]
    spacing = lax.axis_size("seq") // HEADS
    own = lax.axis_index("seq").astype(jnp.int32)
    if spacing == 1:
        info = jnp.stack([own, own, jnp.zeros_like(own)])
        gather, spread, collect, collect_grads = gather_rows, all_swap, swap, all_swap
    else:
        info = jnp.stack([jnp.zeros_like(own), own // spacing, own % spacing])

        def gather(x, top_after, bottom_after):
            copies = jnp.broadcast_to(x, (HEADS, *x.shape))
            return [(k, 0, block) for k, block in enumerate(to_heads(copies, own, spacing))]

        def spread(blocks):
            return to_heads(blocks, own, spacing)

        def collect(blocks):
            return list(to_tokens(jnp.stack(blocks), own, spacing, tokens))

        def collect_grads(blocks):
            return to_tokens(blocks, own, spacing, tokens)

    own_head = w_rows.reshape(3, HEADS, HD, -1)
    own_head = lax.dynamic_index_in_dim(own_head, info[1], 1, keepdims=False)
    own_head = own_head.reshape(3 * HD, -1)
    grad_attention = spread(spread_grads(upstream, w_fin))
    stored_pieces = gather(stored, [], [grad_attention])
    earlier = [block for k, _, block in stored_pieces if k == HEADS - 2]
    normed = norm_after(current, [*earlier, grad_attention])
    kept, scales = head_project(info, stored_pieces, own_head, [normed])
    current_pieces = gather(normed, [scales], [])
    grads = head_backward(info, tile_cluster, kept, scales, grad_attention, spacing)
    returned_grads = collect_grads(grads)
    outputs = head_forward(info, tile_cluster, current_pieces, own_head, spacing, [grads])
    returned = collect(outputs)
    grad_self = finish_back(returned_grads, stored, upstream, w_rows)
    grad_input = passed_along(grad_self, "pipe", -1)
    result = finish(info, returned, current, w_fin, [grad_self])
    next_input = passed_along(result, "pipe", 1)
    return (next_input[None], grad_input[None])


def solution(mesh):
    return jax.shard_map(
        per_device,
        mesh=mesh,
        in_specs=(
            P("pipe", "seq", None),
            P("pipe", "seq", None),
            P("pipe", "seq", None),
            P("pipe", None, None),
            P("pipe", None, None),
            P(),
        ),
        out_specs=(P("pipe", "seq", None), P("pipe", "seq", None)),
        check_vma=False,
    )
```

```python
import functools

import jax
import jax.numpy as jnp
from jax import lax
from jax.experimental import pallas as pl
from jax.experimental.pallas import tpu as pltpu
from jax.sharding import PartitionSpec as P

HEADS = 8
HD = 128
TILE = 128
CAPACITY = 3
EPSILON = 1e-05
MIB = 1024 * 1024
MICROSECOND = 1150000000
NT = (((1,), (1,)), ((), ()))
NN = (((1,), (0,)), ((), ()))
TN = (((0,), (0,)), ((), ()))
HBM = pl.BlockSpec(memory_space=pl.ANY)
SMEM = pl.BlockSpec(memory_space=pltpu.SMEM)
VMEM = pl.BlockSpec(memory_space=pltpu.VMEM)


def dot(left, right, dims):
    return lax.dot_general(left, right, dims, preferred_element_type=jnp.float32)


def low(values):
    return values.astype(jnp.bfloat16)


def high(values):
    return values.astype(jnp.float32)


def rows_rsqrt(values):
    return lax.rsqrt(jnp.mean(values * values, axis=-1, keepdims=True) + EPSILON)


def call(kernel, operands, in_specs, out_shape, scratch, flops, moved, grant=24 * MIB):
    return pl.pallas_call(
        kernel,
        in_specs=in_specs,
        out_specs=[VMEM] * len(out_shape) if isinstance(out_shape, list) else VMEM,
        out_shape=out_shape,
        scratch_shapes=scratch,
        compiler_params=pltpu.CompilerParams(vmem_limit_bytes=grant),
        cost_estimate=pl.CostEstimate(flops=flops, bytes_accessed=moved, transcendentals=0),
    )(*operands)


def fetch(source, target, sem):
    copy = pltpu.make_async_copy(source, target, sem)
    copy.start()
    return copy


def forward_cluster(tiles, kept, out):
    def load(c):
        return jnp.concatenate([kept[t, :, c * HD : (c + 1) * HD] for t in tiles], axis=0)

    q, k, v = load(0), load(1), load(2)
    weights = low(jnp.exp(dot(q, k, NT) * (HD ** -0.5)))
    wide = jnp.concatenate([v, jnp.ones_like(v)], axis=1)
    sums = dot(weights, wide, NN)
    result = low(sums[:, :HD] / sums[:, HD:])
    for i, t in enumerate(tiles):
        out[t] = result[i * TILE : (i + 1) * TILE]


def backward_cluster(tiles, kept, out, scales, grads):
    def load(c):
        return jnp.concatenate([kept[t, :, c * HD : (c + 1) * HD] for t in tiles], axis=0)

    def scale(c):
        return jnp.concatenate([scales[t, :, c * HD : (c + 1) * HD] for t in tiles], axis=0)

    q, k, v = load(0), load(1), load(2)
    g = jnp.concatenate([grads[t] for t in tiles], axis=0)
    factor = HD ** -0.5
    weights = jnp.exp(dot(k, q, NT) * factor)
    softmax = weights * (1.0 / jnp.sum(weights, axis=0, keepdims=True))
    soft_low = low(softmax)
    grad_soft = dot(v, g, NT)
    delta = jnp.sum(high(soft_low) * grad_soft, axis=0, keepdims=True)
    grad_scores = low(softmax * (grad_soft - delta))
    grad_values = low(dot(soft_low, g, NN))
    results = [grad_values]
    for c, unit, grad in (
        (1, k, dot(grad_scores, q, NN)),
        (0, q, dot(grad_scores, k, TN)),
    ):
        rounded = high(low(grad * factor))
        unit = high(unit)
        mean = jnp.mean(unit * rounded, axis=1, keepdims=True)
        results.append(low(scale(c) * (rounded - unit * mean)))
    for c, result in zip((2, 1, 0), results):
        for i, t in enumerate(tiles):
            half = pl.ds(t % 2 * TILE, TILE)
            out[t // 2, half, c * HD : (c + 1) * HD] = result[i * TILE : (i + 1) * TILE]


def head_kernel(back, unread, pieces, spacing, *refs):
    cluster_ref, info_ref, w_ref = refs[:3]
    x_refs = refs[3 : 3 + len(pieces)]
    refs = refs[3 + len(pieces) :]
    if back:
        grads, refs = refs[0], refs[1:]
    refs = refs[unread:]
    if back:
        out, kept, count, member, scales = refs
    else:
        out_refs, (kept, count, member, out) = refs[:HEADS], refs[HEADS:]
    flip, residue = info_ref[0], info_ref[2]
    tiles = kept.shape[0]
    clusters = count.shape[0]
    for c in range(clusters):
        count[c] = 0

    def enter(t, carry):
        c = cluster_ref[t * spacing + residue] // spacing
        place = count[c]
        member[c * CAPACITY + place] = t
        count[c] = place + 1
        return carry

    lax.fori_loop(0, tiles, enter, 0)

    weights = w_ref[...]
    for (slot, start, rows), x_ref in zip(pieces, x_refs):
        normed = x_ref[...]
        if back:
            x = high(normed)
            normed = low(x * rows_rsqrt(x))
        mixed = dot(normed, weights, NT)
        place = 2 * (flip ^ slot) + start // TILE
        for c in range(3):
            u = mixed[:, c * HD : (c + 1) * HD]
            if c < 2:
                scale = rows_rsqrt(u)
                u = u * scale
            for j in range(rows // TILE):
                kept[place + j, :, c * HD : (c + 1) * HD] = low(u[j * TILE : (j + 1) * TILE])
                if back and c < 2:
                    scales[place + j, :, c * HD : (c + 1) * HD] = jnp.broadcast_to(
                        scale[j * TILE : (j + 1) * TILE], (TILE, HD)
                    )

    def visit(c, carry):
        for n in range(1, CAPACITY + 1):

            @pl.when(count[c] == n)
            def _():
                held = [member[c * CAPACITY + i] for i in range(n)]
                if back:
                    backward_cluster(held, kept, out, scales, grads)
                else:
                    forward_cluster(held, kept, out)

        return carry

    lax.fori_loop(0, clusters, visit, 0)
    if not back:
        for k in range(HEADS):
            out_refs[k][...] = out[pl.ds(2 * (flip ^ k), 2)].reshape(out_refs[k].shape)


def head_work(info, tile_cluster, pieces, weights, spacing, grads=None, earlier=()):
    back = grads is not None
    width = weights.shape[1]
    tiles = 2 * HEADS
    wide = 3 * HD if back else HD
    tokens = tiles * TILE
    operands = [tile_cluster, info, weights] + [array for _, _, array in pieces]
    if back:
        operands.append(grads.reshape(tiles, TILE, HD))
    scratch = [
        pltpu.VMEM((tiles, TILE, 3 * HD), jnp.bfloat16),
        pltpu.SMEM((tiles // 2,), jnp.int32),
        pltpu.SMEM((tiles // 2 * CAPACITY,), jnp.int32),
    ]
    if back:
        scratch.append(pltpu.VMEM((tiles, TILE, 2 * HD), jnp.float32))
        shape = jax.ShapeDtypeStruct((HEADS, 2 * TILE, wide), jnp.bfloat16)
    else:
        scratch.append(pltpu.VMEM((tiles, TILE, HD), jnp.bfloat16))
        shape = [jax.ShapeDtypeStruct((2 * TILE, HD), jnp.bfloat16) for _ in range(HEADS)]
    shapes = tuple((k, start, array.shape[0]) for k, start, array in pieces)
    return call(
        functools.partial(head_kernel, back, len(earlier), shapes, spacing),
        operands + list(earlier),
        [SMEM, SMEM] + [VMEM] * (len(operands) - 2) + [HBM] * len(earlier),
        shape,
        scratch,
        MICROSECOND * (12 if back else 8),
        2 * tokens * (width + 2 * wide),
    )

def copy_kernel(starts, *refs):
    count = len(starts)
    outs, sems = refs[-count - 1 : -1], refs[-1]
    copies = [
        fetch(refs[i].at[pl.ds(start, outs[i].shape[0])], outs[i], sems.at[i])
        for i, start in enumerate(starts)
    ]
    for copy in copies:
        copy.wait()


def rows_after(arrays, starts, rows, earlier):
    return pl.pallas_call(
        functools.partial(copy_kernel, starts),
        in_specs=[HBM] * (len(arrays) + len(earlier)),
        out_specs=[VMEM] * len(arrays),
        out_shape=[jax.ShapeDtypeStruct((rows, *a.shape[1:]), a.dtype) for a in arrays],
        scratch_shapes=[pltpu.SemaphoreType.DMA((len(arrays),))],
        compiler_params=pltpu.CompilerParams(vmem_limit_bytes=24 * MIB),
        cost_estimate=pl.CostEstimate(flops=MICROSECOND, bytes_accessed=0, transcendentals=0),
    )(*arrays, *earlier)


def norm_kernel(x_ref, *refs):
    out_ref = refs[-1]
    x = high(x_ref[...])
    out_ref[...] = low(x * rows_rsqrt(x))


def norm_after(x, earlier):
    return call(
        norm_kernel,
        [x, *earlier],
        [VMEM] + [HBM] * len(earlier),
        jax.ShapeDtypeStruct(x.shape, jnp.bfloat16),
        [],
        MICROSECOND * 10,
        4 * x.size,
    )


def spread_kernel(up_ref, w_ref, out_ref, rows, sems):
    copies = [fetch(w_ref.at[k], rows.at[k], sems.at[k]) for k in range(HEADS)]
    for k in range(0, HEADS, 2):
        copies[k].wait()
        copies[k + 1].wait()
        pair = rows[k : k + 2].reshape(2 * HD, -1)
        g = low(dot(up_ref[...], pair, NT))
        out_ref[k] = g[:, :HD]
        out_ref[k + 1] = g[:, HD:]


def spread_grads(upstream, w_fin):
    tokens, width = upstream.shape
    return call(
        spread_kernel,
        [upstream, w_fin.reshape(HEADS, HD, width)],
        [VMEM, HBM],
        jax.ShapeDtypeStruct((HEADS, tokens, HD), jnp.bfloat16),
        [
            pltpu.VMEM((HEADS, HD, width), jnp.bfloat16),
            pltpu.SemaphoreType.DMA((HEADS,)),
        ],
        MICROSECOND * 3,
        2 * width * HEADS * HD,
    )


def finish_kernel(info_ref, *refs):
    att_refs, (x_ref, w_ref, _, out_ref) = refs[:HEADS], refs[HEADS:]
    flip = info_ref[0]
    att = jnp.concatenate([ref[...] for ref in att_refs], axis=1)
    block = 256
    for start in range(0, x_ref.shape[1], block):
        columns = slice(start, start + block)
        w = jnp.concatenate([w_ref[flip ^ k, :, columns] for k in range(HEADS)], axis=0)
        out_ref[:, columns] = low(high(x_ref[:, columns]) + dot(att, w, NN))


def finish(info, attention, current, w_fin, earlier):
    tokens, width = current.shape
    return call(
        finish_kernel,
        [info, *attention, current, w_fin.reshape(HEADS, HD, width), earlier],
        [SMEM] + [VMEM] * (HEADS + 2) + [HBM],
        jax.ShapeDtypeStruct((tokens, width), jnp.bfloat16),
        [],
        2 * tokens * width * HEADS * HD,
        2 * width * HEADS * HD,
    )


def finish_back_kernel(grad_ref, x_ref, up_ref, w_ref, out_ref, grads, x, up, rows, total, sems):
    chunks = rows.shape[0]
    depth = rows.shape[1]
    held = depth // HD
    copies = [fetch(grad_ref, grads, sems.at[0])]
    copies += [
        fetch(w_ref.at[pl.ds(i * depth, depth)], rows.at[i], sems.at[1 + i]) for i in range(chunks)
    ]
    copies.append(fetch(x_ref, x, sems.at[1 + chunks]))
    copies.append(fetch(up_ref, up, sems.at[2 + chunks]))
    copies[0].wait()
    for i in range(chunks):
        c, first = i * held // HEADS, i * held % HEADS
        columns = slice(c * HD, (c + 1) * HD)
        block = jnp.concatenate([grads[first + j, :, columns] for j in range(held)], axis=1)
        copies[1 + i].wait()
        product = dot(block, rows[i], NN)
        if i == 0:
            total[...] = product
        else:
            total[...] += product
    copies[1 + chunks].wait()
    copies[2 + chunks].wait()
    stored = high(x[...])
    scale = rows_rsqrt(stored)
    unit = stored * scale
    g = total[...]
    pulled = scale * (g - unit * jnp.mean(unit * g, axis=1, keepdims=True))
    out_ref[...] = low(high(up[...]) + pulled)


def finish_back(grads, stored, upstream, w_qkv):
    tokens, width = stored.shape
    chunks = 6
    return call(
        finish_back_kernel,
        [grads, stored, upstream, w_qkv],
        [HBM] * 4,
        jax.ShapeDtypeStruct((tokens, width), jnp.bfloat16),
        [
            pltpu.VMEM(grads.shape, jnp.bfloat16),
            pltpu.VMEM((tokens, width), jnp.bfloat16),
            pltpu.VMEM((tokens, width), jnp.bfloat16),
            pltpu.VMEM((chunks, w_qkv.shape[0] // chunks, width), jnp.bfloat16),
            pltpu.VMEM((tokens, width), jnp.float32),
            pltpu.SemaphoreType.DMA((chunks + 3,)),
        ],
        MICROSECOND * 5,
        6 * width * HEADS * HD,
        grant=58 * MIB,
    )


def partner(block, distance):
    route = [(i, i ^ distance) for i in range(lax.axis_size("seq"))]
    return lax.ppermute(block, "seq", route)


def gather_rows(x, earlier):
    half = x.shape[0] // 2
    over_x, over_y = partner(x, 2), partner(x, 4)
    relay_top, relay_bottom = rows_after([over_x, over_y], [0, half], half, earlier)
    far_top, far_bottom = partner(relay_top, 4), partner(relay_bottom, 2)
    pieces = [(0, 0, x), (2, 0, over_x), (4, 0, over_y), (6, 0, far_top), (6, half, far_bottom)]
    return pieces + [(k + 1, start, partner(block, 1)) for k, start, block in pieces]


def swap(blocks):
    moved = {k: partner(blocks[k], k) for k in (2, 4, 6, 3, 5, 7, 1)}
    return [blocks[0]] + [moved[k] for k in range(1, HEADS)]


def all_swap(blocks):
    return lax.all_to_all(blocks, "seq", split_axis=0, concat_axis=0, tiled=True)


def to_heads(blocks, own, spacing):
    heads, tokens, width = blocks.shape
    held = tokens // TILE
    places = spacing // held
    tiled = blocks.reshape(heads, 1, held, TILE, width)
    padded = jnp.zeros((heads, places, held, TILE, width), blocks.dtype)
    padded = lax.dynamic_update_slice_in_dim(padded, tiled, own % places, 1)
    arrived = all_swap(padded.reshape(heads * spacing, TILE, width))
    arrived = arrived.reshape(-1, places, TILE, width)
    mine = lax.dynamic_index_in_dim(arrived, own % spacing // held, 1, keepdims=False)
    return mine.reshape(HEADS, 2 * TILE, width)


def to_tokens(blocks, own, spacing, tokens):
    held = tokens // TILE
    places = spacing // held
    tiled = blocks.reshape(2 * HEADS, 1, TILE, -1)
    padded = jnp.zeros((2 * HEADS, places, TILE, tiled.shape[3]), tiled.dtype)
    padded = lax.dynamic_update_slice_in_dim(padded, tiled, own % spacing // held, 1)
    returned = all_swap(padded.reshape(-1, TILE, tiled.shape[3]))
    returned = returned.reshape(HEADS, places, held * TILE, tiled.shape[3])
    return lax.dynamic_index_in_dim(returned, own % places, 1, keepdims=False)


def passed_along(block, axis, distance):
    devices = range(lax.axis_size(axis))
    route = [(i - distance, i) for i in devices if i - distance in devices]
    return lax.ppermute(block, axis, route)


def per_device(section_input, saved_input, grad_output, w_qkv, w_out, tile_cluster):
    current, stored, upstream = section_input[0], saved_input[0], grad_output[0]
    w_rows, w_fin = w_qkv[0], w_out[0]
    tokens = current.shape[0]
    spacing = lax.axis_size("seq") // HEADS
    own = lax.axis_index("seq").astype(jnp.int32)
    if spacing == 1:
        info = jnp.stack([own, own, jnp.zeros_like(own)])
        gather, spread, collect, collect_each = gather_rows, all_swap, all_swap, swap
    else:
        info = jnp.stack([jnp.zeros_like(own), own // spacing, own % spacing])

        def gather(x, earlier):
            copies = jnp.broadcast_to(x, (HEADS, *x.shape))
            return [(k, 0, block) for k, block in enumerate(to_heads(copies, own, spacing))]

        def spread(blocks):
            return to_heads(blocks, own, spacing)

        def collect(blocks):
            return to_tokens(blocks, own, spacing, tokens)

        def collect_each(blocks):
            return list(collect(jnp.stack(blocks)))

    own_head = w_rows.reshape(3, HEADS, HD, -1)
    own_head = lax.dynamic_index_in_dim(own_head, info[1], 1, keepdims=False)
    own_head = own_head.reshape(3 * HD, -1)
    spreading = spread_grads(upstream, w_fin)
    stored_pieces = gather(stored, [spreading])
    grad_attention = spread(spreading)
    earlier = [block for k, _, block in stored_pieces if k == HEADS - 2]
    normed = norm_after(current, [*earlier, grad_attention])
    grads = head_work(
        info, tile_cluster, stored_pieces, own_head, spacing, grad_attention, [normed]
    )
    current_pieces = gather(normed, [grads])
    returned_grads = collect(grads)
    outputs = head_work(
        info, tile_cluster, current_pieces, own_head, spacing, earlier=[grads]
    )
    returned = collect_each(outputs)
    grad_self = finish_back(returned_grads, stored, upstream, w_rows)
    grad_input = passed_along(grad_self, "pipe", -1)
    result = finish(info, returned, current, w_fin, grad_self)
    next_input = passed_along(result, "pipe", 1)
    return (next_input[None], grad_input[None])


def solution(mesh):
    return jax.shard_map(
        per_device,
        mesh=mesh,
        in_specs=(
            P("pipe", "seq", None),
            P("pipe", "seq", None),
            P("pipe", "seq", None),
            P("pipe", None, None),
            P("pipe", None, None),
            P(),
        ),
        out_specs=(P("pipe", "seq", None), P("pipe", "seq", None)),
        check_vma=False,
    )
```

```python
import functools

import jax
import jax.numpy as jnp
from jax import lax
from jax.experimental import pallas as pl
from jax.experimental.pallas import tpu as pltpu
from jax.sharding import PartitionSpec as P

HEADS = 8
HD = 128
TILE = 128
CAPACITY = 3
EPSILON = 1e-05
MIB = 1024 * 1024
MICROSECOND = 1150000000
NT = (((1,), (1,)), ((), ()))
NN = (((1,), (0,)), ((), ()))
TN = (((0,), (0,)), ((), ()))
HBM = pl.BlockSpec(memory_space=pl.ANY)
SMEM = pl.BlockSpec(memory_space=pltpu.SMEM)
VMEM = pl.BlockSpec(memory_space=pltpu.VMEM)


def dot(left, right, dims):
    return lax.dot_general(left, right, dims, preferred_element_type=jnp.float32)


def low(values):
    return values.astype(jnp.bfloat16)


def high(values):
    return values.astype(jnp.float32)


def rows_rsqrt(values):
    return lax.rsqrt(jnp.mean(values * values, axis=-1, keepdims=True) + EPSILON)


def call(kernel, operands, in_specs, out_shape, scratch, flops, moved, grant=24 * MIB):
    return pl.pallas_call(
        kernel,
        in_specs=in_specs,
        out_specs=[VMEM] * len(out_shape) if isinstance(out_shape, list) else VMEM,
        out_shape=out_shape,
        scratch_shapes=scratch,
        compiler_params=pltpu.CompilerParams(vmem_limit_bytes=grant),
        cost_estimate=pl.CostEstimate(flops=flops, bytes_accessed=moved, transcendentals=0),
    )(*operands)


def fetch(source, target, sem):
    copy = pltpu.make_async_copy(source, target, sem)
    copy.start()
    return copy


def forward_cluster(tiles, kept, out):
    def load(c):
        return jnp.concatenate([kept[t, :, c * HD : (c + 1) * HD] for t in tiles], axis=0)

    q, k, v = load(0), load(1), load(2)
    weights = low(jnp.exp(dot(q, k, NT) * (HD ** -0.5)))
    wide = jnp.concatenate([v, jnp.ones_like(v)], axis=1)
    sums = dot(weights, wide, NN)
    result = low(sums[:, :HD] / sums[:, HD:])
    for i, t in enumerate(tiles):
        out[t] = result[i * TILE : (i + 1) * TILE]


def backward_cluster(tiles, kept, out, scales, grads):
    def load(c):
        return jnp.concatenate([kept[t, :, c * HD : (c + 1) * HD] for t in tiles], axis=0)

    def scale(c):
        return jnp.concatenate([scales[t, :, c * HD : (c + 1) * HD] for t in tiles], axis=0)

    q, k, v = load(0), load(1), load(2)
    g = jnp.concatenate([grads[t] for t in tiles], axis=0)
    factor = HD ** -0.5
    weights = jnp.exp(dot(k, q, NT) * factor)
    softmax = weights * (1.0 / jnp.sum(weights, axis=0, keepdims=True))
    soft_low = low(softmax)
    grad_soft = dot(v, g, NT)
    delta = jnp.sum(high(soft_low) * grad_soft, axis=0, keepdims=True)
    grad_scores = low(softmax * (grad_soft - delta))
    grad_values = low(dot(soft_low, g, NN))
    results = [grad_values]
    for c, unit, grad in (
        (1, k, dot(grad_scores, q, NN)),
        (0, q, dot(grad_scores, k, TN)),
    ):
        rounded = high(low(grad * factor))
        unit = high(unit)
        mean = jnp.mean(unit * rounded, axis=1, keepdims=True)
        results.append(low(scale(c) * (rounded - unit * mean)))
    for c, result in zip((2, 1, 0), results):
        for i, t in enumerate(tiles):
            half = pl.ds(t % 2 * TILE, TILE)
            out[t // 2, half, c * HD : (c + 1) * HD] = result[i * TILE : (i + 1) * TILE]


def head_kernel(back, unread, pieces, spacing, *refs):
    cluster_ref, info_ref, w_ref = refs[:3]
    x_refs = refs[3 : 3 + len(pieces)]
    refs = refs[3 + len(pieces) :]
    if back:
        grads, refs = refs[0], refs[1:]
    refs = refs[unread:]
    if back:
        out, kept, count, member, scales = refs
    else:
        out_refs, (kept, count, member, out) = refs[:HEADS], refs[HEADS:]
    flip, residue = info_ref[0], info_ref[2]
    tiles = kept.shape[0]
    clusters = count.shape[0]
    for c in range(clusters):
        count[c] = 0

    def enter(t, carry):
        c = cluster_ref[t * spacing + residue] // spacing
        place = count[c]
        member[c * CAPACITY + place] = t
        count[c] = place + 1
        return carry

    lax.fori_loop(0, tiles, enter, 0)

    weights = w_ref[...]
    for (slot, start, rows), x_ref in zip(pieces, x_refs):
        normed = x_ref[...]
        if back:
            x = high(normed)
            normed = low(x * rows_rsqrt(x))
        mixed = dot(normed, weights, NT)
        place = 2 * (flip ^ slot) + start // TILE
        for c in range(3):
            u = mixed[:, c * HD : (c + 1) * HD]
            if c < 2:
                scale = rows_rsqrt(u)
                u = u * scale
            for j in range(rows // TILE):
                kept[place + j, :, c * HD : (c + 1) * HD] = low(u[j * TILE : (j + 1) * TILE])
                if back and c < 2:
                    scales[place + j, :, c * HD : (c + 1) * HD] = jnp.broadcast_to(
                        scale[j * TILE : (j + 1) * TILE], (TILE, HD)
                    )

    def visit(c, carry):
        for n in range(1, CAPACITY + 1):

            @pl.when(count[c] == n)
            def _():
                held = [member[c * CAPACITY + i] for i in range(n)]
                if back:
                    backward_cluster(held, kept, out, scales, grads)
                else:
                    forward_cluster(held, kept, out)

        return carry

    lax.fori_loop(0, clusters, visit, 0)
    if not back:
        for k in range(HEADS):
            out_refs[k][...] = out[pl.ds(2 * (flip ^ k), 2)].reshape(out_refs[k].shape)


def head_work(info, tile_cluster, pieces, weights, spacing, grads=None, earlier=()):
    back = grads is not None
    width = weights.shape[1]
    tiles = 2 * HEADS
    wide = 3 * HD if back else HD
    tokens = tiles * TILE
    operands = [tile_cluster, info, weights] + [array for _, _, array in pieces]
    if back:
        operands.append(grads.reshape(tiles, TILE, HD))
    scratch = [
        pltpu.VMEM((tiles, TILE, 3 * HD), jnp.bfloat16),
        pltpu.SMEM((tiles // 2,), jnp.int32),
        pltpu.SMEM((tiles // 2 * CAPACITY,), jnp.int32),
    ]
    if back:
        scratch.append(pltpu.VMEM((tiles, TILE, 2 * HD), jnp.float32))
        shape = jax.ShapeDtypeStruct((HEADS, 2 * TILE, wide), jnp.bfloat16)
    else:
        scratch.append(pltpu.VMEM((tiles, TILE, HD), jnp.bfloat16))
        shape = [jax.ShapeDtypeStruct((2 * TILE, HD), jnp.bfloat16) for _ in range(HEADS)]
    shapes = tuple((k, start, array.shape[0]) for k, start, array in pieces)
    return call(
        functools.partial(head_kernel, back, len(earlier), shapes, spacing),
        operands + list(earlier),
        [SMEM, SMEM] + [VMEM] * (len(operands) - 2) + [HBM] * len(earlier),
        shape,
        scratch,
        MICROSECOND * (12 if back else 8),
        2 * tokens * (width + 2 * wide),
    )

def copy_kernel(starts, *refs):
    count = len(starts)
    outs, sems = refs[-count - 1 : -1], refs[-1]
    copies = [
        fetch(refs[i].at[pl.ds(start, outs[i].shape[0])], outs[i], sems.at[i])
        for i, start in enumerate(starts)
    ]
    for copy in copies:
        copy.wait()


def rows_after(arrays, starts, rows, earlier):
    return pl.pallas_call(
        functools.partial(copy_kernel, starts),
        in_specs=[HBM] * (len(arrays) + len(earlier)),
        out_specs=[VMEM] * len(arrays),
        out_shape=[jax.ShapeDtypeStruct((rows, *a.shape[1:]), a.dtype) for a in arrays],
        scratch_shapes=[pltpu.SemaphoreType.DMA((len(arrays),))],
        compiler_params=pltpu.CompilerParams(vmem_limit_bytes=24 * MIB),
        cost_estimate=pl.CostEstimate(flops=MICROSECOND, bytes_accessed=0, transcendentals=0),
    )(*arrays, *earlier)


def norm_kernel(x_ref, *refs):
    out_ref = refs[-1]
    x = high(x_ref[...])
    out_ref[...] = low(x * rows_rsqrt(x))


def norm_after(x, earlier):
    return call(
        norm_kernel,
        [x, *earlier],
        [VMEM] + [HBM] * len(earlier),
        jax.ShapeDtypeStruct(x.shape, jnp.bfloat16),
        [],
        MICROSECOND * 10,
        4 * x.size,
    )


def spread_kernel(up_ref, w_ref, out_ref, rows, sems):
    copies = [fetch(w_ref.at[k], rows.at[k], sems.at[k]) for k in range(HEADS)]
    for k in range(0, HEADS, 2):
        copies[k].wait()
        copies[k + 1].wait()
        pair = rows[k : k + 2].reshape(2 * HD, -1)
        g = low(dot(up_ref[...], pair, NT))
        out_ref[k] = g[:, :HD]
        out_ref[k + 1] = g[:, HD:]


def spread_grads(upstream, w_fin):
    tokens, width = upstream.shape
    return call(
        spread_kernel,
        [upstream, w_fin.reshape(HEADS, HD, width)],
        [VMEM, HBM],
        jax.ShapeDtypeStruct((HEADS, tokens, HD), jnp.bfloat16),
        [
            pltpu.VMEM((HEADS, HD, width), jnp.bfloat16),
            pltpu.SemaphoreType.DMA((HEADS,)),
        ],
        MICROSECOND * 3,
        2 * width * HEADS * HD,
    )


def finish_kernel(info_ref, *refs):
    att_refs, refs = refs[:HEADS], refs[HEADS:]
    x_ref, w_ref, grad_ref, first_ref, second_ref, x, sem = refs
    flip, odd = info_ref[0], info_ref[3]
    x_copy = fetch(x_ref, x, sem)
    att = jnp.concatenate([ref[...] for ref in att_refs], axis=1)
    x_copy.wait()
    block = 256
    for start in range(0, x_ref.shape[1], block):
        columns = slice(start, start + block)
        w = jnp.concatenate([w_ref[flip ^ k, :, columns] for k in range(HEADS)], axis=0)
        result = low(high(x[:, columns]) + dot(att, w, NN))
        grad = grad_ref[:, columns]
        first_ref[:, columns] = jnp.where(odd == 0, result, grad)
        second_ref[:, columns] = jnp.where(odd == 0, grad, result)


def finish(info, attention, current, w_fin, grad_self):
    tokens, width = current.shape
    return call(
        finish_kernel,
        [info, *attention, current, w_fin.reshape(HEADS, HD, width), grad_self],
        [SMEM] + [VMEM] * HEADS + [HBM] + [VMEM] * 2,
        [jax.ShapeDtypeStruct((tokens, width), jnp.bfloat16)] * 2,
        [pltpu.VMEM((tokens, width), jnp.bfloat16), pltpu.SemaphoreType.DMA],
        MICROSECOND,
        2 * width * HEADS * HD,
    )


def finish_back_kernel(grad_ref, x_ref, up_ref, w_ref, out_ref, grads, x, up, rows, total, sems):
    chunks = rows.shape[0]
    depth = rows.shape[1]
    held = depth // HD
    copies = [fetch(grad_ref, grads, sems.at[0])]
    copies += [
        fetch(w_ref.at[pl.ds(i * depth, depth)], rows.at[i], sems.at[1 + i]) for i in range(chunks)
    ]
    copies.append(fetch(x_ref, x, sems.at[1 + chunks]))
    copies.append(fetch(up_ref, up, sems.at[2 + chunks]))
    copies[0].wait()
    for i in range(chunks):
        c, first = i * held // HEADS, i * held % HEADS
        columns = slice(c * HD, (c + 1) * HD)
        block = jnp.concatenate([grads[first + j, :, columns] for j in range(held)], axis=1)
        copies[1 + i].wait()
        product = dot(block, rows[i], NN)
        if i == 0:
            total[...] = product
        else:
            total[...] += product
    copies[1 + chunks].wait()
    copies[2 + chunks].wait()
    stored = high(x[...])
    scale = rows_rsqrt(stored)
    unit = stored * scale
    g = total[...]
    pulled = scale * (g - unit * jnp.mean(unit * g, axis=1, keepdims=True))
    out_ref[...] = low(high(up[...]) + pulled)


def finish_back(grads, stored, upstream, w_qkv):
    tokens, width = stored.shape
    chunks = 6
    return call(
        finish_back_kernel,
        [grads, stored, upstream, w_qkv],
        [HBM] * 4,
        jax.ShapeDtypeStruct((tokens, width), jnp.bfloat16),
        [
            pltpu.VMEM(grads.shape, jnp.bfloat16),
            pltpu.VMEM((tokens, width), jnp.bfloat16),
            pltpu.VMEM((tokens, width), jnp.bfloat16),
            pltpu.VMEM((chunks, w_qkv.shape[0] // chunks, width), jnp.bfloat16),
            pltpu.VMEM((tokens, width), jnp.float32),
            pltpu.SemaphoreType.DMA((chunks + 3,)),
        ],
        MICROSECOND * 5,
        6 * width * HEADS * HD,
        grant=58 * MIB,
    )


def partner(block, distance):
    route = [(i, i ^ distance) for i in range(lax.axis_size("seq"))]
    return lax.ppermute(block, "seq", route)


def gather_rows(x, earlier):
    half = x.shape[0] // 2
    over_x, over_y = partner(x, 2), partner(x, 4)
    relay_top, relay_bottom = rows_after([over_x, over_y], [0, half], half, earlier)
    far_top, far_bottom = partner(relay_top, 4), partner(relay_bottom, 2)
    pieces = [(0, 0, x), (2, 0, over_x), (4, 0, over_y), (6, 0, far_top), (6, half, far_bottom)]
    return pieces + [(k + 1, start, partner(block, 1)) for k, start, block in pieces]


def swap(blocks):
    moved = {k: partner(blocks[k], k) for k in (2, 4, 6, 3, 5, 7, 1)}
    return [blocks[0]] + [moved[k] for k in range(1, HEADS)]


def all_swap(blocks):
    return lax.all_to_all(blocks, "seq", split_axis=0, concat_axis=0, tiled=True)


def to_heads(blocks, own, spacing):
    heads, tokens, width = blocks.shape
    held = tokens // TILE
    places = spacing // held
    tiled = blocks.reshape(heads, 1, held, TILE, width)
    padded = jnp.zeros((heads, places, held, TILE, width), blocks.dtype)
    padded = lax.dynamic_update_slice_in_dim(padded, tiled, own % places, 1)
    arrived = all_swap(padded.reshape(heads * spacing, TILE, width))
    arrived = arrived.reshape(-1, places, TILE, width)
    mine = lax.dynamic_index_in_dim(arrived, own % spacing // held, 1, keepdims=False)
    return mine.reshape(HEADS, 2 * TILE, width)


def to_tokens(blocks, own, spacing, tokens):
    held = tokens // TILE
    places = spacing // held
    tiled = blocks.reshape(2 * HEADS, 1, TILE, -1)
    padded = jnp.zeros((2 * HEADS, places, TILE, tiled.shape[3]), tiled.dtype)
    padded = lax.dynamic_update_slice_in_dim(padded, tiled, own % spacing // held, 1)
    returned = all_swap(padded.reshape(-1, TILE, tiled.shape[3]))
    returned = returned.reshape(HEADS, places, held * TILE, tiled.shape[3])
    return lax.dynamic_index_in_dim(returned, own % places, 1, keepdims=False)


def swapped(block, first):
    planes = lax.axis_size("pipe")
    route = []
    for i in range(first, planes - 1, 2):
        route += [(i, i + 1), (i + 1, i)]
    return lax.ppermute(block, "pipe", route)


def per_device(section_input, saved_input, grad_output, w_qkv, w_out, tile_cluster):
    current, stored, upstream = section_input[0], saved_input[0], grad_output[0]
    w_rows, w_fin = w_qkv[0], w_out[0]
    tokens = current.shape[0]
    spacing = lax.axis_size("seq") // HEADS
    own = lax.axis_index("seq").astype(jnp.int32)
    odd = lax.axis_index("pipe").astype(jnp.int32) % 2
    if spacing == 1:
        info = jnp.stack([own, own, jnp.zeros_like(own), odd])
        gather, spread, collect, collect_each = gather_rows, all_swap, all_swap, swap
    else:
        info = jnp.stack([jnp.zeros_like(own), own // spacing, own % spacing, odd])

        def gather(x, earlier):
            copies = jnp.broadcast_to(x, (HEADS, *x.shape))
            return [(k, 0, block) for k, block in enumerate(to_heads(copies, own, spacing))]

        def spread(blocks):
            return to_heads(blocks, own, spacing)

        def collect(blocks):
            return to_tokens(blocks, own, spacing, tokens)

        def collect_each(blocks):
            return list(collect(jnp.stack(blocks)))

    own_head = w_rows.reshape(3, HEADS, HD, -1)
    own_head = lax.dynamic_index_in_dim(own_head, info[1], 1, keepdims=False)
    own_head = own_head.reshape(3 * HD, -1)
    spreading = spread_grads(upstream, w_fin)
    stored_pieces = gather(stored, [spreading])
    grad_attention = spread(spreading)
    earlier = [block for k, _, block in stored_pieces if k == HEADS - 2]
    normed = norm_after(current, [*earlier, grad_attention])
    grads = head_work(
        info, tile_cluster, stored_pieces, own_head, spacing, grad_attention, [normed]
    )
    current_pieces = gather(normed, [grads])
    returned_grads = collect(grads)
    outputs = head_work(
        info, tile_cluster, current_pieces, own_head, spacing, earlier=[grads]
    )
    returned = collect_each(outputs)
    grad_self = finish_back(returned_grads, stored, upstream, w_rows)
    first, second = finish(info, returned, current, w_fin, grad_self)
    first, second = swapped(first, 0), swapped(second, 1)
    next_input = jnp.where(odd == 1, first, second)
    grad_input = jnp.where(odd == 1, second, first)
    return (next_input[None], grad_input[None])


def solution(mesh):
    return jax.shard_map(
        per_device,
        mesh=mesh,
        in_specs=(
            P("pipe", "seq", None),
            P("pipe", "seq", None),
            P("pipe", "seq", None),
            P("pipe", None, None),
            P("pipe", None, None),
            P(),
        ),
        out_specs=(P("pipe", "seq", None), P("pipe", "seq", None)),
        check_vma=False,
    )
```

```python
import functools

import jax
import jax.numpy as jnp
from jax import lax
from jax.experimental import pallas as pl
from jax.experimental.pallas import tpu as pltpu
from jax.sharding import PartitionSpec as P

HEADS = 8
HD = 128
TILE = 128
CAPACITY = 3
EPSILON = 1e-05
MIB = 1024 * 1024
MICROSECOND = 1150000000
NT = (((1,), (1,)), ((), ()))
NN = (((1,), (0,)), ((), ()))
TN = (((0,), (0,)), ((), ()))
HBM = pl.BlockSpec(memory_space=pl.ANY)
SMEM = pl.BlockSpec(memory_space=pltpu.SMEM)
VMEM = pl.BlockSpec(memory_space=pltpu.VMEM)


def dot(left, right, dims):
    return lax.dot_general(left, right, dims, preferred_element_type=jnp.float32)


def low(values):
    return values.astype(jnp.bfloat16)


def high(values):
    return values.astype(jnp.float32)


def rows_rsqrt(values):
    return lax.rsqrt(jnp.mean(values * values, axis=-1, keepdims=True) + EPSILON)


def call(kernel, operands, in_specs, out_shape, scratch, flops, moved, grant=24 * MIB):
    return pl.pallas_call(
        kernel,
        in_specs=in_specs,
        out_specs=[VMEM] * len(out_shape) if isinstance(out_shape, list) else VMEM,
        out_shape=out_shape,
        scratch_shapes=scratch,
        compiler_params=pltpu.CompilerParams(vmem_limit_bytes=grant),
        cost_estimate=pl.CostEstimate(flops=flops, bytes_accessed=moved, transcendentals=0),
    )(*operands)


def fetch(source, target, sem):
    copy = pltpu.make_async_copy(source, target, sem)
    copy.start()
    return copy


def forward_cluster(tiles, kept, out):
    def load(c):
        return jnp.concatenate([kept[t, :, c * HD : (c + 1) * HD] for t in tiles], axis=0)

    q, k, v = load(0), load(1), load(2)
    weights = low(jnp.exp(dot(q, k, NT) * (HD ** -0.5)))
    wide = jnp.concatenate([v, jnp.ones_like(v)], axis=1)
    sums = dot(weights, wide, NN)
    result = low(sums[:, :HD] / sums[:, HD:])
    for i, t in enumerate(tiles):
        out[t] = result[i * TILE : (i + 1) * TILE]


def backward_cluster(tiles, kept, out, scales, grads):
    def load(c):
        return jnp.concatenate([kept[t, :, c * HD : (c + 1) * HD] for t in tiles], axis=0)

    def scale(c):
        return jnp.concatenate([scales[t, :, c * HD : (c + 1) * HD] for t in tiles], axis=0)

    q, k, v = load(0), load(1), load(2)
    g = jnp.concatenate([grads[t] for t in tiles], axis=0)
    factor = HD ** -0.5
    weights = jnp.exp(dot(k, q, NT) * factor)
    softmax = weights * (1.0 / jnp.sum(weights, axis=0, keepdims=True))
    soft_low = low(softmax)
    grad_soft = dot(v, g, NT)
    delta = jnp.sum(high(soft_low) * grad_soft, axis=0, keepdims=True)
    grad_scores = low(softmax * (grad_soft - delta))
    grad_values = low(dot(soft_low, g, NN))
    results = [grad_values]
    for c, unit, grad in (
        (1, k, dot(grad_scores, q, NN)),
        (0, q, dot(grad_scores, k, TN)),
    ):
        rounded = high(low(grad * factor))
        unit = high(unit)
        mean = jnp.mean(unit * rounded, axis=1, keepdims=True)
        results.append(low(scale(c) * (rounded - unit * mean)))
    for c, result in zip((2, 1, 0), results):
        for i, t in enumerate(tiles):
            half = pl.ds(t % 2 * TILE, TILE)
            out[t // 2, half, c * HD : (c + 1) * HD] = result[i * TILE : (i + 1) * TILE]


def head_kernel(back, unread, pieces, spacing, *refs):
    cluster_ref, info_ref, w_ref = refs[:3]
    x_refs = refs[3 : 3 + len(pieces)]
    refs = refs[3 + len(pieces) :]
    if back:
        grads, refs = refs[0], refs[1:]
    refs = refs[unread:]
    if back:
        out, kept, count, member, scales = refs
    else:
        out_refs, (kept, count, member, out) = refs[:HEADS], refs[HEADS:]
    flip, residue = info_ref[0], info_ref[2]
    tiles = kept.shape[0]
    clusters = count.shape[0]
    for c in range(clusters):
        count[c] = 0

    def enter(t, carry):
        c = cluster_ref[t * spacing + residue] // spacing
        place = count[c]
        member[c * CAPACITY + place] = t
        count[c] = place + 1
        return carry

    lax.fori_loop(0, tiles, enter, 0)

    weights = w_ref[...]
    for (slot, start, rows), x_ref in zip(pieces, x_refs):
        normed = x_ref[...]
        if back:
            x = high(normed)
            normed = low(x * rows_rsqrt(x))
        mixed = dot(normed, weights, NT)
        place = 2 * (flip ^ slot) + start // TILE
        for c in range(3):
            u = mixed[:, c * HD : (c + 1) * HD]
            if c < 2:
                scale = rows_rsqrt(u)
                u = u * scale
            for j in range(rows // TILE):
                kept[place + j, :, c * HD : (c + 1) * HD] = low(u[j * TILE : (j + 1) * TILE])
                if back and c < 2:
                    scales[place + j, :, c * HD : (c + 1) * HD] = jnp.broadcast_to(
                        scale[j * TILE : (j + 1) * TILE], (TILE, HD)
                    )

    def visit(pair, carry):
        swap = (count[2 * pair] < count[2 * pair + 1]).astype(jnp.int32)
        large, small = 2 * pair + swap, 2 * pair + 1 - swap
        for n in range(1, CAPACITY + 1):
            for m in range(0, n + 1):

                @pl.when((count[large] == n) & (count[small] == m))
                def _():
                    for c, size in ((large, n), (small, m)):
                        if size > 0:
                            held = [member[c * CAPACITY + i] for i in range(size)]
                            if back:
                                backward_cluster(held, kept, out, scales, grads)
                            else:
                                forward_cluster(held, kept, out)

        return carry

    lax.fori_loop(0, clusters // 2, visit, 0)
    if not back:
        for k in range(HEADS):
            out_refs[k][...] = out[pl.ds(2 * (flip ^ k), 2)].reshape(out_refs[k].shape)


def head_work(info, tile_cluster, pieces, weights, spacing, grads=None, earlier=()):
    back = grads is not None
    width = weights.shape[1]
    tiles = 2 * HEADS
    wide = 3 * HD if back else HD
    tokens = tiles * TILE
    operands = [tile_cluster, info, weights] + [array for _, _, array in pieces]
    if back:
        operands.append(grads.reshape(tiles, TILE, HD))
    scratch = [
        pltpu.VMEM((tiles, TILE, 3 * HD), jnp.bfloat16),
        pltpu.SMEM((tiles // 2,), jnp.int32),
        pltpu.SMEM((tiles // 2 * CAPACITY,), jnp.int32),
    ]
    if back:
        scratch.append(pltpu.VMEM((tiles, TILE, 2 * HD), jnp.float32))
        shape = jax.ShapeDtypeStruct((HEADS, 2 * TILE, wide), jnp.bfloat16)
    else:
        scratch.append(pltpu.VMEM((tiles, TILE, HD), jnp.bfloat16))
        shape = [jax.ShapeDtypeStruct((2 * TILE, HD), jnp.bfloat16) for _ in range(HEADS)]
    shapes = tuple((k, start, array.shape[0]) for k, start, array in pieces)
    return call(
        functools.partial(head_kernel, back, len(earlier), shapes, spacing),
        operands + list(earlier),
        [SMEM, SMEM] + [VMEM] * (len(operands) - 2) + [HBM] * len(earlier),
        shape,
        scratch,
        MICROSECOND * (12 if back else 8),
        2 * tokens * (width + 2 * wide),
    )

def copy_kernel(starts, *refs):
    count = len(starts)
    outs, sems = refs[-count - 1 : -1], refs[-1]
    copies = [
        fetch(refs[i].at[pl.ds(start, outs[i].shape[0])], outs[i], sems.at[i])
        for i, start in enumerate(starts)
    ]
    for copy in copies:
        copy.wait()


def rows_after(arrays, starts, rows, earlier):
    return pl.pallas_call(
        functools.partial(copy_kernel, starts),
        in_specs=[HBM] * (len(arrays) + len(earlier)),
        out_specs=[VMEM] * len(arrays),
        out_shape=[jax.ShapeDtypeStruct((rows, *a.shape[1:]), a.dtype) for a in arrays],
        scratch_shapes=[pltpu.SemaphoreType.DMA((len(arrays),))],
        compiler_params=pltpu.CompilerParams(vmem_limit_bytes=24 * MIB),
        cost_estimate=pl.CostEstimate(flops=MICROSECOND, bytes_accessed=0, transcendentals=0),
    )(*arrays, *earlier)


def norm_kernel(x_ref, *refs):
    out_ref = refs[-1]
    x = high(x_ref[...])
    out_ref[...] = low(x * rows_rsqrt(x))


def norm_after(x, earlier):
    return call(
        norm_kernel,
        [x, *earlier],
        [VMEM] + [HBM] * len(earlier),
        jax.ShapeDtypeStruct(x.shape, jnp.bfloat16),
        [],
        MICROSECOND * 10,
        4 * x.size,
    )


def spread_kernel(up_ref, w_ref, out_ref, rows, sems):
    copies = [fetch(w_ref.at[k], rows.at[k], sems.at[k]) for k in range(HEADS)]
    for k in range(0, HEADS, 2):
        copies[k].wait()
        copies[k + 1].wait()
        pair = rows[k : k + 2].reshape(2 * HD, -1)
        g = low(dot(up_ref[...], pair, NT))
        out_ref[k] = g[:, :HD]
        out_ref[k + 1] = g[:, HD:]


def spread_grads(upstream, w_fin):
    tokens, width = upstream.shape
    return call(
        spread_kernel,
        [upstream, w_fin.reshape(HEADS, HD, width)],
        [VMEM, HBM],
        jax.ShapeDtypeStruct((HEADS, tokens, HD), jnp.bfloat16),
        [
            pltpu.VMEM((HEADS, HD, width), jnp.bfloat16),
            pltpu.SemaphoreType.DMA((HEADS,)),
        ],
        MICROSECOND * 3,
        2 * width * HEADS * HD,
    )


def finish_kernel(info_ref, *refs):
    att_refs, refs = refs[:HEADS], refs[HEADS:]
    x, w_ref, grad_ref, first_ref, second_ref = refs
    flip, odd = info_ref[0], info_ref[3]
    att = jnp.concatenate([ref[...] for ref in att_refs], axis=1)
    block = 256
    for start in range(0, x.shape[1], block):
        columns = slice(start, start + block)
        w = jnp.concatenate([w_ref[flip ^ k, :, columns] for k in range(HEADS)], axis=0)
        result = low(high(x[:, columns]) + dot(att, w, NN))
        grad = grad_ref[:, columns]
        first_ref[:, columns] = jnp.where(odd == 0, result, grad)
        second_ref[:, columns] = jnp.where(odd == 0, grad, result)


def finish(info, attention, current, w_fin, grad_self):
    tokens, width = current.shape
    return call(
        finish_kernel,
        [info, *attention, current, w_fin.reshape(HEADS, HD, width), grad_self],
        [SMEM] + [VMEM] * (HEADS + 3),
        [jax.ShapeDtypeStruct((tokens, width), jnp.bfloat16)] * 2,
        [],
        MICROSECOND,
        2 * width * HEADS * HD,
    )


def finish_back_kernel(grad_ref, x_ref, up_ref, w_ref, near_ref, out_ref, near, grads, x, up, rows, total, sems):
    chunks = rows.shape[0]
    depth = rows.shape[1]
    held = depth // HD
    copies = [fetch(grad_ref, grads, sems.at[0])]
    copies += [
        fetch(w_ref.at[pl.ds(i * depth, depth)], rows.at[i], sems.at[1 + i]) for i in range(chunks)
    ]
    copies.append(fetch(x_ref, x, sems.at[1 + chunks]))
    copies.append(fetch(up_ref, up, sems.at[2 + chunks]))
    near_copy = fetch(near_ref, near, sems.at[3 + chunks])
    copies[0].wait()
    for i in range(chunks):
        c, first = i * held // HEADS, i * held % HEADS
        columns = slice(c * HD, (c + 1) * HD)
        block = jnp.concatenate([grads[first + j, :, columns] for j in range(held)], axis=1)
        copies[1 + i].wait()
        product = dot(block, rows[i], NN)
        if i == 0:
            total[...] = product
        else:
            total[...] += product
    copies[1 + chunks].wait()
    copies[2 + chunks].wait()
    stored = high(x[...])
    scale = rows_rsqrt(stored)
    unit = stored * scale
    g = total[...]
    pulled = scale * (g - unit * jnp.mean(unit * g, axis=1, keepdims=True))
    out_ref[...] = low(high(up[...]) + pulled)
    near_copy.wait()


def finish_back(grads, stored, upstream, w_qkv, near):
    tokens, width = stored.shape
    chunks = 6
    return call(
        finish_back_kernel,
        [grads, stored, upstream, w_qkv, near],
        [HBM] * 5,
        [jax.ShapeDtypeStruct((tokens, width), jnp.bfloat16)] * 2,
        [
            pltpu.VMEM(grads.shape, jnp.bfloat16),
            pltpu.VMEM((tokens, width), jnp.bfloat16),
            pltpu.VMEM((tokens, width), jnp.bfloat16),
            pltpu.VMEM((chunks, w_qkv.shape[0] // chunks, width), jnp.bfloat16),
            pltpu.VMEM((tokens, width), jnp.float32),
            pltpu.SemaphoreType.DMA((chunks + 4,)),
        ],
        MICROSECOND * 5,
        6 * width * HEADS * HD,
        grant=52 * MIB,
    )


def partner(block, distance):
    route = [(i, i ^ distance) for i in range(lax.axis_size("seq"))]
    return lax.ppermute(block, "seq", route)


def gather_rows(x, earlier):
    half = x.shape[0] // 2
    over_x, over_y = partner(x, 2), partner(x, 4)
    relay_top, relay_bottom = rows_after([over_x, over_y], [0, half], half, earlier)
    far_top, far_bottom = partner(relay_top, 4), partner(relay_bottom, 2)
    pieces = [(0, 0, x), (2, 0, over_x), (4, 0, over_y), (6, 0, far_top), (6, half, far_bottom)]
    return pieces + [(k + 1, start, partner(block, 1)) for k, start, block in pieces]


def swap(blocks):
    moved = {k: partner(blocks[k], k) for k in (2, 4, 6, 3, 5, 7, 1)}
    return [blocks[0]] + [moved[k] for k in range(1, HEADS)]


def all_swap(blocks):
    return lax.all_to_all(blocks, "seq", split_axis=0, concat_axis=0, tiled=True)


def to_heads(blocks, own, spacing):
    heads, tokens, width = blocks.shape
    held = tokens // TILE
    places = spacing // held
    tiled = blocks.reshape(heads, 1, held, TILE, width)
    padded = jnp.zeros((heads, places, held, TILE, width), blocks.dtype)
    padded = lax.dynamic_update_slice_in_dim(padded, tiled, own % places, 1)
    arrived = all_swap(padded.reshape(heads * spacing, TILE, width))
    arrived = arrived.reshape(-1, places, TILE, width)
    mine = lax.dynamic_index_in_dim(arrived, own % spacing // held, 1, keepdims=False)
    return mine.reshape(HEADS, 2 * TILE, width)


def to_tokens(blocks, own, spacing, tokens):
    held = tokens // TILE
    places = spacing // held
    tiled = blocks.reshape(2 * HEADS, 1, TILE, -1)
    padded = jnp.zeros((2 * HEADS, places, TILE, tiled.shape[3]), tiled.dtype)
    padded = lax.dynamic_update_slice_in_dim(padded, tiled, own % spacing // held, 1)
    returned = all_swap(padded.reshape(-1, TILE, tiled.shape[3]))
    returned = returned.reshape(HEADS, places, held * TILE, tiled.shape[3])
    return lax.dynamic_index_in_dim(returned, own % places, 1, keepdims=False)


def swapped(block, first):
    planes = lax.axis_size("pipe")
    route = []
    for i in range(first, planes - 1, 2):
        route += [(i, i + 1), (i + 1, i)]
    return lax.ppermute(block, "pipe", route)


def per_device(section_input, saved_input, grad_output, w_qkv, w_out, tile_cluster):
    current, stored, upstream = section_input[0], saved_input[0], grad_output[0]
    w_rows, w_fin = w_qkv[0], w_out[0]
    tokens = current.shape[0]
    spacing = lax.axis_size("seq") // HEADS
    own = lax.axis_index("seq").astype(jnp.int32)
    odd = lax.axis_index("pipe").astype(jnp.int32) % 2
    if spacing == 1:
        info = jnp.stack([own, own, jnp.zeros_like(own), odd])
        gather, spread, collect, collect_each = gather_rows, all_swap, all_swap, swap
    else:
        info = jnp.stack([jnp.zeros_like(own), own // spacing, own % spacing, odd])

        def gather(x, earlier):
            copies = jnp.broadcast_to(x, (HEADS, *x.shape))
            return [(k, 0, block) for k, block in enumerate(to_heads(copies, own, spacing))]

        def spread(blocks):
            return to_heads(blocks, own, spacing)

        def collect(blocks):
            return to_tokens(blocks, own, spacing, tokens)

        def collect_each(blocks):
            return list(collect(jnp.stack(blocks)))

    own_head = w_rows.reshape(3, HEADS, HD, -1)
    own_head = lax.dynamic_index_in_dim(own_head, info[1], 1, keepdims=False)
    own_head = own_head.reshape(3 * HD, -1)
    spreading = spread_grads(upstream, w_fin)
    stored_pieces = gather(stored, [spreading])
    grad_attention = spread(spreading)
    earlier = [block for k, _, block in stored_pieces if k == HEADS - 2]
    normed = norm_after(current, [*earlier, grad_attention])
    grads = head_work(
        info, tile_cluster, stored_pieces, own_head, spacing, grad_attention, [normed]
    )
    current_pieces = gather(normed, [grads])
    returned_grads = collect(grads)
    outputs = head_work(
        info, tile_cluster, current_pieces, own_head, spacing, earlier=[grads]
    )
    returned = collect_each(outputs)
    grad_self, near = finish_back(returned_grads, stored, upstream, w_rows, current)
    first, second = finish(info, returned, near, w_fin, grad_self)
    first, second = swapped(first, 0), swapped(second, 1)
    next_input = jnp.where(odd == 1, first, second)
    grad_input = jnp.where(odd == 1, second, first)
    return (next_input[None], grad_input[None])


def solution(mesh):
    return jax.shard_map(
        per_device,
        mesh=mesh,
        in_specs=(
            P("pipe", "seq", None),
            P("pipe", "seq", None),
            P("pipe", "seq", None),
            P("pipe", None, None),
            P("pipe", None, None),
            P(),
        ),
        out_specs=(P("pipe", "seq", None), P("pipe", "seq", None)),
        check_vma=False,
    )
```

```python
import functools

import jax
import jax.numpy as jnp
from jax import lax
from jax.experimental import pallas as pl
from jax.experimental.pallas import tpu as pltpu
from jax.sharding import PartitionSpec as P

HEADS = 8
HD = 128
TILE = 128
CAPACITY = 3
EPSILON = 1e-05
MIB = 1024 * 1024
MICROSECOND = 1150000000
NT = (((1,), (1,)), ((), ()))
NN = (((1,), (0,)), ((), ()))
TN = (((0,), (0,)), ((), ()))
HBM = pl.BlockSpec(memory_space=pl.ANY)
SMEM = pl.BlockSpec(memory_space=pltpu.SMEM)
VMEM = pl.BlockSpec(memory_space=pltpu.VMEM)


def dot(left, right, dims):
    return lax.dot_general(left, right, dims, preferred_element_type=jnp.float32)


def low(values):
    return values.astype(jnp.bfloat16)


def high(values):
    return values.astype(jnp.float32)


def rows_rsqrt(values):
    return lax.rsqrt(jnp.mean(values * values, axis=-1, keepdims=True) + EPSILON)


def call(kernel, operands, in_specs, out_shape, scratch, flops, moved, grant=24 * MIB):
    return pl.pallas_call(
        kernel,
        in_specs=in_specs,
        out_specs=[VMEM] * len(out_shape) if isinstance(out_shape, list) else VMEM,
        out_shape=out_shape,
        scratch_shapes=scratch,
        compiler_params=pltpu.CompilerParams(vmem_limit_bytes=grant),
        cost_estimate=pl.CostEstimate(flops=flops, bytes_accessed=moved, transcendentals=0),
    )(*operands)


def fetch(source, target, sem):
    copy = pltpu.make_async_copy(source, target, sem)
    copy.start()
    return copy


def forward_cluster(tiles, kept, out):
    def load(c):
        return jnp.concatenate([kept[t, :, c * HD : (c + 1) * HD] for t in tiles], axis=0)

    q, k, v = load(0), load(1), load(2)
    weights = low(jnp.exp(dot(q, k, NT) * (HD ** -0.5)))
    wide = jnp.concatenate([v, jnp.ones_like(v)], axis=1)
    sums = dot(weights, wide, NN)
    result = low(sums[:, :HD] / sums[:, HD:])
    for i, t in enumerate(tiles):
        out[t] = result[i * TILE : (i + 1) * TILE]


def backward_cluster(tiles, kept, out, scales, grads):
    def load(c):
        return jnp.concatenate([kept[t, :, c * HD : (c + 1) * HD] for t in tiles], axis=0)

    def scale(c):
        return jnp.concatenate([scales[t, :, c * HD : (c + 1) * HD] for t in tiles], axis=0)

    q, k, v = load(0), load(1), load(2)
    g = jnp.concatenate([grads[t] for t in tiles], axis=0)
    factor = HD ** -0.5
    weights = jnp.exp(dot(k, q, NT) * factor)
    softmax = weights * (1.0 / jnp.sum(weights, axis=0, keepdims=True))
    soft_low = low(softmax)
    grad_soft = dot(v, g, NT)
    delta = jnp.sum(high(soft_low) * grad_soft, axis=0, keepdims=True)
    grad_scores = low(softmax * (grad_soft - delta))
    grad_values = low(dot(soft_low, g, NN))
    results = [grad_values]
    for c, unit, grad in (
        (1, k, dot(grad_scores, q, NN)),
        (0, q, dot(grad_scores, k, TN)),
    ):
        rounded = high(low(grad * factor))
        unit = high(unit)
        mean = jnp.mean(unit * rounded, axis=1, keepdims=True)
        results.append(low(scale(c) * (rounded - unit * mean)))
    for c, result in zip((2, 1, 0), results):
        for i, t in enumerate(tiles):
            half = pl.ds(t % 2 * TILE, TILE)
            out[t // 2, half, c * HD : (c + 1) * HD] = result[i * TILE : (i + 1) * TILE]


def head_kernel(back, unread, pieces, spacing, *refs):
    cluster_ref, info_ref, w_ref = refs[:3]
    x_refs = refs[3 : 3 + len(pieces)]
    refs = refs[3 + len(pieces) :]
    if back:
        grads, refs = refs[0], refs[1:]
    refs = refs[unread:]
    if back:
        out, kept, count, member, scales = refs
    else:
        out_refs, (kept, count, member, out) = refs[:HEADS], refs[HEADS:]
    flip, residue = info_ref[0], info_ref[2]
    tiles = kept.shape[0]
    clusters = count.shape[0]
    for c in range(clusters):
        count[c] = 0

    def enter(t, carry):
        c = cluster_ref[t * spacing + residue] // spacing
        place = count[c]
        member[c * CAPACITY + place] = t
        count[c] = place + 1
        return carry

    lax.fori_loop(0, tiles, enter, 0)

    weights = w_ref[...]
    for (slot, start, rows), x_ref in zip(pieces, x_refs):
        normed = x_ref[...]
        if back:
            x = high(normed)
            normed = low(x * rows_rsqrt(x))
        mixed = dot(normed, weights, NT)
        place = 2 * (flip ^ slot) + start // TILE
        for c in range(3):
            u = mixed[:, c * HD : (c + 1) * HD]
            if c < 2:
                scale = rows_rsqrt(u)
                u = u * scale
            for j in range(rows // TILE):
                kept[place + j, :, c * HD : (c + 1) * HD] = low(u[j * TILE : (j + 1) * TILE])
                if back and c < 2:
                    scales[place + j, :, c * HD : (c + 1) * HD] = jnp.broadcast_to(
                        scale[j * TILE : (j + 1) * TILE], (TILE, HD)
                    )

    def visit(pair, carry):
        swap = (count[2 * pair] < count[2 * pair + 1]).astype(jnp.int32)
        large, small = 2 * pair + swap, 2 * pair + 1 - swap
        for n in range(1, CAPACITY + 1):
            for m in range(0, n + 1):

                @pl.when((count[large] == n) & (count[small] == m))
                def _():
                    for c, size in ((large, n), (small, m)):
                        if size > 0:
                            held = [member[c * CAPACITY + i] for i in range(size)]
                            if back:
                                backward_cluster(held, kept, out, scales, grads)
                            else:
                                forward_cluster(held, kept, out)

        return carry

    lax.fori_loop(0, clusters // 2, visit, 0)
    if not back:
        for k in range(HEADS):
            out_refs[k][...] = out[pl.ds(2 * (flip ^ k), 2)].reshape(out_refs[k].shape)


def head_work(info, tile_cluster, pieces, weights, spacing, grads=None, earlier=()):
    back = grads is not None
    width = weights.shape[1]
    tiles = 2 * HEADS
    wide = 3 * HD if back else HD
    tokens = tiles * TILE
    operands = [tile_cluster, info, weights] + [array for _, _, array in pieces]
    if back:
        operands.append(grads.reshape(tiles, TILE, HD))
    scratch = [
        pltpu.VMEM((tiles, TILE, 3 * HD), jnp.bfloat16),
        pltpu.SMEM((tiles // 2,), jnp.int32),
        pltpu.SMEM((tiles // 2 * CAPACITY,), jnp.int32),
    ]
    if back:
        scratch.append(pltpu.VMEM((tiles, TILE, 2 * HD), jnp.float32))
        shape = jax.ShapeDtypeStruct((HEADS, 2 * TILE, wide), jnp.bfloat16)
    else:
        scratch.append(pltpu.VMEM((tiles, TILE, HD), jnp.bfloat16))
        shape = [jax.ShapeDtypeStruct((2 * TILE, HD), jnp.bfloat16) for _ in range(HEADS)]
    shapes = tuple((k, start, array.shape[0]) for k, start, array in pieces)
    return call(
        functools.partial(head_kernel, back, len(earlier), shapes, spacing),
        operands + list(earlier),
        [SMEM, SMEM] + [VMEM] * (len(operands) - 2) + [HBM] * len(earlier),
        shape,
        scratch,
        MICROSECOND * (15 if back else 9),
        2 * tokens * (width + 2 * wide),
    )

def copy_kernel(starts, *refs):
    count = len(starts)
    outs, sems = refs[-count - 1 : -1], refs[-1]
    copies = [
        fetch(refs[i].at[pl.ds(start, outs[i].shape[0])], outs[i], sems.at[i])
        for i, start in enumerate(starts)
    ]
    for copy in copies:
        copy.wait()


def rows_after(arrays, starts, rows, earlier):
    return pl.pallas_call(
        functools.partial(copy_kernel, starts),
        in_specs=[HBM] * (len(arrays) + len(earlier)),
        out_specs=[VMEM] * len(arrays),
        out_shape=[jax.ShapeDtypeStruct((rows, *a.shape[1:]), a.dtype) for a in arrays],
        scratch_shapes=[pltpu.SemaphoreType.DMA((len(arrays),))],
        compiler_params=pltpu.CompilerParams(vmem_limit_bytes=24 * MIB),
        cost_estimate=pl.CostEstimate(flops=0, bytes_accessed=0, transcendentals=0),
    )(*arrays, *earlier)


def norm_kernel(x_ref, *refs):
    out_ref = refs[-1]
    x = high(x_ref[...])
    out_ref[...] = low(x * rows_rsqrt(x))


def norm_after(x, earlier):
    return call(
        norm_kernel,
        [x, *earlier],
        [VMEM] + [HBM] * len(earlier),
        jax.ShapeDtypeStruct(x.shape, jnp.bfloat16),
        [],
        MICROSECOND * 10,
        4 * x.size,
    )


def spread_kernel(up_ref, w_ref, out_ref, rows, sems):
    copies = [fetch(w_ref.at[k], rows.at[k], sems.at[k]) for k in range(HEADS)]
    for k in range(0, HEADS, 2):
        copies[k].wait()
        copies[k + 1].wait()
        pair = rows[k : k + 2].reshape(2 * HD, -1)
        g = low(dot(up_ref[...], pair, NT))
        out_ref[k] = g[:, :HD]
        out_ref[k + 1] = g[:, HD:]


def spread_grads(upstream, w_fin):
    tokens, width = upstream.shape
    return call(
        spread_kernel,
        [upstream, w_fin.reshape(HEADS, HD, width)],
        [VMEM, HBM],
        jax.ShapeDtypeStruct((HEADS, tokens, HD), jnp.bfloat16),
        [
            pltpu.VMEM((HEADS, HD, width), jnp.bfloat16),
            pltpu.SemaphoreType.DMA((HEADS,)),
        ],
        MICROSECOND * 3,
        2 * width * HEADS * HD,
    )


def finish_kernel(info_ref, *refs):
    att_refs, refs = refs[:HEADS], refs[HEADS:]
    x, w_ref, grad_ref, first_ref, second_ref = refs
    flip, odd = info_ref[0], info_ref[3]
    att = jnp.concatenate([ref[...] for ref in att_refs], axis=1)
    block = 256
    for start in range(0, x.shape[1], block):
        columns = slice(start, start + block)
        w = jnp.concatenate([w_ref[flip ^ k, :, columns] for k in range(HEADS)], axis=0)
        result = low(high(x[:, columns]) + dot(att, w, NN))
        grad = grad_ref[:, columns]
        first_ref[:, columns] = jnp.where(odd == 0, result, grad)
        second_ref[:, columns] = jnp.where(odd == 0, grad, result)


def finish(info, attention, current, w_fin, grad_self):
    tokens, width = current.shape
    return call(
        finish_kernel,
        [info, *attention, current, w_fin.reshape(HEADS, HD, width), grad_self],
        [SMEM] + [VMEM] * (HEADS + 3),
        [jax.ShapeDtypeStruct((tokens, width), jnp.bfloat16)] * 2,
        [],
        MICROSECOND,
        2 * width * HEADS * HD,
    )


def finish_back_kernel(grad_ref, x_ref, up_ref, w_ref, near_ref, out_ref, near, grads, x, up, rows, total, sems):
    chunks = rows.shape[0]
    depth = rows.shape[1]
    held = depth // HD
    copies = [fetch(grad_ref, grads, sems.at[0])]
    copies += [
        fetch(w_ref.at[pl.ds(i * depth, depth)], rows.at[i], sems.at[1 + i]) for i in range(chunks)
    ]
    copies.append(fetch(x_ref, x, sems.at[1 + chunks]))
    copies.append(fetch(up_ref, up, sems.at[2 + chunks]))
    near_copy = fetch(near_ref, near, sems.at[3 + chunks])
    copies[0].wait()
    for i in range(chunks):
        c, first = i * held // HEADS, i * held % HEADS
        columns = slice(c * HD, (c + 1) * HD)
        block = jnp.concatenate([grads[first + j, :, columns] for j in range(held)], axis=1)
        copies[1 + i].wait()
        product = dot(block, rows[i], NN)
        if i == 0:
            total[...] = product
        else:
            total[...] += product
    copies[1 + chunks].wait()
    copies[2 + chunks].wait()
    stored = high(x[...])
    scale = rows_rsqrt(stored)
    unit = stored * scale
    g = total[...]
    pulled = scale * (g - unit * jnp.mean(unit * g, axis=1, keepdims=True))
    out_ref[...] = low(high(up[...]) + pulled)
    near_copy.wait()


def finish_back(grads, stored, upstream, w_qkv, near):
    tokens, width = stored.shape
    chunks = 6
    return call(
        finish_back_kernel,
        [grads, stored, upstream, w_qkv, near],
        [HBM] * 5,
        [jax.ShapeDtypeStruct((tokens, width), jnp.bfloat16)] * 2,
        [
            pltpu.VMEM(grads.shape, jnp.bfloat16),
            pltpu.VMEM((tokens, width), jnp.bfloat16),
            pltpu.VMEM((tokens, width), jnp.bfloat16),
            pltpu.VMEM((chunks, w_qkv.shape[0] // chunks, width), jnp.bfloat16),
            pltpu.VMEM((tokens, width), jnp.float32),
            pltpu.SemaphoreType.DMA((chunks + 4,)),
        ],
        MICROSECOND * 5,
        6 * width * HEADS * HD,
        grant=52 * MIB,
    )


def partner(block, distance):
    route = [(i, i ^ distance) for i in range(lax.axis_size("seq"))]
    return lax.ppermute(block, "seq", route)


def gather_rows(x, earlier):
    half = x.shape[0] // 2
    over_x, over_y = partner(x, 2), partner(x, 4)
    relay_top, relay_bottom = rows_after([over_x, over_y], [0, half], half, earlier)
    far_top, far_bottom = partner(relay_top, 4), partner(relay_bottom, 2)
    pieces = [(0, 0, x), (2, 0, over_x), (4, 0, over_y), (6, 0, far_top), (6, half, far_bottom)]
    return pieces + [(k + 1, start, partner(block, 1)) for k, start, block in pieces]


def swap(blocks):
    moved = {k: partner(blocks[k], k) for k in (7, 5, 3, 6, 4, 2, 1)}
    return [blocks[0]] + [moved[k] for k in range(1, HEADS)]


def all_swap(blocks):
    return lax.all_to_all(blocks, "seq", split_axis=0, concat_axis=0, tiled=True)


def to_heads(blocks, own, spacing):
    heads, tokens, width = blocks.shape
    held = tokens // TILE
    places = spacing // held
    tiled = blocks.reshape(heads, 1, held, TILE, width)
    padded = jnp.zeros((heads, places, held, TILE, width), blocks.dtype)
    padded = lax.dynamic_update_slice_in_dim(padded, tiled, own % places, 1)
    arrived = all_swap(padded.reshape(heads * spacing, TILE, width))
    arrived = arrived.reshape(-1, places, TILE, width)
    mine = lax.dynamic_index_in_dim(arrived, own % spacing // held, 1, keepdims=False)
    return mine.reshape(HEADS, 2 * TILE, width)


def to_tokens(blocks, own, spacing, tokens):
    held = tokens // TILE
    places = spacing // held
    tiled = blocks.reshape(2 * HEADS, 1, TILE, -1)
    padded = jnp.zeros((2 * HEADS, places, TILE, tiled.shape[3]), tiled.dtype)
    padded = lax.dynamic_update_slice_in_dim(padded, tiled, own % spacing // held, 1)
    returned = all_swap(padded.reshape(-1, TILE, tiled.shape[3]))
    returned = returned.reshape(HEADS, places, held * TILE, tiled.shape[3])
    return lax.dynamic_index_in_dim(returned, own % places, 1, keepdims=False)


def swapped(block, first):
    planes = lax.axis_size("pipe")
    route = []
    for i in range(first, planes - 1, 2):
        route += [(i, i + 1), (i + 1, i)]
    return lax.ppermute(block, "pipe", route)


def per_device(section_input, saved_input, grad_output, w_qkv, w_out, tile_cluster):
    current, stored, upstream = section_input[0], saved_input[0], grad_output[0]
    w_rows, w_fin = w_qkv[0], w_out[0]
    tokens = current.shape[0]
    spacing = lax.axis_size("seq") // HEADS
    own = lax.axis_index("seq").astype(jnp.int32)
    odd = lax.axis_index("pipe").astype(jnp.int32) % 2
    if spacing == 1:
        info = jnp.stack([own, own, jnp.zeros_like(own), odd])
        gather, spread, collect, collect_each = gather_rows, all_swap, all_swap, swap
    else:
        info = jnp.stack([jnp.zeros_like(own), own // spacing, own % spacing, odd])

        def gather(x, earlier):
            copies = jnp.broadcast_to(x, (HEADS, *x.shape))
            return [(k, 0, block) for k, block in enumerate(to_heads(copies, own, spacing))]

        def spread(blocks):
            return to_heads(blocks, own, spacing)

        def collect(blocks):
            return to_tokens(blocks, own, spacing, tokens)

        def collect_each(blocks):
            return list(collect(jnp.stack(blocks)))

    own_head = w_rows.reshape(3, HEADS, HD, -1)
    own_head = lax.dynamic_index_in_dim(own_head, info[1], 1, keepdims=False)
    own_head = own_head.reshape(3 * HD, -1)
    spreading = spread_grads(upstream, w_fin)
    stored_pieces = gather(stored, [spreading])
    grad_attention = spread(spreading)
    earlier = [block for k, _, block in stored_pieces if k == HEADS - 2]
    normed = norm_after(current, [*earlier, grad_attention])
    grads = head_work(
        info, tile_cluster, stored_pieces, own_head, spacing, grad_attention, [normed]
    )
    current_pieces = gather(normed, [grads])
    returned_grads = collect(grads)
    outputs = head_work(
        info, tile_cluster, current_pieces, own_head, spacing, earlier=[grads]
    )
    returned = collect_each(outputs)
    grad_self, near = finish_back(returned_grads, stored, upstream, w_rows, current)
    first, second = finish(info, returned, near, w_fin, grad_self)
    second = swapped(second, 1)
    first = swapped(first, 0)
    next_input = jnp.where(odd == 1, first, second)
    grad_input = jnp.where(odd == 1, second, first)
    return (next_input[None], grad_input[None])


def solution(mesh):
    return jax.shard_map(
        per_device,
        mesh=mesh,
        in_specs=(
            P("pipe", "seq", None),
            P("pipe", "seq", None),
            P("pipe", "seq", None),
            P("pipe", None, None),
            P("pipe", None, None),
            P(),
        ),
        out_specs=(P("pipe", "seq", None), P("pipe", "seq", None)),
        check_vma=False,
    )
```
